32 devices in a mesh: dp: 8 (over z, x), feat: 4 (over y, core).
Axes of the slice: x: 2, y: 2, z: 4, core: 2. Of those that a mesh axis runs over, the one named last changes fastest.
Arguments:
- tokens: bfloat16 [4096, 1024], P('dp'), may hold values from -6 to 6
- gain_one: float32 [1024], replicated, may hold values from 0.5 to 1.5
- w_query: bfloat16 [1024, 256], replicated, may hold values from -0.1875 to 0.1875
- w_key: bfloat16 [1024, 256], replicated, may hold values from -0.1875 to 0.1875
- w_value: bfloat16 [1024, 1024], replicated, may hold values from -0.1875 to 0.1875
- w_out: bfloat16 [1024, 1024], replicated, may hold values from -1.5 to 1.5
- gain_two: float32 [1024], replicated, may hold values from 0.5 to 1.5
- w_gate: bfloat16 [1024, 2752], P(None, 'feat'), may hold values from -0.1875 to 0.1875
- w_up: bfloat16 [1024, 2752], P(None, 'feat'), may hold values from -0.1875 to 0.1875
- w_down: bfloat16 [2752, 1024], P('feat'), may hold values from -0.109375 to 0.109375
- lengths: int32 [8, 4], P('dp'), may hold values from 0 to 512, as said below
- cotangent: bfloat16 [4096, 1024], P('dp'), may hold values from -6 to 6
Outputs:
- output: bfloat16 [4096, 1024], P('dp')
- grad_input: bfloat16 [4096, 1024], P('dp')
- grad_gain_one: float32 [1024], P('dp')
- grad_w_query: float32 [1024, 256], P('dp')
- grad_w_key: float32 [1024, 256], P('dp')
- grad_w_value: float32 [1024, 1024], P('dp')
- grad_w_out: float32 [1024, 1024], P('feat', 'dp')
- grad_gain_two: float32 [1024], P('dp')
- grad_w_gate: float32 [1024, 2752], P('dp', 'feat')
- grad_w_up: float32 [1024, 2752], P('dp', 'feat')
- grad_w_down: float32 [2752, 1024], P('feat', 'dp')
The draws below stay inside these ranges and needn't reach their ends.
Inputs may be any that keep to these rules, and one draw needn't show every extreme that they name: `lengths`: row p lists the sequences packed from slot 0 of dp position p, in order; a row sums to at most 512, zeros are empty slots, and the slots after the sum are padding. One dp position holds a single sequence of 512 tokens.
All inputs are finite; a program needn't handle non-finite values.
Results may differ from the reference program's by a relative error of at most 0.023.
Values may be sent and summed in bfloat16 or wider, within the bound.
No kernel may reach another device: no remote copies, remote signals or barrier semaphores. Data moves between devices by JAX's collectives and lax.ppermute only.
A program may use at most 192 MiB of HBM per device.

```python
import math
import jax
import jax.numpy as jnp
from jax import lax

D = 1024
HEADS = 16
QK = 16
VD = 64
FF = 2752
TOK_DEV = 512
SLOTS = 4
VW = 1024
FPAD = 276
TOKENS = 4096


def draw_lengths(key, part):
    row_count = TOKENS // TOK_DEV
    first_key, second_key = jax.random.split(jax.random.fold_in(key, 11))
    spread = jax.random.randint(first_key, (row_count, SLOTS), TOK_DEV // 16, TOK_DEV // 4 + 1)
    chosen_row = jax.random.randint(second_key, (), 0, row_count)
    picked = jnp.arange(row_count)[:, None] == chosen_row
    leading = jnp.arange(SLOTS)[None, :] == 0
    single = jnp.where(leading, TOK_DEV, 0)
    return jnp.where(picked, single, spread).astype(jnp.int32)


def steps_of(stream_key, shape, pieces, least, high):
    gain = 1.0
    for axis_at, shards_of in pieces:
        draws = jax.random.uniform(jax.random.fold_in(jax.random.fold_in(stream_key, 6), axis_at), (shards_of,), jnp.float32, least / len(pieces), high / len(pieces))
        gain = gain * jnp.repeat(jnp.exp(draws), shape[axis_at] // shards_of).reshape((-1,) + (1,) * (len(shape) - 1 - axis_at))
    return gain


def gaussian(key, extent, scale, limit, cuts=(), kind=jnp.bfloat16):
    loudness = steps_of(key, extent, cuts, -0.22, 0.18) if cuts else 1.0
    result = jax.random.normal(key, extent, jnp.float32) * scale * loudness
    return jnp.minimum(jnp.maximum(result, -limit), limit).astype(kind)


def setup_inputs(seed: int = 0) -> dict:
    keys = jax.random.split(jax.random.key(seed), 13)
    tokens = gaussian(keys[0], (TOKENS, D), 1.0, 6.0, ((0, 8),))
    gain_one = jnp.clip(1.0 + 0.1 * jax.random.normal(keys[1], (D,), jnp.float32), 0.5, 1.5)
    w_query = gaussian(keys[2], (D, HEADS * QK), D ** -0.5, 0.1875)
    w_key = gaussian(keys[3], (D, HEADS * QK), D ** -0.5, 0.1875)
    w_value = gaussian(keys[4], (D, VW), D ** -0.5, 0.1875)
    w_out = gaussian(keys[5], (VW, D), (D // 64) ** -0.5, 1.5)
    gain_two = jnp.clip(1.0 + 0.1 * jax.random.normal(keys[6], (D,), jnp.float32), 0.5, 1.5)
    w_gate = gaussian(keys[7], (D, FF), D ** -0.5, 0.1875, ((1, 4),))
    w_up = gaussian(keys[8], (D, FF), D ** -0.5, 0.1875, ((1, 4),))
    w_down = gaussian(keys[9], (FF, D), FF ** -0.5, 0.109375, ((0, 4),))
    lengths = draw_lengths(jax.random.fold_in(keys[12], 71), 0)
    cotangent = gaussian(keys[11], (TOKENS, D), 1.0, 6.0, ((0, 8),))
    return dict(tokens=tokens, gain_one=gain_one, w_query=w_query, w_key=w_key, w_value=w_value, w_out=w_out, gain_two=gain_two, w_gate=w_gate, w_up=w_up, w_down=w_down, lengths=lengths, cotangent=cotangent)


@jax.custom_vjp
def low(v):
    return lax.optimization_barrier(v.astype(jnp.bfloat16)).astype(jnp.float32)

@jax.custom_vjp
def low_back(v):
    return v

def low_keep(v):
    return (low(v), None)

def low_pass(kept, grad):
    return (grad,)

def back_keep(v):
    return (v, None)

def back_low(kept, grad):
    return (low(grad),)
low.defvjp(low_keep, low_pass)
low_back.defvjp(back_keep, back_low)
EPSILON = 1e-05
HIGH = lax.Precision.HIGHEST

def matmul(left_side, right_side):
    return jnp.dot(left_side, right_side, precision=HIGH)

def rms_scale(values, gain_row):
    return values * lax.rsqrt(lax.optimization_barrier(jnp.mean(values * values, axis=-1, keepdims=True)) + EPSILON) * gain_row

def feature_map(projected, heads_count, width, padded):
    row_count = projected.shape[0]
    split_heads = projected.reshape(row_count, heads_count, width)
    ones_part = jnp.ones((row_count, heads_count, 1), jnp.float32)
    linear = split_heads * width ** (-0.25)
    square = (split_heads[:, :, :, None] * split_heads[:, :, None, :]).reshape(row_count, heads_count, width * width) / math.sqrt(2.0 * width)
    zeros_part = jnp.zeros((row_count, heads_count, padded - 1 - width - width * width), jnp.float32)
    return jnp.concatenate([ones_part, linear, square, zeros_part], axis=2)

def segment_ids(lengths):
    bounds = jnp.cumsum(lengths, axis=1).astype(jnp.int32)
    places = jnp.arange(TOK_DEV, dtype=jnp.int32)
    segments = lax.optimization_barrier(jnp.sum((places[None, :, None] >= bounds[:, None, :]).astype(jnp.int32), axis=2))
    live_rows = places[None, :] < bounds[:, -1:]
    return (segments, live_rows)

def attend_device(inputs):
    query_feats, key_feats, value_rows, segments = inputs
    places = jnp.arange(query_feats.shape[0], dtype=jnp.int32)
    allowed = (places[:, None] >= places[None, :]) & (segments[:, None] == segments[None, :])
    scores = jnp.einsum('ihf,jhf->hij', query_feats, key_feats, precision=HIGH)
    scores = jnp.where(allowed[None], scores, 0.0)
    numerator = jnp.einsum('hij,jhc->ihc', scores, value_rows, precision=HIGH)
    denominator = lax.optimization_barrier(jnp.sum(scores, axis=2)).T
    return (numerator, denominator)

def reference(tokens, gain_one, w_query, w_key, w_value, w_out, gain_two, w_gate, w_up, w_down, lengths, cotangent):
    segments, live_rows = segment_ids(lengths)
    live_mask = live_rows.reshape(-1, 1).astype(jnp.float32)
    device_count = lengths.shape[0]

    def forward(inputs, gain_first, query_weight, key_weight, value_weight, out_weight, gain_second, gate_weight, up_weight, down_weight):
        normed = low(rms_scale(inputs, gain_first))
        queries = low_back(matmul(normed, query_weight))
        key_rows = low_back(matmul(normed, key_weight))
        values = low(low_back(matmul(normed, value_weight)))
        query_feats = low(feature_map(queries, HEADS, QK, FPAD)).reshape(device_count, TOK_DEV, HEADS, FPAD)
        key_feats = low(feature_map(key_rows, HEADS, QK, FPAD)).reshape(device_count, TOK_DEV, HEADS, FPAD)
        value_heads = values.reshape(device_count, TOK_DEV, HEADS, VD)
        numerator, denominator = lax.map(jax.checkpoint(attend_device), (query_feats, key_feats, value_heads, segments))
        context = low(low_back(numerator / denominator[..., None])).reshape(TOKENS, VW)
        mixed_rows = low_back(matmul(context, out_weight))
        residual = inputs + live_mask * mixed_rows
        normed_two = low(rms_scale(residual, gain_second))
        gate_values = low_back(matmul(normed_two, gate_weight))
        up_values = low_back(matmul(normed_two, up_weight))
        inner_rows = low(jax.nn.silu(gate_values) * up_values)
        return residual + live_mask * matmul(inner_rows, down_weight)
    primals = (tokens.astype(jnp.float32), gain_one.astype(jnp.float32), w_query.astype(jnp.float32), w_key.astype(jnp.float32), w_value.astype(jnp.float32), w_out.astype(jnp.float32), gain_two.astype(jnp.float32), w_gate.astype(jnp.float32), w_up.astype(jnp.float32), w_down.astype(jnp.float32))
    output, pullback = jax.vjp(forward, *primals)
    gradients = pullback(cotangent.astype(jnp.float32))
    return (output.astype(jnp.bfloat16), gradients[0].astype(jnp.bfloat16), gradients[1], gradients[2], gradients[3], gradients[4], gradients[5], gradients[6], gradients[7], gradients[8], gradients[9])
```

```python
import math

import jax
import jax.numpy as jnp
from jax import lax
from jax.sharding import PartitionSpec as P

HEADS = 16
QK = 16
VD = 64
BLOCK = 512


EPSILON = 1e-05


def rms_factor(values):
    return lax.rsqrt(jnp.mean(values * values, axis=-1, keepdims=True) + EPSILON)


def norm_back(values, factor, gain_row, incoming):
    weighted = incoming * gain_row
    gain_grad = jnp.sum(incoming * values * factor, axis=0)
    value_grad = factor * weighted - values * factor * factor * factor * jnp.mean(
        weighted * values, axis=-1, keepdims=True
    )
    return (gain_grad, value_grad)


def split_parts(array):
    if array.dtype == jnp.bfloat16:
        return (array,)
    leading = array.astype(jnp.bfloat16)
    remainder = (array - leading.astype(jnp.float32)).astype(jnp.bfloat16)
    return (leading, remainder)


def exact_einsum(form, first, second):
    first_parts = split_parts(first)
    second_parts = split_parts(second)
    total = None
    for left_rank, left_part in enumerate(first_parts):
        for right_rank, right_part in enumerate(second_parts):
            if left_rank + right_rank < 2:
                term = jnp.einsum(form, left_part, right_part, preferred_element_type=jnp.float32)
                total = term if total is None else total + term
    return total


def feature_slice(projected, first_feature, slice_width, padded):
    row_count = projected.shape[0]
    split_heads = projected.reshape(row_count, -1, QK)
    heads_count = split_heads.shape[1]
    ones_part = jnp.ones((row_count, heads_count, 1), jnp.float32)
    linear = split_heads * QK ** (-0.25)
    square = (split_heads[:, :, :, None] * split_heads[:, :, None, :]).reshape(
        row_count, heads_count, QK * QK
    ) / math.sqrt(2.0 * QK)
    zeros_part = jnp.zeros((row_count, heads_count, padded - 1 - QK - QK * QK), jnp.float32)
    whole_map = jnp.concatenate([ones_part, linear, square, zeros_part], axis=2)
    return lax.dynamic_slice_in_dim(whole_map, first_feature, slice_width, 2)


def block_allowed(seg_block):
    places = jnp.arange(seg_block.shape[0], dtype=jnp.int32)
    return (places[:, None] >= places[None, :]) & (seg_block[:, None] == seg_block[None, :])


def segment_states(key_side, value_side, extra_side, seg_blocks, reverse):
    heads_count = key_side.shape[2]
    feature_count = key_side.shape[3]
    column_count = value_side.shape[3]

    def advance(carry_data, block_data):
        carried_state, carried_total, marker = carry_data
        key_block, value_block, extra_block, seg_block = block_data
        edge_segment = seg_block[0] if reverse else seg_block[-1]
        keep_state = (edge_segment == marker).astype(jnp.float32)
        chosen = seg_block == edge_segment
        key_selected = jnp.where(chosen[:, None, None], key_block, jnp.zeros_like(key_block))
        state_next = keep_state * carried_state + exact_einsum(
            "jhf,jhc->hfc", key_selected, value_block
        )
        total_next = keep_state * carried_total + exact_einsum(
            "jhf,jh->hf", key_selected, extra_block
        )
        return ((state_next, total_next, edge_segment), (carried_state, carried_total, marker))

    initial = (
        jnp.zeros((heads_count, feature_count, column_count), jnp.float32),
        jnp.zeros((heads_count, feature_count), jnp.float32),
        jnp.int32(-1),
    )
    _, entering = lax.scan(
        advance, initial, (key_side, value_side, extra_side, seg_blocks), reverse=reverse
    )
    return entering


def forward_block(inputs):
    query_block, key_block, value_block, seg_block, carried_state, carried_total, marker = inputs
    allowed = block_allowed(seg_block)
    scores = jnp.einsum("ihf,jhf->hij", query_block, key_block, preferred_element_type=jnp.float32)
    scores = jnp.where(allowed[None], scores, 0.0)
    numerator = exact_einsum("hij,jhc->ihc", scores, value_block)
    denominator = jnp.sum(scores, axis=2).T
    carried = (seg_block == marker).astype(jnp.float32)
    numerator = numerator + carried[:, None, None] * exact_einsum(
        "ihf,hfc->ihc", query_block, carried_state
    )
    denominator = denominator + carried[:, None] * exact_einsum(
        "ihf,hf->ih", query_block, carried_total
    )
    return (numerator, denominator)


def backward_block(inputs):
    (
        query_block,
        key_block,
        value_block,
        seg_block,
        grad_numer,
        grad_denom,
        carried_state,
        carried_total,
        marker,
        later_state,
        later_total,
        later_marker,
    ) = inputs
    allowed = block_allowed(seg_block)
    scores = jnp.einsum("ihf,jhf->hij", query_block, key_block, preferred_element_type=jnp.float32)
    scores = jnp.where(allowed[None], scores, 0.0)
    grad_scores = exact_einsum("ihc,jhc->hij", grad_numer, value_block) + grad_denom.T[:, :, None]
    grad_scores = jnp.where(allowed[None], grad_scores, 0.0)
    grad_query = exact_einsum("hij,jhf->ihf", grad_scores, key_block)
    grad_key = exact_einsum("hij,ihf->jhf", grad_scores, query_block)
    grad_value = exact_einsum("hij,ihc->jhc", scores, grad_numer)
    forward_on = (seg_block == marker).astype(jnp.float32)[:, None, None]
    grad_query = grad_query + forward_on * (
        exact_einsum("ihc,hfc->ihf", grad_numer, carried_state)
        + grad_denom[:, :, None] * carried_total[None]
    )
    later_on = (seg_block == later_marker).astype(jnp.float32)[:, None, None]
    grad_key = grad_key + later_on * (
        exact_einsum("jhc,hfc->jhf", value_block, later_state) + later_total[None]
    )
    grad_value = grad_value + later_on * exact_einsum("jhf,hfc->jhc", key_block, later_state)
    return (grad_query, grad_key, grad_value)


def local(
    tokens,
    gain_one,
    w_query,
    w_key,
    w_value,
    w_out,
    gain_two,
    w_gate,
    w_up,
    w_down,
    lengths,
    cotangent,
):
    token_count = tokens.shape[0]
    feat_count = lax.axis_size("feat")
    feat_index = lax.axis_index("feat")
    padded = (1 + QK + QK * QK + feat_count - 1) // feat_count * feat_count
    slice_width = padded // feat_count
    head_share = HEADS // feat_count
    column_share = head_share * VD
    block_count = token_count // BLOCK
    places = jnp.arange(token_count, dtype=jnp.int32)
    slots = jnp.arange(lengths.shape[1])
    bounds = jnp.sum(jnp.where(slots[None, :] <= slots[:, None], lengths[0][None, :], 0), axis=1)
    segments = jnp.sum((places[:, None] >= bounds[None, :]).astype(jnp.int32), axis=1)
    live_rows = (places < bounds[-1]).astype(jnp.float32)[:, None]

    def blocked(array):
        return array.reshape((block_count, BLOCK) + array.shape[1:])

    first_feature = feat_index * slice_width

    def make_features(projected):
        return feature_slice(projected, first_feature, slice_width, padded)

    inputs = tokens.astype(jnp.float32)
    scale_one = rms_factor(inputs)
    normed = (inputs * scale_one * gain_one).astype(jnp.bfloat16)
    queries = jnp.dot(normed, w_query, preferred_element_type=jnp.float32)
    key_rows = jnp.dot(normed, w_key, preferred_element_type=jnp.float32)
    values = jnp.dot(normed, w_value, preferred_element_type=jnp.float32).astype(jnp.bfloat16)
    query_feats = make_features(queries).astype(jnp.bfloat16)
    key_feats = make_features(key_rows).astype(jnp.bfloat16)
    value_heads = values.reshape(token_count, -1, VD)
    heads_here = value_heads.shape[1]
    seg_blocks = segments.reshape(block_count, BLOCK)
    query_blocks = blocked(query_feats)
    key_blocks = blocked(key_feats)
    value_blocks = blocked(value_heads)
    ones_extra = jnp.ones((block_count, BLOCK, heads_here), jnp.bfloat16)
    states, totals, markers = segment_states(
        key_blocks, value_blocks, ones_extra, seg_blocks, False
    )
    numerator, denominator = lax.map(
        forward_block, (query_blocks, key_blocks, value_blocks, seg_blocks, states, totals, markers)
    )
    numerator = numerator.reshape(token_count, heads_here * VD)
    denominator = denominator.reshape(token_count, heads_here)
    own_numer, own_denom = (
        lax.psum_scatter(numerator, "feat", scatter_dimension=1, tiled=True),
        lax.psum_scatter(denominator, "feat", scatter_dimension=1, tiled=True),
    )
    context_exact = own_numer.reshape(token_count, head_share, VD) / own_denom[:, :, None]
    context_low = context_exact.reshape(token_count, column_share).astype(jnp.bfloat16)
    out_rows = lax.dynamic_slice_in_dim(w_out, feat_index * column_share, column_share, 0)
    mixed_rows = jnp.dot(
        lax.all_gather(context_low, "feat", axis=1, tiled=True),
        w_out,
        preferred_element_type=jnp.float32,
    )
    residual = inputs + live_rows * mixed_rows
    scale_two = rms_factor(residual)
    normed_two = (residual * scale_two * gain_two).astype(jnp.bfloat16)
    gate_values = jnp.dot(normed_two, w_gate, preferred_element_type=jnp.float32)
    up_values = jnp.dot(normed_two, w_up, preferred_element_type=jnp.float32)
    gate_sigmoid = jax.nn.sigmoid(gate_values)
    activated = gate_values * gate_sigmoid
    inner_rows = (activated * up_values).astype(jnp.bfloat16)
    feed_rows = lax.psum(
        jnp.dot(inner_rows, w_down, preferred_element_type=jnp.float32).astype(jnp.bfloat16), "feat"
    ).astype(jnp.float32)
    output = (residual + live_rows * feed_rows).astype(jnp.bfloat16)
    grad_output = cotangent.astype(jnp.float32)
    grad_feed = (grad_output * live_rows).astype(jnp.bfloat16)
    grad_wdown = jnp.einsum("tf,td->fd", inner_rows, grad_feed, preferred_element_type=jnp.float32)
    grad_inner = jnp.dot(grad_feed, w_down.T, preferred_element_type=jnp.float32)
    grad_gate = (
        grad_inner * up_values * gate_sigmoid * (1.0 + gate_values * (1.0 - gate_sigmoid))
    ).astype(jnp.bfloat16)
    grad_upper = (grad_inner * activated).astype(jnp.bfloat16)
    grad_wgate = jnp.einsum("td,tf->df", normed_two, grad_gate, preferred_element_type=jnp.float32)
    grad_wup = jnp.einsum("td,tf->df", normed_two, grad_upper, preferred_element_type=jnp.float32)
    grad_normed_part = jnp.dot(grad_gate, w_gate.T, preferred_element_type=jnp.float32) + jnp.dot(
        grad_upper, w_up.T, preferred_element_type=jnp.float32
    )
    grad_normed_two = lax.psum(grad_normed_part.astype(jnp.bfloat16), "feat").astype(jnp.float32)
    grad_gain_second, grad_resid_norm = norm_back(residual, scale_two, gain_two, grad_normed_two)
    grad_residual = grad_output + grad_resid_norm
    grad_mixed = (live_rows * grad_residual).astype(jnp.bfloat16)
    grad_wout = jnp.einsum("tc,td->cd", context_low, grad_mixed, preferred_element_type=jnp.float32)
    grad_context = jnp.dot(grad_mixed, out_rows.T, preferred_element_type=jnp.float32).astype(
        jnp.bfloat16
    )
    grad_context_heads = grad_context.astype(jnp.float32).reshape(token_count, head_share, VD)
    grad_own_numer = grad_context_heads / own_denom[:, :, None]
    grad_own_denom = -jnp.sum(grad_context_heads * context_exact, axis=2) / own_denom
    grad_numer, grad_denom = (
        lax.all_gather(
            grad_own_numer.reshape(token_count, column_share).astype(jnp.bfloat16),
            "feat",
            axis=1,
            tiled=True,
        ).astype(jnp.float32),
        lax.all_gather(grad_own_denom.astype(jnp.bfloat16), "feat", axis=1, tiled=True).astype(
            grad_own_denom.dtype
        ),
    )
    grad_numer_blocks = blocked(grad_numer.reshape(token_count, heads_here, VD))
    grad_denom_blocks = blocked(grad_denom)
    later_states, later_totals, later_markers = segment_states(
        query_blocks, grad_numer_blocks, grad_denom_blocks, seg_blocks, True
    )
    grad_qfeat, grad_kfeat, grad_vpart = lax.map(
        backward_block,
        (
            query_blocks,
            key_blocks,
            value_blocks,
            seg_blocks,
            grad_numer_blocks,
            grad_denom_blocks,
            states,
            totals,
            markers,
            later_states,
            later_totals,
            later_markers,
        ),
    )
    _, query_pull = jax.vjp(make_features, queries)
    _, key_pull = jax.vjp(make_features, key_rows)
    grad_query_part = query_pull(grad_qfeat.reshape(token_count, heads_here, slice_width))[0]
    grad_key_part = key_pull(grad_kfeat.reshape(token_count, heads_here, slice_width))[0]
    grad_value_part = grad_vpart.reshape(token_count, heads_here * VD)
    summed_query, summed_key, summed_value = (
        lax.psum(grad_query_part.astype(jnp.bfloat16), "feat").astype(jnp.float32),
        lax.psum(grad_key_part.astype(jnp.bfloat16), "feat").astype(jnp.float32),
        lax.psum(grad_value_part.astype(jnp.bfloat16), "feat").astype(jnp.float32),
    )
    grad_queries = summed_query.astype(jnp.bfloat16)
    grad_keys = summed_key.astype(jnp.bfloat16)
    grad_values = summed_value.astype(jnp.bfloat16)
    grad_wquery = jnp.einsum("td,tk->dk", normed, grad_queries, preferred_element_type=jnp.float32)
    grad_wkey = jnp.einsum("td,tk->dk", normed, grad_keys, preferred_element_type=jnp.float32)
    grad_wvalue = jnp.einsum("td,tk->dk", normed, grad_values, preferred_element_type=jnp.float32)
    grad_normed = (
        jnp.dot(grad_queries, w_query.T, preferred_element_type=jnp.float32)
        + jnp.dot(grad_keys, w_key.T, preferred_element_type=jnp.float32)
        + jnp.dot(grad_values, w_value.T, preferred_element_type=jnp.float32)
    )
    grad_gain_first, grad_input_norm = norm_back(inputs, scale_one, gain_one, grad_normed)
    grad_input = (grad_residual + grad_input_norm).astype(jnp.bfloat16)
    summed_all = (
        lax.psum_scatter(
            grad_wquery.astype(jnp.bfloat16), "dp", scatter_dimension=0, tiled=True
        ).astype(jnp.float32),
        lax.psum_scatter(
            grad_wkey.astype(jnp.bfloat16), "dp", scatter_dimension=0, tiled=True
        ).astype(jnp.float32),
        lax.psum_scatter(
            grad_wvalue.astype(jnp.bfloat16), "dp", scatter_dimension=0, tiled=True
        ).astype(jnp.float32),
        lax.psum_scatter(
            grad_wout.astype(jnp.bfloat16), "dp", scatter_dimension=1, tiled=True
        ).astype(jnp.float32),
        lax.psum_scatter(
            grad_gain_first.astype(jnp.bfloat16), "dp", scatter_dimension=0, tiled=True
        ).astype(jnp.float32),
        lax.psum_scatter(
            grad_wgate.astype(jnp.bfloat16), "dp", scatter_dimension=0, tiled=True
        ).astype(jnp.float32),
        lax.psum_scatter(
            grad_wup.astype(jnp.bfloat16), "dp", scatter_dimension=0, tiled=True
        ).astype(jnp.float32),
        lax.psum_scatter(
            grad_wdown.astype(jnp.bfloat16), "dp", scatter_dimension=1, tiled=True
        ).astype(jnp.float32),
        lax.psum_scatter(
            grad_gain_second.astype(jnp.bfloat16), "dp", scatter_dimension=0, tiled=True
        ).astype(jnp.float32),
    )
    (
        sum_query,
        sum_key,
        sum_value,
        sum_out,
        sum_gain_first,
        sum_gate,
        sum_up,
        sum_down,
        sum_gain_second,
    ) = summed_all
    return (
        output,
        grad_input,
        sum_gain_first,
        sum_query,
        sum_key,
        sum_value,
        sum_out,
        sum_gain_second,
        sum_gate,
        sum_up,
        sum_down,
    )


def solution(mesh):
    in_specs = (
        P("dp", None),
        P(),
        P(),
        P(),
        P(),
        P(),
        P(),
        P(None, "feat"),
        P(None, "feat"),
        P("feat", None),
        P("dp", None),
        P("dp", None),
    )
    out_specs = (
        P("dp", None),
        P("dp", None),
        P("dp"),
        P("dp", None),
        P("dp", None),
        P("dp", None),
        P("feat", "dp"),
        P("dp"),
        P("dp", "feat"),
        P("dp", "feat"),
        P("feat", "dp"),
    )
    return jax.shard_map(local, mesh=mesh, in_specs=in_specs, out_specs=out_specs, check_vma=False)
```

```python
import functools

import jax
import jax.numpy as jnp
from jax import lax
from jax.experimental import pallas as pl
from jax.experimental.pallas import tpu as pltpu
from jax.sharding import PartitionSpec as P

HEADS = 16
QK = 16
VD = 64
EPSILON = 1e-05
F32 = jnp.float32
BF16 = jnp.bfloat16
VMEM_LIMIT = 48 * 1024 * 1024


def dot(a, b):
    return lax.dot_general(a, b, (((1,), (0,)), ((), ())), preferred_element_type=F32)


def dot_nt(a, b):
    return lax.dot_general(a, b, (((1,), (1,)), ((), ())), preferred_element_type=F32)


def dot_tn(a, b):
    return lax.dot_general(a, b, (((0,), (0,)), ((), ())), preferred_element_type=F32)


def lane_mask(shape, width, head):
    return lax.broadcasted_iota(jnp.int32, shape, 1) // width == head


def only_head(array, width, head):
    return jnp.where(lane_mask(array.shape, width, head), array, jnp.zeros_like(array))


def absolute_order(blocks, place):
    blocks = list(blocks)
    mask = 1
    while mask < len(blocks):
        flip = (place & mask) != 0
        blocks = [jnp.where(flip, blocks[j ^ mask], blocks[j]) for j in range(len(blocks))]
        mask *= 2
    return blocks


def attend_kernel(tok, gain, weights, start, n_out, r_out, q_out, k_out, v_out, ctx_out, exact_out, den_out):
    rows = tok.shape[0]
    hq, hv = q_out.shape[1], v_out.shape[1]
    block = rows // 2
    x = tok[...].astype(F32)
    r = lax.rsqrt(jnp.mean(x * x, axis=1, keepdims=True) + EPSILON)
    n = (x * r * gain[...]).astype(BF16)
    n_out[...] = n
    r_out[...] = r
    projected = dot(n, weights[...])
    v = projected[:, :hv].astype(BF16)
    q = (projected[:, hv : hv + hq] * QK**-0.5).astype(BF16)
    k = projected[:, hv + hq :].astype(BF16)
    v_out[...] = v
    q_out[...] = q
    k_out[...] = k
    for part in range(2):
        low, high = part * block, (part + 1) * block
        row = lax.broadcasted_iota(jnp.int32, (block, high), 0) + low
        col = lax.broadcasted_iota(jnp.int32, (block, high), 1)
        allowed = (col <= row) & (col >= start[low:high, :])
        number = jnp.zeros((block, hv), F32)
        total = jnp.zeros((block, hv), F32)
        for head in range(hq // QK):
            t = dot_nt(only_head(q[low:high], QK, head), k[:high]) + 1.0
            p = jnp.where(allowed, t * t + 1.0, 0.0).astype(BF16)
            number = number + dot(p, only_head(v[:high], VD, head))
            ones = jnp.where(lane_mask((high, hv), VD, head), 1.0, 0.0).astype(BF16)
            total = total + dot(p, ones)
        exact = number / total
        exact_out[low:high, :] = exact
        ctx_out[low:high, :] = exact.astype(BF16)
        den_out[low:high, :] = total


def feed_kernel(place, *refs, share):
    ctx = refs[:share]
    tok, live, gain, w_out, w_gate, w_up, w_down, gfeed = refs[share : share + 8]
    res_out, r_out, n_out, inner_out, gg_out, gu_out, back_out = refs[share + 8 :]
    context = jnp.concatenate(absolute_order([c[...] for c in ctx], place[0]), axis=1)
    mixed = dot(context, w_out[...])
    residual = tok[...].astype(F32) + live[...] * mixed
    res_out[...] = residual
    r = lax.rsqrt(jnp.mean(residual * residual, axis=1, keepdims=True) + EPSILON)
    r_out[...] = r
    n = (residual * r * gain[...]).astype(BF16)
    n_out[...] = n
    gate = dot(n, w_gate[...])
    up = dot(n, w_up[...])
    ginner = dot_nt(gfeed[...], w_down[...])
    sig = jax.nn.sigmoid(gate)
    act = gate * sig
    inner_out[...] = (act * up).astype(BF16)
    ggate = (ginner * up * sig * (1.0 + gate * (1.0 - sig))).astype(BF16)
    gup = (ginner * act).astype(BF16)
    gg_out[...] = ggate
    gu_out[...] = gup
    back_out[...] = (dot_nt(ggate, w_gate[...]) + dot_nt(gup, w_up[...])).astype(BF16)


def back_kernel(
    place, own, other, res, r2, cot, live, gain, w_own, start_row, q_in, k_in, v_in, exact_in, den_in,
    gr_out, gm_out, g_out, gain_out, gctx,
):
    rows = res.shape[0]
    hq, hv = q_in.shape[1], v_in.shape[1]
    half = rows // 2
    core = place[0] & 1
    gain_sum = jnp.zeros_like(gain_out)
    for which, source in ((core, own), (1 - core, other)):
        here = pl.ds(pl.multiple_of(which * half, half), half)
        e = source[...].astype(F32)
        residual, r = res[here, :], r2[here, :]
        weighted = e * gain[...]
        gain_sum = gain_sum + jnp.sum(e * residual * r, axis=0, keepdims=True)
        scale = r * r * r * jnp.mean(weighted * residual, axis=1, keepdims=True)
        grad = cot[here, :].astype(F32) + r * weighted - residual * scale
        gr_out[here, :] = grad
        gm = (live[here, :] * grad).astype(BF16)
        gm_out[here, :] = gm
        gctx[here, :] = dot_nt(gm, w_own[...]).astype(BF16)
    gain_out[...] = gain_sum
    number = gctx[...].astype(F32) / den_in[...]
    gn = number.astype(BF16)
    product = number * exact_in[...]
    leading = product.astype(BF16)
    remainder = (product - leading.astype(F32)).astype(BF16)
    select = (
        lax.broadcasted_iota(jnp.int32, (16, hv), 1) // VD == lax.broadcasted_iota(jnp.int32, (16, hv), 0)
    )
    select = jnp.where(select, 1.0, 0.0).astype(BF16)
    shift = dot_nt(select, leading) + dot_nt(select, remainder)
    q, k, v = q_in[...], k_in[...], v_in[...]
    gq = [jnp.zeros((half, hq), F32) for _ in range(2)]
    for part in range(2):
        low, high = part * half, (part + 1) * half
        row = lax.broadcasted_iota(jnp.int32, (half, rows - low), 0) + low
        col = lax.broadcasted_iota(jnp.int32, (half, rows - low), 1) + low
        allowed = (row <= col) & (row >= start_row[:, low:])
        gk = jnp.zeros((half, hq), F32)
        gv = jnp.zeros((half, hv), F32)
        for head in range(hq // QK):
            q_head = only_head(q[low:], QK, head)
            g_head = only_head(gn[low:], VD, head)
            t = dot_nt(k[low:high], q_head) + 1.0
            p = jnp.where(allowed, t * t + 1.0, 0.0).astype(BF16)
            g = dot_nt(v[low:high], g_head) - shift[head : head + 1, low:]
            ds = jnp.where(allowed, g * t, 0.0).astype(BF16)
            gv = gv + dot(p, g_head)
            gk = gk + dot(ds, q_head)
            k_head = only_head(k[low:high], QK, head)
            for second in range(part, 2):
                piece = ds[:, second * half - low : (second + 1) * half - low]
                gq[second] = gq[second] + dot_tn(piece, k_head)
        g_out[low:high, :hv] = gv.astype(BF16)
        g_out[low:high, hv + hq :] = (gk * 2.0).astype(BF16)
    for part in range(2):
        g_out[part * half : (part + 1) * half, hv : hv + hq] = (gq[part] * (2.0 * QK**-0.5)).astype(BF16)


def input_kernel(place, *refs, share, hv, hq):
    grads = refs[:share]
    gr, tok, r1, gain, w_query, w_key, w_value, out = refs[share:]
    blocks = absolute_order([g[...] for g in grads], place[0])
    values = jnp.concatenate([b[:, :hv] for b in blocks], axis=1)
    queries = jnp.concatenate([b[:, hv : hv + hq] for b in blocks], axis=1)
    keys = jnp.concatenate([b[:, hv + hq :] for b in blocks], axis=1)
    e = dot_nt(queries, w_query[...]) + dot_nt(keys, w_key[...]) + dot_nt(values, w_value[...])
    x, r = tok[...].astype(F32), r1[...]
    weighted = e * gain[...]
    scale = r * r * r * jnp.mean(weighted * x, axis=1, keepdims=True)
    out[...] = (gr[...] + r * weighted - x * scale).astype(BF16)


def whole(array):
    return pl.BlockSpec(array.shape, lambda *_: (0,) * len(array.shape))


def by_rows(array, block):
    return pl.BlockSpec((block,) + array.shape[1:], lambda i, *_: (i, 0))


def shape_of(rows, columns, kind):
    return jax.ShapeDtypeStruct((rows, columns), kind)


def params():
    return pltpu.CompilerParams(vmem_limit_bytes=VMEM_LIMIT)


def cost(flops, moved):
    return pl.CostEstimate(flops=flops, bytes_accessed=moved, transcendentals=0)


def local(
    tokens, gain_one, w_query, w_key, w_value, w_out, gain_two, w_gate, w_up, w_down, lengths, cotangent
):
    rows, width = tokens.shape
    share, groups = lax.axis_size("feat"), lax.axis_size("dp")
    feat, group = lax.axis_index("feat"), lax.axis_index("dp")
    hq, hv = w_query.shape[1] // share, w_value.shape[1] // share
    hidden = w_gate.shape[1]
    chunk = width // groups
    place = feat.astype(jnp.int32).reshape(1)
    half = rows // 2

    def swap(array, axis, mask):
        count = share if axis == "feat" else groups
        return lax.ppermute(array, axis, [(i, i ^ mask) for i in range(count)])

    def masks_of(count):
        found, mask = [], 1
        while mask < count:
            found.append(mask)
            mask *= 2
        return found

    feat_masks = masks_of(share)[::-1]
    dp_masks = masks_of(groups)

    def gather_feat(own):
        held = {0: own}
        for mask in feat_masks:
            for j in list(held):
                held[j ^ mask] = swap(held[j], "feat", mask)
        return [held[j] for j in range(share)]

    def sum_feat(part):
        core = feat & 1
        away = lax.dynamic_slice_in_dim(part, (1 - core) * half, half, 0)
        own = lax.dynamic_slice_in_dim(part, core * half, half, 0)
        total = (own.astype(F32) + swap(away, "feat", 1).astype(F32)).astype(BF16)
        for mask in feat_masks[:-1]:
            total = (total.astype(F32) + swap(total, "feat", mask).astype(F32)).astype(BF16)
        return total

    def bit_of(mask):
        return (group & mask) // mask

    def bit_axes(array, masks):
        lead = array.shape[:-1]
        return array.reshape(lead + (2,) * len(masks) + (array.shape[-1] // 2 ** len(masks),))

    def side(array, axis, bit):
        return lax.dynamic_index_in_dim(array, bit, axis, keepdims=False)

    def columns_side(array, mask, away):
        order = dp_masks[::-1]
        bits = bit_axes(array, order)
        bit = bit_of(mask)
        picked = side(bits, 1 + order.index(mask), 1 - bit if away else bit)
        return picked.reshape(array.shape[0], -1)

    def finish(total, masks, hops, lead):
        for mask in hops:
            axis = lead + masks.index(mask)
            bit = bit_of(mask)
            sent = side(total, axis, 1 - bit).astype(BF16)
            total = side(total, axis, bit) + swap(sent, "dp", mask).astype(F32)
            masks = [m for m in masks if m != mask]
        return total

    def sum_rows(left_away, left_keep, right, hops):
        sent = swap(dot_tn(left_away, right).astype(BF16), "dp", hops[0])
        total = dot_tn(left_keep, right) + sent.astype(F32)
        masks = [m for m in dp_masks[::-1] if m != hops[0]]
        total = total.reshape((2,) * len(masks) + (chunk, right.shape[1]))
        return finish(total, masks, hops[1:], 0)

    def sum_columns(left, right_away, right_keep, hops):
        sent = swap(dot_tn(left, right_away).astype(BF16), "dp", hops[0])
        total = dot_tn(left, right_keep) + sent.astype(F32)
        masks = [m for m in dp_masks[::-1] if m != hops[0]]
        total = total.reshape((left.shape[1],) + (2,) * len(masks) + (chunk,))
        return finish(total, masks, hops[1:], 1)

    x_first = dp_masks
    z_first = dp_masks[1:] + dp_masks[:1]

    places = jnp.arange(rows, dtype=jnp.int32)
    slots = jnp.arange(lengths.shape[1], dtype=jnp.int32)
    bounds = jnp.sum(jnp.where(slots[None, :] <= slots[:, None], lengths[0][None, :], 0), axis=1)
    passed = places[:, None] >= bounds[None, :]
    start = jnp.max(jnp.where(passed, bounds[None, :], 0), axis=1)
    live = (places < bounds[-1]).astype(F32)[:, None]

    gain_a, gain_b = gain_one[None, :], gain_two[None, :]

    def own_columns(array, count):
        return lax.dynamic_slice_in_dim(array, feat * count, count, 1)

    w_own = jnp.concatenate(
        [own_columns(w_value, hv), own_columns(w_query, hq), own_columns(w_key, hq)], axis=1
    )
    pack = hv + 2 * hq
    heads = hq // QK
    normed, r_one, q, k, v, ctx, exact, den = pl.pallas_call(
        attend_kernel,
        out_shape=[
            shape_of(rows, width, BF16),
            shape_of(rows, 1, F32),
            shape_of(rows, hq, BF16),
            shape_of(rows, hq, BF16),
            shape_of(rows, hv, BF16),
            shape_of(rows, hv, BF16),
            shape_of(rows, hv, F32),
            shape_of(rows, hv, F32),
        ],
        compiler_params=params(),
        cost_estimate=cost(2 * rows * width * pack + heads * 6 * rows * rows * 256, 4 * rows * width),
        name="attend",
    )(tokens, gain_a, w_own, start[:, None])

    ctx_all = gather_feat(ctx)
    grad_feed = (cotangent.astype(F32) * live).astype(BF16)

    feed_in = [*ctx_all, tokens, live, gain_b, w_out, w_gate, w_up, w_down, grad_feed]
    specs = [by_rows(a, half) for a in ctx_all + [tokens, live]]
    specs += [whole(a) for a in (gain_b, w_out, w_gate, w_up, w_down)] + [by_rows(grad_feed, half)]
    feed_shapes = [
        shape_of(rows, width, F32),
        shape_of(rows, 1, F32),
        shape_of(rows, width, BF16),
        shape_of(rows, hidden, BF16),
        shape_of(rows, hidden, BF16),
        shape_of(rows, hidden, BF16),
        shape_of(rows, width, BF16),
    ]
    residual, r_two, normed_two, inner, grad_gate, grad_up, back_part = pl.pallas_call(
        functools.partial(feed_kernel, share=share),
        grid_spec=pltpu.PrefetchScalarGridSpec(
            num_scalar_prefetch=1,
            grid=(2,),
            in_specs=specs,
            out_specs=[by_rows(s, half) for s in feed_shapes],
        ),
        out_shape=feed_shapes,
        compiler_params=params(),
        cost_estimate=cost(2 * rows * width * (width + 5 * hidden), 16 * width * width),
        name="feed",
    )(place, *feed_in)

    back_own = sum_feat(back_part)
    back_other = swap(back_own, "feat", 1)

    feed_part = dot(inner, w_down).astype(BF16)
    feed_own = sum_feat(feed_part)
    core_start = (feat & 1) * half
    own_rows = lambda array: lax.dynamic_slice_in_dim(array, core_start, half, 0)
    out_own = (own_rows(residual) + own_rows(live) * feed_own.astype(F32)).astype(BF16)
    out_other = swap(out_own, "feat", 1)
    output = jnp.concatenate(absolute_order([out_own, out_other], feat & 1), axis=0)

    n_away, n_keep = columns_side(normed_two, x_first[0], True), columns_side(normed_two, x_first[0], False)
    f_away, f_keep = columns_side(grad_feed, x_first[0], True), columns_side(grad_feed, x_first[0], False)
    sum_down = sum_columns(inner, f_away, f_keep, x_first)
    sum_gate = sum_rows(n_away, n_keep, grad_gate, x_first)
    sum_up = sum_rows(n_away, n_keep, grad_up, x_first)

    w_out_own = lax.dynamic_slice_in_dim(w_out, feat * hv, hv, 0)
    vmem = pl.BlockSpec(memory_space=pltpu.VMEM)
    grad_res, grad_mixed, grads, gain_part = pl.pallas_call(
        back_kernel,
        in_specs=[pl.BlockSpec(memory_space=pltpu.SMEM)] + [vmem] * 14,
        out_shape=[
            shape_of(rows, width, F32),
            shape_of(rows, width, BF16),
            shape_of(rows, pack, BF16),
            shape_of(1, width, F32),
        ],
        scratch_shapes=[pltpu.VMEM((rows, hv), BF16)],
        compiler_params=params(),
        cost_estimate=cost(2 * rows * width * hv + heads * 10 * rows * rows * 256, 12 * rows * width),
        name="back",
    )(
        place, back_own, back_other, residual, r_two, cotangent, live, gain_b, w_out_own, start[None, :],
        q, k, v, exact, den,
    )

    m_away, m_keep = columns_side(grad_mixed, z_first[0], True), columns_side(grad_mixed, z_first[0], False)
    sum_out = sum_columns(ctx, m_away, m_keep, z_first)
    gain_bits = gain_part.reshape((2,) * len(dp_masks) + (chunk,))
    masks = dp_masks[::-1]
    sum_gain_two = gain_bits
    left = list(masks)
    for mask in z_first:
        axis = left.index(mask)
        sent = side(sum_gain_two, axis, 1 - bit_of(mask))
        sum_gain_two = side(sum_gain_two, axis, bit_of(mask)) + swap(sent, "dp", mask)
        left.remove(mask)

    own_away, own_keep = columns_side(normed, x_first[0], True), columns_side(normed, x_first[0], False)
    sum_own = sum_rows(own_away, own_keep, grads, x_first).astype(BF16)

    grads_all = gather_feat(grads)
    in_args = [*grads_all, grad_res, tokens, r_one, gain_a, w_query, w_key, w_value]
    in_specs = [by_rows(a, half) for a in grads_all + [grad_res, tokens, r_one]]
    in_specs += [whole(a) for a in (gain_a, w_query, w_key, w_value)]
    grad_input = pl.pallas_call(
        functools.partial(input_kernel, share=share, hv=hv, hq=hq),
        grid_spec=pltpu.PrefetchScalarGridSpec(
            num_scalar_prefetch=1,
            grid=(2,),
            in_specs=in_specs,
            out_specs=by_rows(shape_of(rows, width, BF16), half),
        ),
        out_shape=shape_of(rows, width, BF16),
        compiler_params=params(),
        cost_estimate=cost(2 * rows * width * pack * share, 12 * rows * width),
        name="grad_input",
    )(place, *in_args)

    sums = absolute_order(gather_feat(sum_own), feat)
    sum_value = jnp.concatenate([s[:, :hv] for s in sums], axis=1).astype(F32)
    sum_query = jnp.concatenate([s[:, hv : hv + hq] for s in sums], axis=1).astype(F32)
    sum_key = jnp.concatenate([s[:, hv + hq :] for s in sums], axis=1).astype(F32)

    def own_chunk(array):
        return lax.dynamic_slice_in_dim(array, group * chunk, chunk, 0)

    sum_gain_one = sum(
        jnp.sum(own_chunk(w).astype(F32) * s, axis=1)
        for w, s in ((w_query, sum_query), (w_key, sum_key), (w_value, sum_value))
    ) / own_chunk(gain_one)

    return (
        output,
        grad_input,
        sum_gain_one,
        sum_query,
        sum_key,
        sum_value,
        sum_out,
        sum_gain_two,
        sum_gate,
        sum_up,
        sum_down,
    )


def solution(mesh):
    in_specs = (
        P("dp", None),
        P(),
        P(),
        P(),
        P(),
        P(),
        P(),
        P(None, "feat"),
        P(None, "feat"),
        P("feat", None),
        P("dp", None),
        P("dp", None),
    )
    out_specs = (
        P("dp", None),
        P("dp", None),
        P("dp"),
        P("dp", None),
        P("dp", None),
        P("dp", None),
        P("feat", "dp"),
        P("dp"),
        P("dp", "feat"),
        P("dp", "feat"),
        P("feat", "dp"),
    )
    return jax.shard_map(local, mesh=mesh, in_specs=in_specs, out_specs=out_specs, check_vma=False)
```

```python
import functools

import jax
import jax.numpy as jnp
from jax import lax
from jax.experimental import pallas as pl
from jax.experimental.pallas import tpu as pltpu
from jax.sharding import PartitionSpec as P

HEADS = 16
QK = 16
VD = 64
EPSILON = 1e-05
F32 = jnp.float32
BF16 = jnp.bfloat16
VMEM_LIMIT = 48 * 1024 * 1024


def dot(a, b):
    return lax.dot_general(a, b, (((1,), (0,)), ((), ())), preferred_element_type=F32)


def dot_nt(a, b):
    return lax.dot_general(a, b, (((1,), (1,)), ((), ())), preferred_element_type=F32)


def dot_tn(a, b):
    return lax.dot_general(a, b, (((0,), (0,)), ((), ())), preferred_element_type=F32)


def lane_mask(shape, width, head):
    return lax.broadcasted_iota(jnp.int32, shape, 1) // width == head


def only_head(array, width, head):
    return jnp.where(lane_mask(array.shape, width, head), array, jnp.zeros_like(array))


def absolute_order(blocks, place):
    blocks = list(blocks)
    mask = 1
    while mask < len(blocks):
        flip = (place & mask) != 0
        blocks = [jnp.where(flip, blocks[j ^ mask], blocks[j]) for j in range(len(blocks))]
        mask *= 2
    return blocks


def bounds_of(lengths):
    bounds, total = [], 0
    for slot in range(lengths.shape[1]):
        total = total + lengths[0, slot]
        bounds.append(total)
    return bounds


def starts_of(bounds, index):
    start = jnp.zeros_like(index)
    for bound in bounds:
        start = jnp.maximum(start, jnp.where(index >= bound, bound, 0))
    return start


def block_columns(ref, index, width):
    if width % 128 == 0:
        return ref[:, pl.ds(pl.multiple_of(index * width, 128), width)]
    each = 128 // width
    wide = ref[:, pl.ds(pl.multiple_of(index // each * 128, 128), 128)]
    picked = wide[:, :width]
    for i in range(1, each):
        picked = jnp.where(index % each == i, wide[:, i * width : (i + 1) * width], picked)
    return picked


def positions(order):
    found = [0]
    for mask in order:
        found = [r for r in found] + [r ^ mask for r in found]
    count = len(found)
    result = []
    for p in range(count):
        r, top = 0, count // 2
        for mask in order:
            if p & top:
                r ^= mask
            top //= 2
        result.append(r)
    return result


def chunk_columns(ref, group, offsets, chunk):
    return jnp.concatenate([block_columns(ref, group ^ r, chunk) for r in offsets], axis=1)


def attend_kernel(
    place, lengths, tok, gain, w_query, w_key, w_value, n_out, r_out, q_out, k_out, v_out, ctx_out, exact_out, den_out
):
    rows = tok.shape[0]
    hq, hv = q_out.shape[1], v_out.shape[1]
    block = rows // 2
    feat = place[0]
    x = tok[...].astype(F32)
    r = lax.rsqrt(jnp.mean(x * x, axis=1, keepdims=True) + EPSILON)
    n = (x * r * gain[...]).astype(BF16)
    n_out[...] = n
    r_out[...] = r
    w_small = jnp.concatenate([block_columns(w_query, feat, hq), block_columns(w_key, feat, hq)], axis=1)
    small = dot(n, w_small)
    v = dot(n, w_value[...]).astype(BF16)
    q = (small[:, :hq] * QK**-0.5).astype(BF16)
    k = small[:, hq:].astype(BF16)
    v_out[...] = v
    q_out[...] = q
    k_out[...] = k
    bounds = bounds_of(lengths)
    for part in range(2):
        low, high = part * block, (part + 1) * block
        row = lax.broadcasted_iota(jnp.int32, (block, high), 0) + low
        col = lax.broadcasted_iota(jnp.int32, (block, high), 1)
        start = starts_of(bounds, lax.broadcasted_iota(jnp.int32, (block, 1), 0) + low)
        allowed = (col <= row) & (col >= start)
        number = jnp.zeros((block, hv), F32)
        total = jnp.zeros((block, hv), F32)
        for head in range(hq // QK):
            t = dot_nt(only_head(q[low:high], QK, head), k[:high]) + 1.0
            p = jnp.where(allowed, t * t + 1.0, 0.0).astype(BF16)
            number = number + dot(p, only_head(v[:high], VD, head))
            ones = jnp.where(lane_mask((high, hv), VD, head), 1.0, 0.0).astype(BF16)
            total = total + dot(p, ones)
        exact = number / total
        exact_out[low:high, :] = exact
        ctx_out[low:high, :] = exact.astype(BF16)
        den_out[low:high, :] = total


def feed_kernel(place, *refs, share):
    lengths = refs[0]
    ctx = refs[1 : 1 + share]
    tok, cot, gain, w_out, w_gate, w_up, w_down = refs[1 + share : 8 + share]
    res_out, r_out, n_out, inner_out, gg_out, gu_out, away_out, own_out = refs[8 + share :]
    step, half = pl.program_id(0), tok.shape[0]
    core = place[0] & 1
    which = jnp.where(step == 0, 1 - core, core)
    index = lax.broadcasted_iota(jnp.int32, (half, 1), 0) + which * half
    live = (index < bounds_of(lengths)[-1]).astype(F32)
    context = jnp.concatenate(absolute_order([c[...] for c in ctx], place[0]), axis=1)
    mixed = dot(context, w_out[...])
    residual = tok[...].astype(F32) + live * mixed
    res_out[...] = residual
    r = lax.rsqrt(jnp.mean(residual * residual, axis=1, keepdims=True) + EPSILON)
    r_out[...] = r
    n = (residual * r * gain[...]).astype(BF16)
    n_out[...] = n
    gate = dot_nt(n, w_gate[...])
    up = dot_nt(n, w_up[...])
    gfeed = (cot[...].astype(F32) * live).astype(BF16)
    ginner = dot_nt(gfeed, w_down[...])
    sig = jax.nn.sigmoid(gate)
    act = gate * sig
    inner_out[...] = (act * up * live).astype(BF16)
    ggate = (ginner * up * sig * (1.0 + gate * (1.0 - sig))).astype(BF16)
    gup = (ginner * act).astype(BF16)
    gg_out[...] = ggate
    gu_out[...] = gup
    back = (dot(ggate, w_gate[...]) + dot(gup, w_up[...])).astype(BF16)

    @pl.when(step == 0)
    def _():
        away_out[...] = back

    @pl.when(step == 1)
    def _():
        own_out[...] = back


def down_kernel(place, inner, w_down, away_out, own_out):
    half = own_out.shape[0]
    core = place[0] & 1
    for which, out in ((1 - core, away_out), (core, own_out)):
        out[...] = dot(inner[pl.ds(pl.multiple_of(which * half, half), half), :], w_down[...]).astype(BF16)


def columns_away_kernel(where, left, right, out, *, order, chunk):
    offsets = positions(order)
    count = len(offsets) // 2
    result = dot_tn(left[...], chunk_columns(right, where[1], offsets[count:], chunk))
    for i in range(count):
        out[i] = result[:, i * chunk : (i + 1) * chunk].astype(BF16)


def columns_keep_kernel(where, left, right, arrived, keep_out, away_out, *, order, chunk):
    offsets = positions(order)
    count = len(offsets) // 2
    result = dot_tn(left[...], chunk_columns(right, where[1], offsets[:count], chunk))
    for i in range(count):
        total = result[:, i * chunk : (i + 1) * chunk] + arrived[i].astype(F32)
        if i < count // 2:
            keep_out[i] = total
        else:
            away_out[i - count // 2] = total.astype(BF16)


def rows_away_kernel(where, left, right, out, *, order, chunk):
    offsets = positions(order)
    count = len(offsets) // 2
    result = dot_tn(chunk_columns(left, where[1], offsets[count:], chunk), right[...])
    for i in range(count):
        out[i] = result[i * chunk : (i + 1) * chunk].astype(BF16)


def rows_keep_kernel(where, left, right, arrived, keep_out, away_out, *, order, chunk):
    offsets = positions(order)
    count = len(offsets) // 2
    result = dot_tn(chunk_columns(left, where[1], offsets[:count], chunk), right[...])
    for i in range(count):
        total = result[i * chunk : (i + 1) * chunk] + arrived[i].astype(F32)
        if i < count // 2:
            keep_out[i] = total
        else:
            away_out[i - count // 2] = total.astype(BF16)


def back_kernel(
    place, lengths, own, other, res, r2, cot, gain, w_own, q_in, k_in, v_in, exact_in, den_in,
    gr_out, gm_out, g_out, gain_out, gctx,
):
    rows = res.shape[0]
    hq, hv = q_in.shape[1], v_in.shape[1]
    half = rows // 2
    core = place[0] & 1
    bounds = bounds_of(lengths)
    gain_sum = jnp.zeros((1, gain_out.shape[1]), F32)
    for which, source in ((core, own), (1 - core, other)):
        here = pl.ds(pl.multiple_of(which * half, half), half)
        live = (lax.broadcasted_iota(jnp.int32, (half, 1), 0) + which * half < bounds[-1]).astype(F32)
        e = source[...].astype(F32)
        residual, r = res[here, :], r2[here, :]
        weighted = e * gain[...]
        gain_sum = gain_sum + jnp.sum(e * residual * r, axis=0, keepdims=True)
        scale = r * r * r * jnp.mean(weighted * residual, axis=1, keepdims=True)
        grad = cot[here, :].astype(F32) + r * weighted - residual * scale
        gr_out[here, :] = grad
        gm = (live * grad).astype(BF16)
        gm_out[here, :] = gm
        gctx[here, :] = dot_nt(gm, w_own[...]).astype(BF16)
    gain_out[...] = gain_sum
    number = gctx[...].astype(F32) / den_in[...]
    gn = number.astype(BF16)
    product = number * exact_in[...]
    leading = product.astype(BF16)
    remainder = (product - leading.astype(F32)).astype(BF16)
    select = (
        lax.broadcasted_iota(jnp.int32, (16, hv), 1) // VD == lax.broadcasted_iota(jnp.int32, (16, hv), 0)
    )
    select = jnp.where(select, 1.0, 0.0).astype(BF16)
    shift = dot_nt(select, leading) + dot_nt(select, remainder)
    q, k, v = q_in[...], k_in[...], v_in[...]
    gq = [jnp.zeros((half, hq), F32) for _ in range(2)]
    for part in range(2):
        low, high = part * half, (part + 1) * half
        row = lax.broadcasted_iota(jnp.int32, (half, rows - low), 0) + low
        col = lax.broadcasted_iota(jnp.int32, (half, rows - low), 1) + low
        start = starts_of(bounds, lax.broadcasted_iota(jnp.int32, (1, rows - low), 1) + low)
        allowed = (row <= col) & (row >= start)
        gk = jnp.zeros((half, hq), F32)
        gv = jnp.zeros((half, hv), F32)
        for head in range(hq // QK):
            q_head = only_head(q[low:], QK, head)
            g_head = only_head(gn[low:], VD, head)
            t = dot_nt(k[low:high], q_head) + 1.0
            p = jnp.where(allowed, t * t + 1.0, 0.0).astype(BF16)
            g = dot_nt(v[low:high], g_head) - shift[head : head + 1, low:]
            ds = jnp.where(allowed, g * t, 0.0).astype(BF16)
            gv = gv + dot(p, g_head)
            gk = gk + dot(ds, q_head)
            k_head = only_head(k[low:high], QK, head)
            for second in range(part, 2):
                piece = ds[:, second * half - low : (second + 1) * half - low]
                gq[second] = gq[second] + dot_tn(piece, k_head)
        g_out[low:high, :hv] = gv.astype(BF16)
        g_out[low:high, hv + hq :] = (gk * 2.0).astype(BF16)
    for part in range(2):
        g_out[part * half : (part + 1) * half, hv : hv + hq] = (gq[part] * (2.0 * QK**-0.5)).astype(BF16)


def out_away_kernel(where, left, right, gain, out, *, order, chunk):
    offsets = positions(order)
    count = len(offsets) // 2
    many = left.shape[1]
    result = dot_tn(left[...], chunk_columns(right, where[1], offsets[count:], chunk))
    gains = chunk_columns(gain, where[1], offsets[count:], chunk)
    for i in range(count):
        out[i, :many, :] = result[:, i * chunk : (i + 1) * chunk].astype(BF16)
        out[i, many:, :] = jnp.broadcast_to(gains[:, i * chunk : (i + 1) * chunk], (16, chunk)).astype(BF16)


def out_keep_kernel(where, left, right, gain, arrived, keep_out, away_out, *, order, chunk):
    offsets = positions(order)
    count = len(offsets) // 2
    many = left.shape[1]
    result = dot_tn(left[...], chunk_columns(right, where[1], offsets[:count], chunk))
    gains = chunk_columns(gain, where[1], offsets[:count], chunk)
    for i in range(count):
        total = result[:, i * chunk : (i + 1) * chunk] + arrived[i, :many, :].astype(F32)
        extra = jnp.broadcast_to(gains[:, i * chunk : (i + 1) * chunk], (16, chunk)) + arrived[i, many:, :].astype(F32)
        if i < count // 2:
            keep_out[i, :many, :] = total
            keep_out[i, many:, :] = extra
        else:
            away_out[i - count // 2, :many, :] = total.astype(BF16)
            away_out[i - count // 2, many:, :] = extra.astype(BF16)


def input_kernel(place, *refs, share, hv, hq):
    grads = refs[:share]
    gr, tok, r1, gain, w_query, w_key, w_value, out = refs[share:]
    blocks = absolute_order([g[...] for g in grads], place[0])
    values = jnp.concatenate([b[:, :hv] for b in blocks], axis=1)
    queries = jnp.concatenate([b[:, hv : hv + hq] for b in blocks], axis=1)
    keys = jnp.concatenate([b[:, hv + hq :] for b in blocks], axis=1)
    e = dot_nt(queries, w_query[...]) + dot_nt(keys, w_key[...]) + dot_nt(values, w_value[...])
    x, r = tok[...].astype(F32), r1[...]
    weighted = e * gain[...]
    scale = r * r * r * jnp.mean(weighted * x, axis=1, keepdims=True)
    out[...] = (gr[...] + r * weighted - x * scale).astype(BF16)


def finish_kernel(where, *refs, share, hv, hq):
    sums = refs[:share]
    gain, w_query, w_key, w_value, q_out, k_out, v_out, gain_out = refs[share:]
    blocks = absolute_order([s[...].astype(F32) for s in sums], where[0])
    values = jnp.concatenate([b[:, :hv] for b in blocks], axis=1)
    queries = jnp.concatenate([b[:, hv : hv + hq] for b in blocks], axis=1)
    keys = jnp.concatenate([b[:, hv + hq :] for b in blocks], axis=1)
    q_out[...] = queries
    k_out[...] = keys
    v_out[...] = values
    total = jnp.sum(values * w_value[...].astype(F32), axis=1, keepdims=True)
    total = total + jnp.sum(queries * w_query[...].astype(F32) + keys * w_key[...].astype(F32), axis=1, keepdims=True)
    spread = jnp.broadcast_to(total, (total.shape[0], total.shape[0]))
    diagonal = lax.broadcasted_iota(jnp.int32, spread.shape, 0) == lax.broadcasted_iota(jnp.int32, spread.shape, 1)
    row = jnp.sum(jnp.where(diagonal, spread, 0.0), axis=0, keepdims=True)
    gain_out[...] = row / block_columns(gain, where[1], gain_out.shape[1])


def whole(array):
    return pl.BlockSpec(array.shape, lambda *_: (0,) * len(array.shape))


SMEM = pl.BlockSpec(memory_space=pltpu.SMEM)


def shape_of(*args):
    return jax.ShapeDtypeStruct(args[:-1], args[-1])


def params():
    return pltpu.CompilerParams(vmem_limit_bytes=VMEM_LIMIT)


def cost(flops, moved):
    return pl.CostEstimate(flops=flops, bytes_accessed=moved, transcendentals=0)


def call(kernel, name, scalars, arrays, shapes, flops, grid=1, specs=None, out_specs=None, scratch=(), **fixed):
    specs, out_specs = specs or {}, out_specs or {}
    moved = sum(a.size * a.dtype.itemsize for a in (*arrays, *shapes))
    return pl.pallas_call(
        functools.partial(kernel, **fixed) if fixed else kernel,
        grid_spec=pltpu.PrefetchScalarGridSpec(
            num_scalar_prefetch=1,
            grid=(grid,),
            in_specs=[specs.get(i, whole(a)) for i, a in enumerate(arrays)],
            out_specs=[out_specs.get(i, whole(s)) for i, s in enumerate(shapes)],
            scratch_shapes=list(scratch),
        ),
        out_shape=list(shapes),
        compiler_params=params(),
        cost_estimate=cost(flops, moved),
        name=name,
    )(scalars, *arrays)


def local(
    tokens, gain_one, w_query, w_key, w_value, w_out, gain_two, w_gate, w_up, w_down, lengths, cotangent
):
    rows, width = tokens.shape
    share, groups = lax.axis_size("feat"), lax.axis_size("dp")
    feat, group = lax.axis_index("feat"), lax.axis_index("dp")
    hq, hv = w_query.shape[1] // share, w_value.shape[1] // share
    hidden = w_gate.shape[1]
    chunk = width // groups
    half = rows // 2
    pack = hv + 2 * hq
    heads = hq // QK
    where = jnp.stack([feat, group]).astype(jnp.int32)
    w_gate, w_up = w_gate.T, w_up.T
    gain_a, gain_b = gain_one[None, :], gain_two[None, :]

    def swap(array, axis, mask):
        count = share if axis == "feat" else groups
        return lax.ppermute(array, axis, [(i, i ^ mask) for i in range(count)])

    def masks_of(count):
        found, mask = [], 1
        while mask < count:
            found.append(mask)
            mask *= 2
        return found

    feat_masks = masks_of(share)[::-1]
    dp_masks = masks_of(groups)
    x_first = dp_masks
    z_first = dp_masks[1:] + dp_masks[:1]

    def gather_feat(own):
        held = {0: own}
        for mask in feat_masks:
            for j in list(held):
                held[j ^ mask] = swap(held[j], "feat", mask)
        return [held[j] for j in range(share)]

    def sum_feat(away, own):
        total = (own.astype(F32) + swap(away, "feat", 1).astype(F32)).astype(BF16)
        for mask in feat_masks[:-1]:
            total = (total.astype(F32) + swap(total, "feat", mask).astype(F32)).astype(BF16)
        return total

    def finish(keep, away, hops):
        for mask in hops:
            total = keep + swap(away, "dp", mask).astype(F32)
            count = total.shape[0] // 2
            keep, away = (total[:count], total[count:].astype(BF16)) if count else (total, None)
        return total[0]

    def reduce_dp(kinds, name, arrays, block, flops, order):
        away_kernel, keep_kernel = kinds
        count = groups // 2
        fixed = dict(order=tuple(order), chunk=chunk)
        [away] = call(
            away_kernel, name + "_away", where, arrays, [shape_of(count, *block, BF16)], flops, **fixed
        )
        arrived = swap(away, "dp", order[0])
        keep, away = call(
            keep_kernel,
            name + "_keep",
            where,
            [*arrays, arrived],
            [shape_of(count // 2, *block, F32), shape_of(count // 2, *block, BF16)],
            flops,
            **fixed,
        )
        return finish(keep, away, order[1:])

    columns = (columns_away_kernel, columns_keep_kernel)

    normed, r_one, q, k, v, ctx, exact, den = call(
        attend_kernel,
        "attend",
        where,
        [lengths, tokens, gain_a, w_query, w_key, w_value],
        [
            shape_of(rows, width, BF16),
            shape_of(rows, 1, F32),
            shape_of(rows, hq, BF16),
            shape_of(rows, hq, BF16),
            shape_of(rows, hv, BF16),
            shape_of(rows, hv, BF16),
            shape_of(rows, hv, F32),
            shape_of(rows, hv, F32),
        ],
        2 * rows * width * pack + heads * 6 * rows * rows * 256,
        specs={0: SMEM, 5: pl.BlockSpec((width, hv), lambda i, p: (0, p[0]))},
    )

    ctx_all = gather_feat(ctx)

    def by_half(array):
        return pl.BlockSpec(
            (half,) + array.shape[1:], lambda i, p: (jnp.where(i == 0, 1 - (p[0] & 1), p[0] & 1), 0)
        )

    feed_in = [lengths, *ctx_all, tokens, cotangent, gain_b, w_out, w_gate, w_up, w_down]
    feed_shapes = [
        shape_of(rows, width, F32),
        shape_of(rows, 1, F32),
        shape_of(rows, width, BF16),
        shape_of(rows, hidden, BF16),
        shape_of(rows, hidden, BF16),
        shape_of(rows, hidden, BF16),
        shape_of(half, width, BF16),
        shape_of(half, width, BF16),
    ]
    residual, r_two, normed_two, inner, grad_gate, grad_up, back_away, back_own = call(
        feed_kernel,
        "feed",
        where,
        feed_in,
        feed_shapes,
        2 * rows * width * (width + 5 * hidden),
        grid=2,
        specs={0: SMEM, **{i: by_half(feed_in[i]) for i in range(1, share + 3)}},
        out_specs={i: by_half(feed_shapes[i]) for i in range(6)},
        share=share,
    )

    back_own = sum_feat(back_away, back_own)
    back_other = swap(back_own, "feat", 1)

    hidden_flops = rows * width * hidden
    sum_gate = reduce_dp(columns, "gate", [grad_gate, normed_two], (hidden, chunk), hidden_flops, x_first)
    sum_down = reduce_dp(columns, "down", [inner, cotangent], (hidden, chunk), hidden_flops, z_first)
    sum_up = reduce_dp(columns, "up", [grad_up, normed_two], (hidden, chunk), hidden_flops, x_first)

    feed_own = sum_feat(
        *call(
            down_kernel,
            "down",
            where,
            [inner, w_down],
            [shape_of(half, width, BF16)] * 2,
            2 * hidden_flops,
        )
    )
    core_start = (feat & 1) * half
    out_own = (lax.dynamic_slice_in_dim(residual, core_start, half, 0) + feed_own.astype(F32)).astype(BF16)
    out_other = swap(out_own, "feat", 1)
    output = jnp.concatenate(absolute_order([out_own, out_other], feat & 1), axis=0)

    grad_res, grad_mixed, grads, gain_part = call(
        back_kernel,
        "back",
        where,
        [lengths, back_own, back_other, residual, r_two, cotangent, gain_b, w_out, q, k, v, exact, den],
        [
            shape_of(rows, width, F32),
            shape_of(rows, width, BF16),
            shape_of(rows, pack, BF16),
            shape_of(1, width, F32),
        ],
        2 * rows * width * hv + heads * 10 * rows * rows * 256,
        specs={0: SMEM, 7: pl.BlockSpec((hv, width), lambda i, p: (p[0], 0))},
        scratch=[pltpu.VMEM((rows, hv), BF16)],
    )

    sum_own = reduce_dp(
        (rows_away_kernel, rows_keep_kernel), "own", [normed, grads], (chunk, pack), rows * width * pack, x_first
    ).astype(BF16)
    sum_out = reduce_dp(
        (out_away_kernel, out_keep_kernel),
        "out",
        [ctx, grad_mixed, gain_part],
        (hv + 16, chunk),
        rows * width * hv,
        z_first,
    )

    grads_all = gather_feat(grads)
    in_args = [*grads_all, grad_res, tokens, r_one, gain_a, w_query, w_key, w_value]

    def by_rows(array):
        return pl.BlockSpec((half,) + array.shape[1:], lambda i, p: (i, 0))

    [grad_input] = call(
        input_kernel,
        "grad_input",
        where,
        in_args,
        [shape_of(rows, width, BF16)],
        2 * rows * width * pack * share,
        grid=2,
        specs={i: by_rows(in_args[i]) for i in range(share + 3)},
        out_specs={0: pl.BlockSpec((half, width), lambda i, p: (i, 0))},
        share=share,
        hv=hv,
        hq=hq,
    )

    def own_rows(array):
        return pl.BlockSpec((chunk, array.shape[1]), lambda i, p: (p[1], 0))

    sum_query, sum_key, sum_value, sum_gain_one = call(
        finish_kernel,
        "finish",
        where,
        [*gather_feat(sum_own), gain_a, w_query, w_key, w_value],
        [
            shape_of(chunk, hq * share, F32),
            shape_of(chunk, hq * share, F32),
            shape_of(chunk, hv * share, F32),
            shape_of(1, chunk, F32),
        ],
        chunk * pack * share,
        specs={
            share + 1: own_rows(w_query),
            share + 2: own_rows(w_key),
            share + 3: own_rows(w_value),
        },
        share=share,
        hv=hv,
        hq=hq,
    )

    return (
        output,
        grad_input,
        sum_gain_one[0],
        sum_query,
        sum_key,
        sum_value,
        sum_out[:hv],
        sum_out[hv],
        sum_gate.T,
        sum_up.T,
        sum_down,
    )


def solution(mesh):
    in_specs = (
        P("dp", None),
        P(),
        P(),
        P(),
        P(),
        P(),
        P(),
        P(None, "feat"),
        P(None, "feat"),
        P("feat", None),
        P("dp", None),
        P("dp", None),
    )
    out_specs = (
        P("dp", None),
        P("dp", None),
        P("dp"),
        P("dp", None),
        P("dp", None),
        P("dp", None),
        P("feat", "dp"),
        P("dp"),
        P("dp", "feat"),
        P("dp", "feat"),
        P("feat", "dp"),
    )
    return jax.shard_map(local, mesh=mesh, in_specs=in_specs, out_specs=out_specs, check_vma=False)
```

```python
import functools

import jax
import jax.numpy as jnp
from jax import lax
from jax.experimental import pallas as pl
from jax.experimental.pallas import tpu as pltpu
from jax.sharding import PartitionSpec as P

HEADS = 16
QK = 16
VD = 64
EPSILON = 1e-05
F32 = jnp.float32
BF16 = jnp.bfloat16
VMEM_LIMIT = 20 * 1024 * 1024


def dot(a, b):
    return lax.dot_general(a, b, (((1,), (0,)), ((), ())), preferred_element_type=F32)


def dot_nt(a, b):
    return lax.dot_general(a, b, (((1,), (1,)), ((), ())), preferred_element_type=F32)


def dot_tn(a, b):
    return lax.dot_general(a, b, (((0,), (0,)), ((), ())), preferred_element_type=F32)


def lane_mask(shape, width, head):
    return lax.broadcasted_iota(jnp.int32, shape, 1) // width == head


def only_head(array, width, head):
    return jnp.where(lane_mask(array.shape, width, head), array, jnp.zeros_like(array))


def absolute_order(blocks, place):
    blocks = list(blocks)
    mask = 1
    while mask < len(blocks):
        flip = (place & mask) != 0
        blocks = [jnp.where(flip, blocks[j ^ mask], blocks[j]) for j in range(len(blocks))]
        mask *= 2
    return blocks


def bounds_of(where):
    bounds, total = [], 0
    for slot in range(2, where.shape[0]):
        total = total + where[slot]
        bounds.append(total)
    return bounds


def starts_of(bounds, index):
    start = jnp.zeros_like(index)
    for bound in bounds:
        start = jnp.maximum(start, jnp.where(index >= bound, bound, 0))
    return start


def pick_columns(wide, index, width):
    each = wide.shape[1] // width
    picked = wide[:, :width]
    for i in range(1, each):
        picked = jnp.where(index % each == i, wide[:, i * width : (i + 1) * width], picked)
    return picked


def block_columns(ref, index, width):
    if width % 128 == 0:
        return ref[:, pl.ds(pl.multiple_of(index * width, 128), width)]
    each = 128 // width
    return pick_columns(ref[:, pl.ds(pl.multiple_of(index // each * 128, 128), 128)], index, width)


def positions(order):
    found = [0]
    for mask in order:
        found = [r for r in found] + [r ^ mask for r in found]
    count = len(found)
    result = []
    for p in range(count):
        r, top = 0, count // 2
        for mask in order:
            if p & top:
                r ^= mask
            top //= 2
        result.append(r)
    return result


def chunk_columns(ref, group, offsets, chunk):
    return jnp.concatenate([block_columns(ref, group ^ r, chunk) for r in offsets], axis=1)


def attend_kernel(
    where, tok, gain, w_query, w_key, w_value, *refs
):
    later, (n_out, q_out, k_out, v_out, ctx_out, den_out), kept, sems = refs[:4], refs[4:10], refs[10:14], refs[14]
    copies = [pltpu.make_async_copy(a, b, sems.at[i]) for i, (a, b) in enumerate(zip(later, kept))]
    for copy in copies:
        copy.start()
    rows = tok.shape[0]
    hq, hv = q_out.shape[1], v_out.shape[1]
    block = rows // 2
    feat = where[0]
    x = tok[...].astype(F32)
    r = lax.rsqrt(jnp.mean(x * x, axis=1, keepdims=True) + EPSILON)
    n = (x * r * gain[...]).astype(BF16)
    n_out[...] = n
    small = dot(n, jnp.concatenate([w_query[...], w_key[...]], axis=1))
    v = dot(n, w_value[...]).astype(BF16)
    wide = w_query.shape[1]
    q = (pick_columns(small[:, :wide], feat, hq) * QK**-0.5).astype(BF16)
    k = pick_columns(small[:, wide:], feat, hq).astype(BF16)
    v_out[...] = v
    q_out[...] = q
    k_out[...] = k
    bounds = bounds_of(where)
    for part in range(2):
        low, high = part * block, (part + 1) * block
        row = lax.broadcasted_iota(jnp.int32, (block, high), 0) + low
        col = lax.broadcasted_iota(jnp.int32, (block, high), 1)
        start = starts_of(bounds, lax.broadcasted_iota(jnp.int32, (block, 1), 0) + low)
        allowed = (col <= row) & (col >= start)
        number = jnp.zeros((block, hv), F32)
        total = jnp.zeros((block, hv), F32)
        for head in range(hq // QK):
            t = dot_nt(only_head(q[low:high], QK, head), k[:high]) + 1.0
            p = jnp.where(allowed, t * t + 1.0, 0.0).astype(BF16)
            number = number + dot(p, only_head(v[:high], VD, head))
            ones = jnp.where(lane_mask((high, hv), VD, head), 1.0, 0.0).astype(BF16)
            total = total + dot(p, ones)
        ctx_out[low:high, :] = (number / total).astype(BF16)
        den_out[low:high, :] = total
    for copy in copies:
        copy.wait()


def feed_kernel(place, *refs, share):
    ctx = refs[:share]
    tok, cot, gain, w_out, w_gate, w_up, w_down = refs[share : 7 + share]
    res_out, n_out, inner_out, gg_out, gu_out, away_out, own_out = refs[7 + share :]
    step, half = pl.program_id(0), tok.shape[0]
    core = place[0] & 1
    which = jnp.where(step == 0, 1 - core, core)
    index = lax.broadcasted_iota(jnp.int32, (half, 1), 0) + which * half
    live = (index < bounds_of(place)[-1]).astype(F32)
    context = jnp.concatenate(absolute_order([c[...] for c in ctx], place[0]), axis=1)
    mixed = dot(context, w_out[...])
    residual = tok[...].astype(F32) + live * mixed
    res_out[...] = residual
    r = lax.rsqrt(jnp.mean(residual * residual, axis=1, keepdims=True) + EPSILON)
    n = (residual * r * gain[...]).astype(BF16)
    n_out[...] = n
    gate = dot_nt(n, w_gate[...])
    up = dot_nt(n, w_up[...])
    gfeed = (cot[...].astype(F32) * live).astype(BF16)
    ginner = dot_nt(gfeed, w_down[...])
    sig = jax.nn.sigmoid(gate)
    act = gate * sig
    inner_out[...] = (act * up * live).astype(BF16)
    ggate = (ginner * up * sig * (1.0 + gate * (1.0 - sig))).astype(BF16)
    gup = (ginner * act).astype(BF16)
    gg_out[...] = ggate
    gu_out[...] = gup
    back = (dot(ggate, w_gate[...]) + dot(gup, w_up[...])).astype(BF16)

    @pl.when(step == 0)
    def _():
        away_out[...] = back

    @pl.when(step == 1)
    def _():
        own_out[...] = back


def down_kernel(place, inner, w_down, away_out, own_out):
    half = own_out.shape[0]
    core = place[0] & 1
    for which, out in ((1 - core, away_out), (core, own_out)):
        out[...] = dot(inner[pl.ds(pl.multiple_of(which * half, half), half), :], w_down[...]).astype(BF16)


def columns_away_kernel(where, left, right, out, *, order, chunk):
    offsets = positions(order)
    count = len(offsets) // 2
    result = dot_tn(left[...], chunk_columns(right, where[1], offsets[count:], chunk))
    for i in range(count):
        out[i] = result[:, i * chunk : (i + 1) * chunk].astype(BF16)


def pair_away_kernel(where, first, second, right, first_out, second_out, *, orders, chunk):
    for left, out, order in ((first, first_out, orders[0]), (second, second_out, orders[1])):
        columns_away_kernel(where, left, right, out, order=order, chunk=chunk)


def columns_keep_kernel(where, left, right, arrived, keep_out, away_out, *, order, chunk):
    offsets = positions(order)
    count = len(offsets) // 2
    result = dot_tn(left[...], chunk_columns(right, where[1], offsets[:count], chunk))
    for i in range(count):
        total = result[:, i * chunk : (i + 1) * chunk] + arrived[i].astype(F32)
        if i < count // 2:
            keep_out[i] = total
        else:
            away_out[i - count // 2] = total.astype(BF16)


def rows_away_kernel(where, left, right, out, *, order, chunk):
    offsets = positions(order)
    count = len(offsets) // 2
    result = dot_tn(chunk_columns(left, where[1], offsets[count:], chunk), right[...])
    for i in range(count):
        out[i] = result[i * chunk : (i + 1) * chunk].astype(BF16)


def rows_direct_kernel(where, left, right, arrived, *outs, order, chunk):
    offsets = positions(order)
    count = len(offsets) // 2
    result = dot_tn(chunk_columns(left, where[1], offsets[:count], chunk), right[...])
    for i in range(count):
        total = result[i * chunk : (i + 1) * chunk] + arrived[i].astype(F32)
        outs[i][...] = total.astype(outs[i].dtype)


def back_kernel(
    place, own, other, res, cot, gain, w_own, q_in, k_in, v_in, ctx_in, den_in,
    gr_out, gm_out, g_out, gain_out, gctx,
):
    rows = res.shape[0]
    hq, hv = q_in.shape[1], v_in.shape[1]
    half = rows // 2
    core = place[0] & 1
    bounds = bounds_of(place)
    gain_sum = jnp.zeros((1, gain_out.shape[1]), F32)
    for which, source in ((core, own), (1 - core, other)):
        here = pl.ds(pl.multiple_of(which * half, half), half)
        live = (lax.broadcasted_iota(jnp.int32, (half, 1), 0) + which * half < bounds[-1]).astype(F32)
        e = source[...].astype(F32)
        residual = res[here, :]
        r = lax.rsqrt(jnp.mean(residual * residual, axis=1, keepdims=True) + EPSILON)
        weighted = e * gain[...]
        gain_sum = gain_sum + jnp.sum(e * residual * r, axis=0, keepdims=True)
        scale = r * r * r * jnp.mean(weighted * residual, axis=1, keepdims=True)
        grad = cot[here, :].astype(F32) + r * weighted - residual * scale
        gr_out[here, :] = grad
        gm = (live * grad).astype(BF16)
        gm_out[here, :] = gm
        gctx[here, :] = dot_nt(gm, w_own[...]).astype(BF16)
    gain_out[...] = gain_sum
    number = gctx[...].astype(F32) / den_in[...]
    gn = number.astype(BF16)
    product = number * ctx_in[...].astype(F32)
    leading = product.astype(BF16)
    remainder = (product - leading.astype(F32)).astype(BF16)
    select = (
        lax.broadcasted_iota(jnp.int32, (16, hv), 1) // VD == lax.broadcasted_iota(jnp.int32, (16, hv), 0)
    )
    select = jnp.where(select, 1.0, 0.0).astype(BF16)
    shift = dot_nt(select, leading) + dot_nt(select, remainder)
    q, k, v = q_in[...], k_in[...], v_in[...]
    gq = [jnp.zeros((half, hq), F32) for _ in range(2)]
    for part in range(2):
        low, high = part * half, (part + 1) * half
        row = lax.broadcasted_iota(jnp.int32, (half, rows - low), 0) + low
        col = lax.broadcasted_iota(jnp.int32, (half, rows - low), 1) + low
        start = starts_of(bounds, lax.broadcasted_iota(jnp.int32, (1, rows - low), 1) + low)
        allowed = (row <= col) & (row >= start)
        gk = jnp.zeros((half, hq), F32)
        gv = jnp.zeros((half, hv), F32)
        for head in range(hq // QK):
            q_head = only_head(q[low:], QK, head)
            g_head = only_head(gn[low:], VD, head)
            t = dot_nt(k[low:high], q_head) + 1.0
            p = jnp.where(allowed, t * t + 1.0, 0.0).astype(BF16)
            g = dot_nt(v[low:high], g_head) - shift[head : head + 1, low:]
            ds = jnp.where(allowed, g * t, 0.0).astype(BF16)
            gv = gv + dot(p, g_head)
            gk = gk + dot(ds, q_head)
            k_head = only_head(k[low:high], QK, head)
            for second in range(part, 2):
                piece = ds[:, second * half - low : (second + 1) * half - low]
                gq[second] = gq[second] + dot_tn(piece, k_head)
        g_out[low:high, :hv] = gv.astype(BF16)
        g_out[low:high, hv + hq :] = (gk * 2.0).astype(BF16)
    for part in range(2):
        g_out[part * half : (part + 1) * half, hv : hv + hq] = (gq[part] * (2.0 * QK**-0.5)).astype(BF16)


def out_away_kernel(where, left, right, gain, out, *, order, chunk):
    offsets = positions(order)
    count = len(offsets) // 2
    many = left.shape[1]
    result = dot_tn(left[...], chunk_columns(right, where[1], offsets[count:], chunk))
    gains = chunk_columns(gain, where[1], offsets[count:], chunk)
    for i in range(count):
        out[i, :many, :] = result[:, i * chunk : (i + 1) * chunk].astype(BF16)
        out[i, many:, :] = jnp.broadcast_to(gains[:, i * chunk : (i + 1) * chunk], (16, chunk)).astype(BF16)


def out_keep_kernel(where, left, right, gain, arrived, keep_out, away_out, *, order, chunk):
    offsets = positions(order)
    count = len(offsets) // 2
    many = left.shape[1]
    result = dot_tn(left[...], chunk_columns(right, where[1], offsets[:count], chunk))
    gains = chunk_columns(gain, where[1], offsets[:count], chunk)
    for i in range(count):
        total = result[:, i * chunk : (i + 1) * chunk] + arrived[i, :many, :].astype(F32)
        extra = jnp.broadcast_to(gains[:, i * chunk : (i + 1) * chunk], (16, chunk)) + arrived[i, many:, :].astype(F32)
        if i < count // 2:
            keep_out[i, :many, :] = total
            keep_out[i, many:, :] = extra
        else:
            away_out[i - count // 2, :many, :] = total.astype(BF16)
            away_out[i - count // 2, many:, :] = extra.astype(BF16)


def input_kernel(place, *refs, share, hv, hq):
    grads = refs[:share]
    gr, tok, gain, w_query, w_key, w_value, out = refs[share:]
    blocks = absolute_order([g[...] for g in grads], place[0])
    values = jnp.concatenate([b[:, :hv] for b in blocks], axis=1)
    queries = jnp.concatenate([b[:, hv : hv + hq] for b in blocks], axis=1)
    keys = jnp.concatenate([b[:, hv + hq :] for b in blocks], axis=1)
    e = dot_nt(queries, w_query[...]) + dot_nt(keys, w_key[...]) + dot_nt(values, w_value[...])
    x = tok[...].astype(F32)
    r = lax.rsqrt(jnp.mean(x * x, axis=1, keepdims=True) + EPSILON)
    weighted = e * gain[...]
    scale = r * r * r * jnp.mean(weighted * x, axis=1, keepdims=True)
    out[...] = (gr[...] + r * weighted - x * scale).astype(BF16)


def finish_kernel(where, *refs, share, hv, hq):
    sums = refs[:share]
    gain, w_query, w_key, w_value, q_out, k_out, v_out, gain_out = refs[share:]
    blocks = absolute_order([s[...].astype(F32) for s in sums], where[0])
    values = jnp.concatenate([b[:, :hv] for b in blocks], axis=1)
    queries = jnp.concatenate([b[:, hv : hv + hq] for b in blocks], axis=1)
    keys = jnp.concatenate([b[:, hv + hq :] for b in blocks], axis=1)
    q_out[...] = queries
    k_out[...] = keys
    v_out[...] = values
    total = jnp.sum(values * w_value[...].astype(F32), axis=1, keepdims=True)
    total = total + jnp.sum(queries * w_query[...].astype(F32) + keys * w_key[...].astype(F32), axis=1, keepdims=True)
    spread = jnp.broadcast_to(total, (total.shape[0], total.shape[0]))
    diagonal = lax.broadcasted_iota(jnp.int32, spread.shape, 0) == lax.broadcasted_iota(jnp.int32, spread.shape, 1)
    row = jnp.sum(jnp.where(diagonal, spread, 0.0), axis=0, keepdims=True)
    gain_out[...] = row / block_columns(gain, where[1], gain_out.shape[1])


def whole(array):
    return pl.BlockSpec(array.shape, lambda *_: (0,) * len(array.shape))


def shape_of(*args):
    return jax.ShapeDtypeStruct(args[:-1], args[-1])


def hbm_of(*args):
    return pltpu.HBM(args[:-1], args[-1])


def params():
    return pltpu.CompilerParams(vmem_limit_bytes=VMEM_LIMIT)


def call(kernel, name, scalars, arrays, shapes, flops, grid=1, specs=None, out_specs=None, scratch=(), **fixed):
    specs, out_specs = specs or {}, out_specs or {}
    return pl.pallas_call(
        functools.partial(kernel, **fixed) if fixed else kernel,
        grid_spec=pltpu.PrefetchScalarGridSpec(
            num_scalar_prefetch=1,
            grid=(grid,),
            in_specs=[specs.get(i, whole(a)) for i, a in enumerate(arrays)],
            out_specs=[out_specs.get(i, whole(s)) for i, s in enumerate(shapes)],
            scratch_shapes=list(scratch),
        ),
        out_shape=list(shapes),
        compiler_params=params(),
        cost_estimate=pl.CostEstimate(flops=1000, bytes_accessed=1000, transcendentals=0),
        name=name,
    )(scalars, *arrays)


def after(arrays, *earlier):
    held = lax.optimization_barrier((*arrays, *earlier))
    return held[: len(arrays)]


def in_hbm(array):
    return pltpu.with_memory_space_constraint(array, pltpu.HBM)


def local(
    tokens, gain_one, w_query, w_key, w_value, w_out, gain_two, w_gate, w_up, w_down, lengths, cotangent
):
    rows, width = tokens.shape
    share, groups = lax.axis_size("feat"), lax.axis_size("dp")
    feat, group = lax.axis_index("feat"), lax.axis_index("dp")
    hq, hv = w_query.shape[1] // share, w_value.shape[1] // share
    hidden = w_gate.shape[1]
    chunk = width // groups
    half = rows // 2
    pack = hv + 2 * hq
    heads = hq // QK
    where = jnp.concatenate([jnp.stack([feat, group]).astype(jnp.int32), lengths[0]])
    w_gate, w_up = w_gate.T, w_up.T
    gain_a, gain_b = gain_one[None, :], gain_two[None, :]

    def swap(array, axis, mask):
        count = share if axis == "feat" else groups
        return lax.ppermute(array, axis, [(i, i ^ mask) for i in range(count)])

    def masks_of(count):
        found, mask = [], 1
        while mask < count:
            found.append(mask)
            mask *= 2
        return found

    feat_masks = masks_of(share)[::-1]
    dp_masks = masks_of(groups)
    x_first = dp_masks
    z_first = dp_masks[1:] + dp_masks[:1]

    def gather_feat(own):
        held = {0: own}
        for mask in feat_masks:
            for j in list(held):
                held[j ^ mask] = swap(held[j], "feat", mask)
        return [held[j] for j in range(share)]

    def sum_feat(away, own):
        total = (own.astype(F32) + swap(away, "feat", 1).astype(F32)).astype(BF16)
        for mask in feat_masks[:-1]:
            total = (total.astype(F32) + swap(total, "feat", mask).astype(F32)).astype(BF16)
        return total

    def finish(keep, away, hops):
        for mask in hops:
            total = keep + swap(away, "dp", mask).astype(F32)
            count = total.shape[0] // 2
            keep, away = (total[:count], total[count:].astype(BF16)) if count else (total, None)
        return total[0]

    def first_hop(kind, name, arrays, block, flops, order):
        fixed = dict(order=tuple(order), chunk=chunk)
        [away] = call(
            kind, name + "_away", where, arrays, [shape_of(groups // 2, *block, BF16)], flops, **fixed
        )
        return away, swap(away, "dp", order[0])

    def last_hops(kind, name, arrays, arrived, block, flops, order):
        fixed = dict(order=tuple(order), chunk=chunk)
        keep, away = call(
            kind,
            name + "_keep",
            where,
            [*arrays, arrived],
            [shape_of(groups // 4, *block, F32), shape_of(groups // 4, *block, BF16)],
            flops,
            **fixed,
        )
        return keep, away

    wide = max(hq, 128)
    near = pl.BlockSpec((width, wide), lambda i, p: (0, p[0] * hq // wide))
    anywhere = pl.BlockSpec(memory_space=pl.ANY)
    later = [w_out, w_gate, w_up, w_down]
    normed, q, k, v, ctx, den, w_out, w_gate, w_up, w_down = call(
        attend_kernel,
        "attend",
        where,
        [in_hbm(a) for a in (tokens, gain_a, w_query, w_key, w_value, *later)],
        [
            hbm_of(rows, width, BF16),
            hbm_of(rows, hq, BF16),
            hbm_of(rows, hq, BF16),
            hbm_of(rows, hv, BF16),
            shape_of(rows, hv, BF16),
            hbm_of(rows, hv, F32),
            *(pltpu.VMEM(a.shape, a.dtype) for a in later),
        ],
        2 * rows * width * pack + heads * 6 * rows * rows * 256,
        specs={
            2: near,
            3: near,
            4: pl.BlockSpec((width, hv), lambda i, p: (0, p[0])),
            **{5 + i: anywhere for i in range(4)},
        },
        out_specs={6 + i: anywhere for i in range(4)},
        scratch=[pltpu.SemaphoreType.DMA((4,))],
    )

    ctx_all = gather_feat(ctx)

    def by_half(array):
        return pl.BlockSpec(
            (half,) + array.shape[1:], lambda i, p: (jnp.where(i == 0, 1 - (p[0] & 1), p[0] & 1), 0)
        )

    feed_in = [*ctx_all, tokens, cotangent, gain_b, w_out, w_gate, w_up, w_down]
    feed_shapes = [
        hbm_of(rows, width, F32),
        shape_of(rows, width, BF16),
        shape_of(rows, hidden, BF16),
        shape_of(rows, hidden, BF16),
        shape_of(rows, hidden, BF16),
        shape_of(half, width, BF16),
        shape_of(half, width, BF16),
    ]
    residual, normed_two, inner, grad_gate, grad_up, back_away, back_own = call(
        feed_kernel,
        "feed",
        where,
        feed_in,
        feed_shapes,
        2 * rows * width * (width + 5 * hidden),
        grid=2,
        specs={i: by_half(feed_in[i]) for i in range(share + 2)},
        out_specs={i: by_half(feed_shapes[i]) for i in range(5)},
        share=share,
    )

    hidden_flops = rows * width * hidden
    block = (hidden, chunk)
    of_down = ("down", [inner, cotangent])
    of_gate = ("gate", [grad_gate, normed_two])
    of_up = ("up", [grad_up, normed_two])
    arrived = swap(back_away, "feat", 1)
    sent_down, come_down = first_hop(columns_away_kernel, *of_down, block, hidden_flops, x_first)
    sent_gate, sent_up = call(
        pair_away_kernel,
        "pair_away",
        where,
        [grad_gate, grad_up, normed_two],
        [shape_of(groups // 2, *block, BF16)] * 2,
        2 * hidden_flops,
        orders=(tuple(x_first), tuple(z_first)),
        chunk=chunk,
    )
    [arrived] = after([arrived], sent_down, sent_up)
    back_own = (back_own.astype(F32) + arrived.astype(F32)).astype(BF16)
    come_gate, come_up = swap(sent_gate, "dp", x_first[0]), swap(sent_up, "dp", z_first[0])
    [inner_in] = after([inner], sent_up)
    feed_away, feed_own = call(
        down_kernel,
        "down",
        where,
        [inner_in, w_down],
        [shape_of(half, width, BF16)] * 2,
        2 * hidden_flops,
    )
    feed_come = swap(feed_away, "feat", 1)
    feed_own = (feed_own.astype(F32) + feed_come.astype(F32)).astype(BF16)
    [back_go] = after([back_own], sent_up)
    come_back = swap(back_go, "feat", feat_masks[0])
    [come_back] = after([come_back], feed_own)
    back_own = (back_own.astype(F32) + come_back.astype(F32)).astype(BF16)
    for mask in feat_masks[1:-1]:
        back_own = (back_own.astype(F32) + swap(back_own, "feat", mask).astype(F32)).astype(BF16)
    back_other = swap(back_own, "feat", 1)
    [feed_own] = after([feed_own], back_own)

    grad_res, grad_mixed, grads, gain_part = call(
        back_kernel,
        "back",
        where,
        [back_own, back_other, residual, cotangent, gain_b, w_out, q, k, v, ctx, den],
        [
            shape_of(rows, width, F32),
            shape_of(rows, width, BF16),
            shape_of(rows, pack, BF16),
            shape_of(1, width, F32),
        ],
        2 * rows * width * hv + heads * 10 * rows * rows * 256,
        specs={5: pl.BlockSpec((hv, width), lambda i, p: (p[0], 0))},
        scratch=[pltpu.VMEM((rows, hv), BF16)],
    )

    of_own = ("own", [normed, grads])
    of_out = ("out", [ctx, grad_mixed, gain_part])
    own_flops, out_flops = rows * width * pack, rows * width * hv
    sent_own, come_own = first_hop(rows_away_kernel, *of_own, (chunk, pack), own_flops, x_first)
    [come_up] = after([come_up], sent_own)
    keep_up, away_up = last_hops(columns_keep_kernel, *of_up, come_up, block, hidden_flops, z_first)
    [ctx_in] = after([ctx], away_up)
    sent_out, come_out = first_hop(
        out_away_kernel, "out", [ctx_in, grad_mixed, gain_part], (hv + 16, chunk), out_flops, x_first
    )
    [come_down] = after([come_down], sent_out)
    keep_down, away_down = last_hops(columns_keep_kernel, *of_down, come_down, block, hidden_flops, x_first)
    [come_gate] = after([come_gate], away_down)
    keep_gate, away_gate = last_hops(columns_keep_kernel, *of_gate, come_gate, block, hidden_flops, x_first)
    [come_own] = after([come_own], away_gate)
    kept_own, *direct_own = call(
        rows_direct_kernel,
        "own_keep",
        where,
        [*of_own[1], come_own],
        [shape_of(chunk, pack, F32)] + [shape_of(chunk, pack, BF16)] * (groups // 2 - 1),
        own_flops,
        order=tuple(x_first),
        chunk=chunk,
    )
    sum_own = kept_own
    for offset, piece in zip(positions(x_first)[1:], direct_own):
        sum_own = sum_own + swap(piece, "dp", offset).astype(F32)
    sum_own = sum_own.astype(BF16)
    [come_out] = after([come_out], *direct_own)
    keep_out, away_out = last_hops(out_keep_kernel, *of_out, come_out, (hv + 16, chunk), out_flops, x_first)
    sum_down = finish(keep_down, away_down, x_first[1:])
    sum_gate = finish(keep_gate, away_gate, x_first[1:])
    sum_up = finish(keep_up, away_up, z_first[1:])
    sum_out = finish(keep_out, away_out, x_first[1:])

    for mask in feat_masks[:-1]:
        feed_own = (feed_own.astype(F32) + swap(feed_own, "feat", mask).astype(F32)).astype(BF16)
    core_start = (feat & 1) * half
    out_own = (lax.dynamic_slice_in_dim(residual, core_start, half, 0) + feed_own.astype(F32)).astype(BF16)
    out_other = swap(out_own, "feat", 1)
    output = jnp.concatenate(absolute_order([out_own, out_other], feat & 1), axis=0)

    grads_all = gather_feat(grads)
    in_args = [*grads_all, grad_res, tokens, gain_a, w_query, w_key, w_value]

    def by_rows(array):
        return pl.BlockSpec((half,) + array.shape[1:], lambda i, p: (i, 0))

    [grad_input] = call(
        input_kernel,
        "grad_input",
        where,
        in_args,
        [shape_of(rows, width, BF16)],
        2 * rows * width * pack * share,
        grid=2,
        specs={i: by_rows(in_args[i]) for i in range(share + 2)},
        out_specs={0: pl.BlockSpec((half, width), lambda i, p: (i, 0))},
        share=share,
        hv=hv,
        hq=hq,
    )

    def own_rows(array):
        return pl.BlockSpec((chunk, array.shape[1]), lambda i, p: (p[1], 0))

    sum_query, sum_key, sum_value, sum_gain_one = call(
        finish_kernel,
        "finish",
        where,
        [*gather_feat(sum_own), gain_a, w_query, w_key, w_value],
        [
            shape_of(chunk, hq * share, F32),
            shape_of(chunk, hq * share, F32),
            shape_of(chunk, hv * share, F32),
            shape_of(1, chunk, F32),
        ],
        chunk * pack * share,
        specs={
            share + 1: own_rows(w_query),
            share + 2: own_rows(w_key),
            share + 3: own_rows(w_value),
        },
        share=share,
        hv=hv,
        hq=hq,
    )

    return (
        output,
        grad_input,
        sum_gain_one[0],
        sum_query,
        sum_key,
        sum_value,
        sum_out[:hv],
        sum_out[hv],
        sum_gate.T,
        sum_up.T,
        sum_down,
    )


def solution(mesh):
    in_specs = (
        P("dp", None),
        P(),
        P(),
        P(),
        P(),
        P(),
        P(),
        P(None, "feat"),
        P(None, "feat"),
        P("feat", None),
        P("dp", None),
        P("dp", None),
    )
    out_specs = (
        P("dp", None),
        P("dp", None),
        P("dp"),
        P("dp", None),
        P("dp", None),
        P("dp", None),
        P("feat", "dp"),
        P("dp"),
        P("dp", "feat"),
        P("dp", "feat"),
        P("feat", "dp"),
    )
    return jax.shard_map(local, mesh=mesh, in_specs=in_specs, out_specs=out_specs, check_vma=False)
```

```python
import functools

import jax
import jax.numpy as jnp
from jax import lax
from jax.experimental import pallas as pl
from jax.experimental.pallas import tpu as pltpu
from jax.sharding import PartitionSpec as P

HEADS = 16
QK = 16
VD = 64
EPSILON = 1e-05
F32 = jnp.float32
BF16 = jnp.bfloat16
COSTS = {"feed": 3000000000, "late": 10000000000}
VMEM_LIMIT = 20 * 1024 * 1024


def dot(a, b):
    return lax.dot_general(a, b, (((1,), (0,)), ((), ())), preferred_element_type=F32)


def dot_nt(a, b):
    return lax.dot_general(a, b, (((1,), (1,)), ((), ())), preferred_element_type=F32)


def dot_tn(a, b):
    return lax.dot_general(a, b, (((0,), (0,)), ((), ())), preferred_element_type=F32)


def lane_mask(shape, width, head):
    return lax.broadcasted_iota(jnp.int32, shape, 1) // width == head


def only_head(array, width, head):
    return jnp.where(lane_mask(array.shape, width, head), array, jnp.zeros_like(array))


def absolute_order(blocks, place):
    blocks = list(blocks)
    mask = 1
    while mask < len(blocks):
        flip = (place & mask) != 0
        blocks = [jnp.where(flip, blocks[j ^ mask], blocks[j]) for j in range(len(blocks))]
        mask *= 2
    return blocks


def bounds_of(where):
    bounds, total = [], 0
    for slot in range(2, where.shape[0]):
        total = total + where[slot]
        bounds.append(total)
    return bounds


def starts_of(bounds, index):
    start = jnp.zeros_like(index)
    for bound in bounds:
        start = jnp.maximum(start, jnp.where(index >= bound, bound, 0))
    return start


def pick_columns(wide, index, width):
    each = wide.shape[1] // width
    picked = wide[:, :width]
    for i in range(1, each):
        picked = jnp.where(index % each == i, wide[:, i * width : (i + 1) * width], picked)
    return picked


def block_columns(ref, index, width):
    if width % 128 == 0:
        return ref[:, pl.ds(pl.multiple_of(index * width, 128), width)]
    each = 128 // width
    return pick_columns(ref[:, pl.ds(pl.multiple_of(index // each * 128, 128), 128)], index, width)


def positions(order):
    found = [0]
    for mask in order:
        found = [r for r in found] + [r ^ mask for r in found]
    count = len(found)
    result = []
    for p in range(count):
        r, top = 0, count // 2
        for mask in order:
            if p & top:
                r ^= mask
            top //= 2
        result.append(r)
    return result


def chunk_columns(ref, group, offsets, chunk):
    return jnp.concatenate([block_columns(ref, group ^ r, chunk) for r in offsets], axis=1)


def attend_kernel(
    where, tok, gain, w_query, w_key, w_value, *refs
):
    n_out, q_out, k_out, v_out, ctx_out, den_out = refs
    rows = tok.shape[0]
    hq, hv = q_out.shape[1], v_out.shape[1]
    block = rows // 2
    feat = where[0]
    x = tok[...].astype(F32)
    r = lax.rsqrt(jnp.mean(x * x, axis=1, keepdims=True) + EPSILON)
    n = (x * r * gain[...]).astype(BF16)
    n_out[...] = n
    small = dot(n, jnp.concatenate([w_query[...], w_key[...]], axis=1))
    v = dot(n, w_value[...]).astype(BF16)
    wide = w_query.shape[1]
    q = (pick_columns(small[:, :wide], feat, hq) * QK**-0.5).astype(BF16)
    k = pick_columns(small[:, wide:], feat, hq).astype(BF16)
    v_out[...] = v
    q_out[...] = q
    k_out[...] = k
    bounds = bounds_of(where)
    for part in range(2):
        low, high = part * block, (part + 1) * block
        row = lax.broadcasted_iota(jnp.int32, (block, high), 0) + low
        col = lax.broadcasted_iota(jnp.int32, (block, high), 1)
        start = starts_of(bounds, lax.broadcasted_iota(jnp.int32, (block, 1), 0) + low)
        allowed = (col <= row) & (col >= start)
        number = jnp.zeros((block, hv), F32)
        total = jnp.zeros((block, hv), F32)
        for head in range(hq // QK):
            t = dot_nt(only_head(q[low:high], QK, head), k[:high]) + 1.0
            p = jnp.where(allowed, t * t + 1.0, 0.0).astype(BF16)
            number = number + dot(p, only_head(v[:high], VD, head))
            ones = jnp.where(lane_mask((high, hv), VD, head), 1.0, 0.0).astype(BF16)
            total = total + dot(p, ones)
        ctx_out[low:high, :] = (number / total).astype(BF16)
        den_out[low:high, :] = total


def fetch_kernel(where, ctx, cot, *refs):
    *refs, ginner_out, sems = refs
    count = len(refs) // 2
    copies = [pltpu.make_async_copy(refs[i], refs[count + i], sems.at[i]) for i in range(count)]
    for copy in copies:
        copy.start()
    copies[0].wait()
    live = lax.broadcasted_iota(jnp.int32, (cot.shape[0], 1), 0) < bounds_of(where)[-1]
    gfeed = jnp.where(live, cot[...], jnp.zeros_like(cot))
    ginner_out[...] = dot_nt(gfeed, refs[count][...])
    for copy in copies[1:]:
        copy.wait()


def feed_kernel(place, *refs, share):
    ctx = refs[:share]
    tok, ginner_in, gain, w_out, w_gate, w_up = refs[share : 6 + share]
    res_out, n_out, inner_out, gg_out, gu_out, away_out, own_out = refs[6 + share :]
    half = tok.shape[0] // 2
    core = place[0] & 1
    contexts = absolute_order([c[...] for c in ctx], place[0])
    context = jnp.concatenate(contexts, axis=1)
    rows = slice(None)
    index = lax.broadcasted_iota(jnp.int32, (2 * half, 1), 0)
    live = (index < bounds_of(place)[-1]).astype(F32)
    residual = tok[...].astype(F32) + live * dot(context, w_out[...])
    res_out[...] = residual
    r = lax.rsqrt(jnp.mean(residual * residual, axis=1, keepdims=True) + EPSILON)
    n = (residual * r * gain[...]).astype(BF16)
    n_out[...] = n
    gate = dot_nt(n, w_gate[...])
    up = dot_nt(n, w_up[...])
    ginner = ginner_in[...]
    sig = jax.nn.sigmoid(gate)
    act = gate * sig
    inner_out[...] = (act * up * live).astype(BF16)
    ggate = (ginner * up * sig * (1.0 + gate * (1.0 - sig))).astype(BF16)
    gup = (ginner * act).astype(BF16)
    gg_out[...] = ggate
    gu_out[...] = gup
    for which, out in ((1 - core, away_out), (core, own_out)):
        here = pl.ds(pl.multiple_of(which * half, half), half)
        out[...] = (dot(gg_out[here, :], w_gate[...]) + dot(gu_out[here, :], w_up[...])).astype(BF16)


def down_kernel(place, inner, w_down, away_out, own_out):
    half = own_out.shape[0]
    core = place[0] & 1
    for which, out in ((1 - core, away_out), (core, own_out)):
        out[...] = dot(inner[pl.ds(pl.multiple_of(which * half, half), half), :], w_down[...]).astype(BF16)


def products(where, pairs, offsets, chunk):
    found = []
    for left, right in pairs:
        part = chunk_columns(right, where[1], offsets, chunk)
        found.append(jnp.broadcast_to(part, (16, part.shape[1])) if left is None else dot_tn(left, part))
    return found


def away_kernel(where, *refs, pairs, order, chunk):
    out = refs[-1]
    offsets = positions(order)
    count = len(offsets) // 2
    low = 0
    for part in products(where, pairs(refs), offsets[count:], chunk):
        high = low + part.shape[0]
        for i in range(count):
            out[i, low:high, :] = part[:, i * chunk : (i + 1) * chunk].astype(BF16)
        low = high


def keep_kernel(where, *refs, pairs, order, chunk):
    arrived, keep_out, away_out = refs[-3:]
    offsets = positions(order)
    count = len(offsets) // 2
    low = 0
    for part in products(where, pairs(refs), offsets[:count], chunk):
        high = low + part.shape[0]
        for i in range(count):
            total = part[:, i * chunk : (i + 1) * chunk] + arrived[i, low:high, :].astype(F32)
            if i < count // 2:
                keep_out[i, low:high, :] = total.astype(keep_out.dtype)
            else:
                away_out[i - count // 2, low:high, :] = total.astype(BF16)
        low = high


def direct_kernel(where, *refs, pairs, order, chunk, inputs):
    arrived, outs = refs[inputs], refs[inputs + 1 :]
    offsets = positions(order)
    count = len(offsets) // 2
    low = 0
    for part in products(where, pairs(refs), offsets[:count], chunk):
        high = low + part.shape[0]
        for i in range(count):
            total = part[:, i * chunk : (i + 1) * chunk] + arrived[i, low:high, :].astype(F32)
            outs[i][low:high, :] = total.astype(outs[i].dtype)
        low = high


def hop_kernel(where, held, come, keep_out, away_out):
    count = keep_out.shape[0]
    for i in range(count):
        keep_out[i] = (held[i].astype(F32) + come[i].astype(F32)).astype(keep_out.dtype)
        away_out[i] = (held[count + i].astype(F32) + come[count + i].astype(F32)).astype(BF16)


def hidden_kernel(where, x_held, x_come, z_held, z_come, down_out, gate_out, up_out):
    hidden = down_out.shape[0]
    split = x_held.shape[1] - hidden
    x = x_held[0].astype(F32) + x_come[0].astype(F32)
    z = z_held[0].astype(F32) + z_come[0].astype(F32)
    down_out[...] = x[:hidden]
    gate_out[:split, :] = x[hidden:]
    gate_out[split:, :] = z[: hidden - split]
    up_out[...] = z[hidden - split :]


def late_kernel(where, held, *refs):
    comes, (out, gain_out, own_out) = refs[:-3], refs[-3:]
    total = held[...].reshape(held.shape[-2:]).astype(F32)
    for come in comes:
        total = total + come[...].reshape(come.shape[-2:]).astype(F32)
    many = out.shape[0]
    out[...] = total[:many]
    gain_out[...] = total[many : many + 1]
    own_out[...] = total[many + 16 :].astype(BF16)


def back_kernel(
    place, own, other, res, cot, gain, w_own, q_in, k_in, v_in, ctx_in, den_in,
    gr_out, gm_out, g_out, gain_out, gctx,
):
    rows = res.shape[0]
    hq, hv = q_in.shape[1], v_in.shape[1]
    half = rows // 2
    core = place[0] & 1
    bounds = bounds_of(place)
    gain_sum = jnp.zeros((1, gain_out.shape[1]), F32)
    for which, source in ((core, own), (1 - core, other)):
        here = pl.ds(pl.multiple_of(which * half, half), half)
        live = (lax.broadcasted_iota(jnp.int32, (half, 1), 0) + which * half < bounds[-1]).astype(F32)
        e = source[...].astype(F32)
        residual = res[here, :]
        r = lax.rsqrt(jnp.mean(residual * residual, axis=1, keepdims=True) + EPSILON)
        weighted = e * gain[...]
        gain_sum = gain_sum + jnp.sum(e * residual * r, axis=0, keepdims=True)
        scale = r * r * r * jnp.mean(weighted * residual, axis=1, keepdims=True)
        grad = cot[here, :].astype(F32) + r * weighted - residual * scale
        gr_out[here, :] = grad
        gm = (live * grad).astype(BF16)
        gm_out[here, :] = gm
        gctx[here, :] = dot_nt(gm, w_own[...]).astype(BF16)
    gain_out[...] = gain_sum
    number = gctx[...].astype(F32) / den_in[...]
    gn = number.astype(BF16)
    product = number * ctx_in[...].astype(F32)
    leading = product.astype(BF16)
    remainder = (product - leading.astype(F32)).astype(BF16)
    select = (
        lax.broadcasted_iota(jnp.int32, (16, hv), 1) // VD == lax.broadcasted_iota(jnp.int32, (16, hv), 0)
    )
    select = jnp.where(select, 1.0, 0.0).astype(BF16)
    shift = dot_nt(select, leading) + dot_nt(select, remainder)
    q, k, v = q_in[...], k_in[...], v_in[...]
    gq = [jnp.zeros((half, hq), F32) for _ in range(2)]
    for part in range(2):
        low, high = part * half, (part + 1) * half
        row = lax.broadcasted_iota(jnp.int32, (half, rows - low), 0) + low
        col = lax.broadcasted_iota(jnp.int32, (half, rows - low), 1) + low
        start = starts_of(bounds, lax.broadcasted_iota(jnp.int32, (1, rows - low), 1) + low)
        allowed = (row <= col) & (row >= start)
        gk = jnp.zeros((half, hq), F32)
        gv = jnp.zeros((half, hv), F32)
        for head in range(hq // QK):
            q_head = only_head(q[low:], QK, head)
            g_head = only_head(gn[low:], VD, head)
            t = dot_nt(k[low:high], q_head) + 1.0
            p = jnp.where(allowed, t * t + 1.0, 0.0).astype(BF16)
            g = dot_nt(v[low:high], g_head) - shift[head : head + 1, low:]
            ds = jnp.where(allowed, g * t, 0.0).astype(BF16)
            gv = gv + dot(p, g_head)
            gk = gk + dot(ds, q_head)
            k_head = only_head(k[low:high], QK, head)
            for second in range(part, 2):
                piece = ds[:, second * half - low : (second + 1) * half - low]
                gq[second] = gq[second] + dot_tn(piece, k_head)
        g_out[low:high, :hv] = gv.astype(BF16)
        g_out[low:high, hv + hq :] = (gk * 2.0).astype(BF16)
    for part in range(2):
        g_out[part * half : (part + 1) * half, hv : hv + hq] = (gq[part] * (2.0 * QK**-0.5)).astype(BF16)


def input_kernel(place, *refs, share, hv, hq):
    grads = refs[:share]
    gr, tok, res, own, other, gain, w_query, w_key, w_value, out, output = refs[share:]
    blocks = absolute_order([g[...] for g in grads], place[0])
    values = jnp.concatenate([b[:, :hv] for b in blocks], axis=1)
    queries = jnp.concatenate([b[:, hv : hv + hq] for b in blocks], axis=1)
    keys = jnp.concatenate([b[:, hv + hq :] for b in blocks], axis=1)
    e = dot_nt(queries, w_query[...]) + dot_nt(keys, w_key[...]) + dot_nt(values, w_value[...])
    x = tok[...].astype(F32)
    r = lax.rsqrt(jnp.mean(x * x, axis=1, keepdims=True) + EPSILON)
    weighted = e * gain[...]
    scale = r * r * r * jnp.mean(weighted * x, axis=1, keepdims=True)
    out[...] = (gr[...] + r * weighted - x * scale).astype(BF16)
    step, half = pl.program_id(0), tok.shape[0]
    index = lax.broadcasted_iota(jnp.int32, (half, 1), 0) + step * half
    live = (index < bounds_of(place)[-1]).astype(F32)
    feed = jnp.where(step == (place[0] & 1), own[...], other[...]).astype(F32)
    output[...] = (res[...] + live * feed).astype(BF16)


def finish_kernel(where, *refs, share, hv, hq):
    sums = refs[:share]
    gain, w_query, w_key, w_value, q_out, k_out, v_out, gain_out = refs[share:]
    blocks = [b.T for b in absolute_order([s[...].astype(F32) for s in sums], where[0])]
    values = jnp.concatenate([b[:, :hv] for b in blocks], axis=1)
    queries = jnp.concatenate([b[:, hv : hv + hq] for b in blocks], axis=1)
    keys = jnp.concatenate([b[:, hv + hq :] for b in blocks], axis=1)
    q_out[...] = queries
    k_out[...] = keys
    v_out[...] = values
    total = jnp.sum(values * w_value[...].astype(F32), axis=1, keepdims=True)
    total = total + jnp.sum(queries * w_query[...].astype(F32) + keys * w_key[...].astype(F32), axis=1, keepdims=True)
    spread = jnp.broadcast_to(total, (total.shape[0], total.shape[0]))
    diagonal = lax.broadcasted_iota(jnp.int32, spread.shape, 0) == lax.broadcasted_iota(jnp.int32, spread.shape, 1)
    row = jnp.sum(jnp.where(diagonal, spread, 0.0), axis=0, keepdims=True)
    gain_out[...] = row / block_columns(gain, where[1], gain_out.shape[1])


def whole(array):
    return pl.BlockSpec(array.shape, lambda *_: (0,) * len(array.shape))


def shape_of(*args):
    return jax.ShapeDtypeStruct(args[:-1], args[-1])


def vmem_of(*args):
    return pltpu.VMEM(args[:-1], args[-1])


def params():
    return pltpu.CompilerParams(vmem_limit_bytes=VMEM_LIMIT)


def call(kernel, name, scalars, arrays, shapes, grid=1, specs=None, out_specs=None, scratch=(), **fixed):
    specs, out_specs = specs or {}, out_specs or {}
    return pl.pallas_call(
        functools.partial(kernel, **fixed) if fixed else kernel,
        grid_spec=pltpu.PrefetchScalarGridSpec(
            num_scalar_prefetch=1,
            grid=(grid,),
            in_specs=[specs.get(i, whole(a)) for i, a in enumerate(arrays)],
            out_specs=[out_specs.get(i, whole(s)) for i, s in enumerate(shapes)],
            scratch_shapes=list(scratch),
        ),
        out_shape=list(shapes),
        compiler_params=params(),
        cost_estimate=pl.CostEstimate(flops=COSTS.get(name, 1000), bytes_accessed=1000, transcendentals=0),
        name=name,
    )(scalars, *arrays)


def after(arrays, *earlier):
    held = lax.optimization_barrier((*arrays, *earlier))
    return held[: len(arrays)]


def in_hbm(array):
    return pltpu.with_memory_space_constraint(array, pltpu.HBM)


def local(
    tokens, gain_one, w_query, w_key, w_value, w_out, gain_two, w_gate, w_up, w_down, lengths, cotangent
):
    rows, width = tokens.shape
    share, groups = lax.axis_size("feat"), lax.axis_size("dp")
    feat, group = lax.axis_index("feat"), lax.axis_index("dp")
    hq, hv = w_query.shape[1] // share, w_value.shape[1] // share
    hidden = w_gate.shape[1]
    chunk = width // groups
    half = rows // 2
    pack = hv + 2 * hq
    where = jnp.concatenate([jnp.stack([feat, group]).astype(jnp.int32), lengths[0]])
    w_gate, w_up = w_gate.T, w_up.T
    gain_a, gain_b = gain_one[None, :], gain_two[None, :]

    def swap(array, axis, mask):
        count = share if axis == "feat" else groups
        return lax.ppermute(array, axis, [(i, i ^ mask) for i in range(count)])

    def masks_of(count):
        found, mask = [], 1
        while mask < count:
            found.append(mask)
            mask *= 2
        return found

    feat_masks = masks_of(share)[::-1]
    dp_masks = masks_of(groups)
    x_first = tuple(dp_masks)
    z_first = tuple(dp_masks[1:] + dp_masks[:1])

    def gather_feat(own, *earlier):
        held = {0: own}
        for mask in feat_masks:
            for j in list(held):
                [held[j ^ mask]] = after([swap(held[j], "feat", mask)], *earlier)
        return [held[j] for j in range(share)]

    def plus(array, come):
        return (array.astype(F32) + come.astype(F32)).astype(BF16)

    wide = max(hq, 128)
    near = pl.BlockSpec((width, wide), lambda i, p: (0, p[0] * hq // wide))
    anywhere = pl.BlockSpec(memory_space=pl.ANY)
    later = [w_down, w_out, w_gate, w_up]
    normed, q, k, v, ctx, den = call(
        attend_kernel,
        "attend",
        where,
        [in_hbm(a) for a in (tokens, gain_a, w_query, w_key, w_value)],
        [
            vmem_of(rows, width, BF16),
            vmem_of(rows, hq, BF16),
            vmem_of(rows, hq, BF16),
            vmem_of(rows, hv, BF16),
            vmem_of(rows, hv, BF16),
            vmem_of(rows, hv, F32),
        ],
        specs={2: near, 3: near, 4: pl.BlockSpec((width, hv), lambda i, p: (0, p[0]))},
    )
    whole_vmem = pl.BlockSpec(memory_space=pltpu.VMEM)
    w_down, w_out, w_gate, w_up, ginner = call(
        fetch_kernel,
        "fetch",
        where,
        [ctx, in_hbm(cotangent), *map(in_hbm, later)],
        [*(pltpu.VMEM(a.shape, a.dtype) for a in later), vmem_of(rows, hidden, F32)],
        specs={i: anywhere for i in (0, 2, 3, 4, 5)},
        out_specs={0: whole_vmem, **{i: anywhere for i in range(1, 4)}},
        scratch=[pltpu.SemaphoreType.DMA((4,))],
    )
    ctx_all = gather_feat(ctx, w_down)

    feed_in = [*ctx_all, tokens, ginner, gain_b, w_out, w_gate, w_up]
    feed_shapes = [
        vmem_of(rows, width, F32),
        vmem_of(rows, width, BF16),
        vmem_of(rows, hidden, BF16),
        vmem_of(rows, hidden, BF16),
        vmem_of(rows, hidden, BF16),
        shape_of(half, width, BF16),
        shape_of(half, width, BF16),
    ]
    residual, normed_two, inner, grad_gate, grad_up, back_away, back_own = call(
        feed_kernel,
        "feed",
        where,
        feed_in,
        feed_shapes,
        share=share,
    )

    z_order = z_first
    split = max(hidden // 256, 1) * 128 + (128 if hidden % 256 >= 128 else 0)
    few = groups // 4
    x_args = [inner, grad_gate, cotangent, normed_two]
    z_args = [grad_gate, grad_up, normed_two]
    x_pairs = lambda refs: [(refs[0][...], refs[2]), (refs[1][:, :split], refs[3])]
    z_pairs = lambda refs: [(refs[0][:, split:], refs[2]), (refs[1][...], refs[2])]
    x_fixed = dict(pairs=x_pairs, order=x_first, chunk=chunk)
    z_fixed = dict(pairs=z_pairs, order=z_order, chunk=chunk)
    x_many, z_many, late_many = hidden + split, 2 * hidden - split, hv + 16 + pack

    def hops(name, held, sent, masks, earlier):
        [come] = after([swap(sent, "dp", masks[0])], earlier)
        for mask in masks[1:]:
            count = held.shape[0] // 2
            shapes = [shape_of(count, *held.shape[1:], BF16)] * 2
            held, sent = call(hop_kernel, name, where, [held, come], shapes)
            come = swap(sent, "dp", mask)
        return held, come, sent

    last = back_own
    feed_away, feed_own = call(
        down_kernel, "down", where, [*after([inner], last), w_down], [shape_of(half, width, BF16)] * 2
    )
    last = feed_own
    [x_sent] = call(
        away_kernel,
        "x_away",
        where,
        [*after(x_args[:1], last), *x_args[1:]],
        [shape_of(2 * few, x_many, chunk, BF16)],
        **x_fixed,
    )
    last = x_sent
    [z_sent] = call(
        away_kernel,
        "z_away",
        where,
        [*after(z_args[:1], last), *z_args[1:]],
        [shape_of(2 * few, z_many, chunk, BF16)],
        **z_fixed,
    )
    last = z_sent
    [come] = after([swap(back_away, "feat", 1)], last)
    last = back_own = plus(back_own, come)
    [come] = after([swap(feed_away, "feat", 1)], last)
    last = feed_own = plus(feed_own, come)
    for mask in feat_masks[:-1]:
        [come] = after([swap(back_own, "feat", mask)], last)
        last = back_own = plus(back_own, come)
    [back_other] = after([swap(back_own, "feat", 1)], last)
    grad_res, grad_mixed, grads, gain_part = call(
        back_kernel,
        "back",
        where,
        [back_own, back_other, residual, cotangent, gain_b, w_out, q, k, v, ctx, den],
        [
            vmem_of(rows, width, F32),
            vmem_of(rows, width, BF16),
            vmem_of(rows, pack, BF16),
            shape_of(1, width, F32),
        ],
        specs={5: pl.BlockSpec((hv, width), lambda i, p: (p[0], 0))},
        scratch=[pltpu.VMEM((rows, hv), BF16)],
    )
    last = gain_part
    late_args = [ctx, grads, normed, grad_mixed, gain_part]
    late_pairs = lambda refs: [(refs[0][...], refs[3]), (None, refs[4]), (refs[1][...], refs[2])]
    late_fixed = dict(pairs=late_pairs, order=x_first, chunk=chunk)
    held = {0: grads}
    for mask in feat_masks[:-1]:
        for j in list(held):
            held[j ^ mask] = swap(held[j], "feat", mask)
    far = [j for j in held if j]
    [late_sent] = call(
        away_kernel,
        "late_away",
        where,
        [*after(late_args[:1], last), *late_args[1:]],
        [shape_of(2 * few, late_many, chunk, BF16)],
        **late_fixed,
    )
    late_come = swap(late_sent, "dp", x_first[0])
    last = late_sent
    [come] = after([swap(z_sent, "dp", z_order[0])], last)
    shapes = [shape_of(few, z_many, chunk, BF16)] * 2
    z_held, z_sent = call(keep_kernel, "z_keep", where, [*z_args, come], shapes, **z_fixed)
    last = z_sent
    [come] = after([swap(x_sent, "dp", x_first[0])], last)
    shapes = [shape_of(few, x_many, chunk, BF16)] * 2
    x_held, x_sent = call(keep_kernel, "x_keep", where, [*x_args, come], shapes, **x_fixed)
    last = x_sent
    for mask in feat_masks[:-1]:
        [come] = after([swap(feed_own, "feat", mask)], last)
        last = feed_own = plus(feed_own, come)
    held.update(zip(far, after([held[j] for j in far], last)))
    last = held[far[-1]]
    [come] = after([late_come], last)
    late, *direct = call(
        direct_kernel,
        "late_keep",
        where,
        [*late_args, come],
        [shape_of(late_many, chunk, F32)] + [shape_of(late_many, chunk, BF16)] * (2 * few - 1),
        inputs=len(late_args),
        **late_fixed,
    )
    comes = [swap(piece, "dp", offset) for offset, piece in zip(positions(x_first)[1:], direct)]
    last = direct[-1]
    z_held, z_come, last = hops("z_hop", z_held, z_sent, z_order[1:], last)
    for j in list(held):
        [held[j ^ 1]] = after([swap(held[j], "feat", 1)], last)
    last = held[1]
    x_held, x_come, last = hops("x_hop", x_held, x_sent, x_first[1:], last)
    sum_out, sum_gain_two, sum_own = call(
        late_kernel,
        "late",
        where,
        [late, *after(comes, last)],
        [shape_of(hv, chunk, F32), shape_of(1, chunk, F32), shape_of(pack, chunk, BF16)],
    )
    last = sum_own
    sums = {0: sum_own}
    for mask in feat_masks[:-1]:
        for j in list(sums):
            sums[j ^ mask] = swap(sums[j], "feat", mask)
    sums_far = [j for j in sums if j]
    [feed_other] = after([swap(feed_own, "feat", 1)], last)
    last = feed_other
    def by_rows(array):
        return pl.BlockSpec((half,) + array.shape[1:], lambda i, p: (i, 0))

    in_args = [*[held[j] for j in range(share)], *after([grad_res], last), tokens, residual, feed_own, feed_other, gain_a, w_query, w_key, w_value]
    grad_input, output = call(
        input_kernel,
        "grad_input",
        where,
        in_args,
        [shape_of(rows, width, BF16)] * 2,
        grid=2,
        specs={i: by_rows(in_args[i]) for i in range(share + 3)},
        out_specs={i: pl.BlockSpec((half, width), lambda i, p: (i, 0)) for i in range(2)},
        share=share,
        hv=hv,
        hq=hq,
    )
    last = grad_input
    for j in list(sums):
        sums[j ^ 1] = swap(sums[j], "feat", 1)

    def own_rows(array):
        return pl.BlockSpec((chunk, array.shape[1]), lambda i, p: (p[1], 0))

    sum_query, sum_key, sum_value, sum_gain_one = call(
        finish_kernel,
        "finish",
        where,
        [*after([sums[j] for j in range(share)], last), gain_a, w_query, w_key, w_value],
        [
            shape_of(chunk, hq * share, F32),
            shape_of(chunk, hq * share, F32),
            shape_of(chunk, hv * share, F32),
            shape_of(1, chunk, F32),
        ],
        specs={
            share + 1: own_rows(w_query),
            share + 2: own_rows(w_key),
            share + 3: own_rows(w_value),
        },
        share=share,
        hv=hv,
        hq=hq,
    )
    last = sum_query
    x_come, z_come = after([x_come, z_come], last)
    sum_down, sum_gate, sum_up = call(
        hidden_kernel, "hidden", where, [x_held, x_come, z_held, z_come], [shape_of(hidden, chunk, F32)] * 3
    )
    last = sum_down

    return (
        output,
        grad_input,
        sum_gain_one[0],
        sum_query,
        sum_key,
        sum_value,
        sum_out,
        sum_gain_two[0],
        sum_gate.T,
        sum_up.T,
        sum_down,
    )


def solution(mesh):
    in_specs = (
        P("dp", None),
        P(),
        P(),
        P(),
        P(),
        P(),
        P(),
        P(None, "feat"),
        P(None, "feat"),
        P("feat", None),
        P("dp", None),
        P("dp", None),
    )
    out_specs = (
        P("dp", None),
        P("dp", None),
        P("dp"),
        P("dp", None),
        P("dp", None),
        P("dp", None),
        P("feat", "dp"),
        P("dp"),
        P("dp", "feat"),
        P("dp", "feat"),
        P("feat", "dp"),
    )
    return jax.shard_map(local, mesh=mesh, in_specs=in_specs, out_specs=out_specs, check_vma=False)
```

```python
import functools

import jax
import jax.numpy as jnp
from jax import lax
from jax.experimental import pallas as pl
from jax.experimental.pallas import tpu as pltpu
from jax.sharding import PartitionSpec as P

HEADS = 16
QK = 16
VD = 64
EPSILON = 1e-05
F32 = jnp.float32
BF16 = jnp.bfloat16
COSTS = {"feed": 3000000000, "grad_input": 1000, "hidden": 10000000000, "late": 3000000000}
VMEM_LIMIT = 20 * 1024 * 1024


def dot(a, b):
    return lax.dot_general(a, b, (((1,), (0,)), ((), ())), preferred_element_type=F32)


def dot_nt(a, b):
    return lax.dot_general(a, b, (((1,), (1,)), ((), ())), preferred_element_type=F32)


def dot_tn(a, b):
    return lax.dot_general(a, b, (((0,), (0,)), ((), ())), preferred_element_type=F32)


def lane_mask(shape, width, head):
    return lax.broadcasted_iota(jnp.int32, shape, 1) // width == head


def only_head(array, width, head):
    return jnp.where(lane_mask(array.shape, width, head), array, jnp.zeros_like(array))


def absolute_order(blocks, place):
    blocks = list(blocks)
    mask = 1
    while mask < len(blocks):
        flip = (place & mask) != 0
        blocks = [jnp.where(flip, blocks[j ^ mask], blocks[j]) for j in range(len(blocks))]
        mask *= 2
    return blocks


def bounds_of(where):
    bounds, total = [], 0
    for slot in range(2, len(where) if isinstance(where, tuple) else where.shape[0]):
        total = total + where[slot]
        bounds.append(total)
    return bounds


def starts_of(bounds, index):
    start = jnp.zeros_like(index)
    for bound in bounds:
        start = jnp.maximum(start, jnp.where(index >= bound, bound, 0))
    return start


def pick_columns(wide, index, width):
    each = wide.shape[1] // width
    picked = wide[:, :width]
    for i in range(1, each):
        picked = jnp.where(index % each == i, wide[:, i * width : (i + 1) * width], picked)
    return picked


def block_columns(ref, index, width):
    if width % 128 == 0:
        return ref[:, pl.ds(pl.multiple_of(index * width, 128), width)]
    each = 128 // width
    return pick_columns(ref[:, pl.ds(pl.multiple_of(index // each * 128, 128), 128)], index, width)


def positions(order):
    found = [0]
    for mask in order:
        found = [r for r in found] + [r ^ mask for r in found]
    count = len(found)
    result = []
    for p in range(count):
        r, top = 0, count // 2
        for mask in order:
            if p & top:
                r ^= mask
            top //= 2
        result.append(r)
    return result


def chunk_columns(ref, group, offsets, chunk):
    return jnp.concatenate([block_columns(ref, group ^ r, chunk) for r in offsets], axis=1)


def attend_kernel(lengths, tok, gain, w_query, w_key, w_value, *refs):
    n_out, q_out, k_out, v_out, ctx_out, den_out = refs
    rows = tok.shape[0]
    hq, hv = q_out.shape[1], v_out.shape[1]
    block = rows // 2
    feat = lax.axis_index("feat")
    where = (0, 0, *[lengths[0, i] for i in range(lengths.shape[1])])
    x = tok[...].astype(F32)
    r = lax.rsqrt(jnp.mean(x * x, axis=1, keepdims=True) + EPSILON)
    n = (x * r * gain[...]).astype(BF16)
    n_out[...] = n
    small = dot(n, jnp.concatenate([w_query[...], w_key[...]], axis=1))
    v = dot(n, w_value[...]).astype(BF16)
    wide = w_query.shape[1]
    q = (pick_columns(small[:, :wide], feat, hq) * QK**-0.5).astype(BF16)
    k = pick_columns(small[:, wide:], feat, hq).astype(BF16)
    v_out[...] = v
    q_out[...] = q
    k_out[...] = k
    bounds = bounds_of(where)
    start = starts_of(bounds, lax.broadcasted_iota(jnp.int32, (rows, 1), 0))
    number = [jnp.zeros((block, hv), F32) for _ in range(2)]
    total = [jnp.zeros((block, hv), F32) for _ in range(2)]
    for part in range(2):
        low, high = part * block, (part + 1) * block
        row = lax.broadcasted_iota(jnp.int32, (rows - low, block), 0) + low
        col = lax.broadcasted_iota(jnp.int32, (rows - low, block), 1) + low
        allowed = (col <= row) & (col >= start[low:])
        for head in range(hq // QK):
            t = dot_nt(only_head(q[low:], QK, head), k[low:high]) + 1.0
            exact = jnp.where(allowed, t * t + 1.0, 0.0)
            p = exact.astype(BF16)
            part_number = dot(p, only_head(v[low:high], VD, head))
            part_total = jnp.where(lane_mask((rows - low, hv), VD, head), jnp.sum(exact, axis=1, keepdims=True), 0.0)
            for i in range(part, 2):
                here = slice(i * block - low, (i + 1) * block - low)
                number[i] = number[i] + part_number[here]
                total[i] = total[i] + part_total[here]
    for i in range(2):
        ctx_out[i * block : (i + 1) * block, :] = (number[i] / total[i]).astype(BF16)
        den_out[i * block : (i + 1) * block, :] = total[i]


def fetch_kernel(where, ctx, cot, *refs):
    *refs, ginner_out, sems = refs
    count = len(refs) // 2
    copies = [pltpu.make_async_copy(refs[i], refs[count + i], sems.at[i]) for i in range(count)]
    for copy in copies:
        copy.start()
    copies[0].wait()
    live = lax.broadcasted_iota(jnp.int32, (cot.shape[0], 1), 0) < bounds_of(where)[-1]
    gfeed = jnp.where(live, cot[...], jnp.zeros_like(cot))
    ginner_out[...] = dot_nt(gfeed, refs[count][...])
    for copy in copies[1:]:
        copy.wait()


def feed_kernel(place, *refs, share):
    ctx = refs[:share]
    tok, ginner_in, gain, w_out, w_gate, w_up = refs[share : 6 + share]
    res_out, n_out, inner_out, gg_out, gu_out, away_out, own_out = refs[6 + share :]
    half = tok.shape[0] // 2
    core = place[0] & 1
    contexts = absolute_order([c[...] for c in ctx], place[0])
    context = jnp.concatenate(contexts, axis=1)
    rows = slice(None)
    index = lax.broadcasted_iota(jnp.int32, (2 * half, 1), 0)
    live = (index < bounds_of(place)[-1]).astype(F32)
    residual = tok[...].astype(F32) + live * dot(context, w_out[...])
    res_out[...] = residual
    r = lax.rsqrt(jnp.mean(residual * residual, axis=1, keepdims=True) + EPSILON)
    n = (residual * r * gain[...]).astype(BF16)
    n_out[...] = n
    gate = dot_nt(n, w_gate[...])
    up = dot_nt(n, w_up[...])
    ginner = ginner_in[...]
    sig = jax.nn.sigmoid(gate)
    act = gate * sig
    inner_out[...] = (act * up * live).astype(BF16)
    ggate = (ginner * up * sig * (1.0 + gate * (1.0 - sig))).astype(BF16)
    gup = (ginner * act).astype(BF16)
    gg_out[...] = ggate
    gu_out[...] = gup
    for which, out in ((1 - core, away_out), (core, own_out)):
        here = pl.ds(pl.multiple_of(which * half, half), half)
        out[...] = (dot(gg_out[here, :], w_gate[...]) + dot(gu_out[here, :], w_up[...])).astype(BF16)


def down_kernel(place, inner, w_down, away_out, own_out):
    half = own_out.shape[0]
    core = place[0] & 1
    for which, out in ((1 - core, away_out), (core, own_out)):
        out[...] = dot(inner[pl.ds(pl.multiple_of(which * half, half), half), :], w_down[...]).astype(BF16)


def products(where, pairs, offsets, chunk):
    found = []
    for left, right in pairs:
        part = chunk_columns(right, where[1], offsets, chunk)
        found.append(jnp.broadcast_to(part, (16, part.shape[1])) if left is None else dot_tn(left, part))
    return found


def away_kernel(where, *refs, pairs, order, chunk):
    out = refs[-1]
    offsets = positions(order)
    count = len(offsets) // 2
    low = 0
    for part in products(where, pairs(refs), offsets[count:], chunk):
        high = low + part.shape[0]
        for i in range(count):
            out[i, low:high, :] = part[:, i * chunk : (i + 1) * chunk].astype(BF16)
        low = high


def aways_kernel(where, inner, gate, up, cot, normed, w_down, x_out, z_out, feed_away, feed_own, *, x_fixed, z_fixed):
    away_kernel(where, inner, gate, cot, normed, x_out, **x_fixed)
    away_kernel(where, gate, up, normed, z_out, **z_fixed)
    down_kernel(where, inner, w_down, feed_away, feed_own)


def keep_kernel(where, *refs, pairs, order, chunk):
    arrived, keep_out, away_out = refs[-3:]
    offsets = positions(order)
    count = len(offsets) // 2
    low = 0
    for part in products(where, pairs(refs), offsets[:count], chunk):
        high = low + part.shape[0]
        for i in range(count):
            total = part[:, i * chunk : (i + 1) * chunk] + arrived[i, low:high, :].astype(F32)
            if i < count // 2:
                keep_out[i, low:high, :] = total.astype(keep_out.dtype)
            else:
                away_out[i - count // 2, low:high, :] = total.astype(BF16)
        low = high


def direct_kernel(where, *refs, pairs, order, chunk, inputs):
    arrived, outs = refs[inputs], refs[inputs + 1 :]
    offsets = positions(order)
    count = len(offsets) // 2
    low = 0
    for part in products(where, pairs(refs), offsets[:count], chunk):
        high = low + part.shape[0]
        for i in range(count):
            total = part[:, i * chunk : (i + 1) * chunk] + arrived[i, low:high, :].astype(F32)
            outs[i][low:high, :] = total.astype(outs[i].dtype)
        low = high


def hop_kernel(where, held, come, keep_out, away_out):
    count = keep_out.shape[0]
    for i in range(count):
        keep_out[i] = (held[i].astype(F32) + come[i].astype(F32)).astype(keep_out.dtype)
        away_out[i] = (held[count + i].astype(F32) + come[count + i].astype(F32)).astype(BF16)


def hidden_kernel(where, x_held, x_come, z_held, z_come, down_out, gate_out, up_out):
    hidden = down_out.shape[0]
    split = x_held.shape[1] - hidden
    x = x_held[0].astype(F32) + x_come[0].astype(F32)
    z = z_held[0].astype(F32) + z_come[0].astype(F32)
    down_out[...] = x[:hidden]
    gate_out[:split, :] = x[hidden:]
    gate_out[split:, :] = z[: hidden - split]
    up_out[...] = z[hidden - split :]


def late_kernel(where, held, *refs):
    comes, (out, gain_out, own_out) = refs[:-3], refs[-3:]
    total = held[...].reshape(held.shape[-2:]).astype(F32)
    for come in comes:
        total = total + come[...].reshape(come.shape[-2:]).astype(F32)
    many = out.shape[0]
    out[...] = total[:many]
    gain_out[...] = total[many : many + 1]
    own_out[...] = total[many + 16 :].astype(BF16)


def prepare_kernel(where, q_in, k_in, res, p_out, t_out, r_out):
    rows, hq = q_in.shape
    half = rows // 2
    bounds = bounds_of(where)
    residual = res[...]
    r_out[...] = lax.rsqrt(jnp.mean(residual * residual, axis=1, keepdims=True) + EPSILON)
    q, k = q_in[...], k_in[...]
    for part in range(2):
        low, high = part * half, (part + 1) * half
        row = lax.broadcasted_iota(jnp.int32, (high, half), 0)
        col = lax.broadcasted_iota(jnp.int32, (high, half), 1) + low
        start = starts_of(bounds, lax.broadcasted_iota(jnp.int32, (1, half), 1) + low)
        allowed = (row <= col) & (row >= start)
        for head in range(hq // QK):
            t = dot_nt(k[:high], only_head(q[low:high], QK, head)) + 1.0
            here = slice(part * half, part * half + high)
            p_out[head, here, :] = jnp.where(allowed, t * t + 1.0, 0.0).astype(BF16)
            t_out[head, here, :] = jnp.where(allowed, t, 0.0).astype(BF16)


def back_kernel(
    place, own, other, res, r_in, cot, gain, w_own, q_in, k_in, v_in, ctx_in, den_in, p_in, t_in,
    gr_out, gm_out, g_out, gain_out, gctx,
):
    rows = res.shape[0]
    hq, hv = q_in.shape[1], v_in.shape[1]
    half = rows // 2
    core = place[0] & 1
    bounds = bounds_of(place)
    gain_sum = jnp.zeros((1, gain_out.shape[1]), F32)
    for which, source in ((core, own), (1 - core, other)):
        here = pl.ds(pl.multiple_of(which * half, half), half)
        live = (lax.broadcasted_iota(jnp.int32, (half, 1), 0) + which * half < bounds[-1]).astype(F32)
        e = source[...].astype(F32)
        residual, r = res[here, :], r_in[here, :]
        weighted = e * gain[...]
        gain_sum = gain_sum + jnp.sum(e * residual * r, axis=0, keepdims=True)
        scale = r * r * r * jnp.mean(weighted * residual, axis=1, keepdims=True)
        grad = cot[here, :].astype(F32) + r * weighted - residual * scale
        gr_out[here, :] = grad
        gm = (live * grad).astype(BF16)
        gm_out[here, :] = gm
        gctx[here, :] = dot_nt(gm, w_own[...]).astype(BF16)
    gain_out[...] = gain_sum
    number = gctx[...].astype(F32) / den_in[...]
    gn = number.astype(BF16)
    product = number * ctx_in[...].astype(F32)
    leading = product.astype(BF16)
    remainder = (product - leading.astype(F32)).astype(BF16)
    select = (
        lax.broadcasted_iota(jnp.int32, (16, hv), 1) // VD == lax.broadcasted_iota(jnp.int32, (16, hv), 0)
    )
    select = jnp.where(select, 1.0, 0.0).astype(BF16)
    shift = dot_nt(select, leading) + dot_nt(select, remainder)
    q, k, v = q_in[...], k_in[...], v_in[...]
    gk = [jnp.zeros((half, hq), F32) for _ in range(2)]
    gv = [jnp.zeros((half, hv), F32) for _ in range(2)]
    for part in range(2):
        low, high = part * half, (part + 1) * half
        gq = jnp.zeros((half, hq), F32)
        for head in range(hq // QK):
            q_head = only_head(q[low:high], QK, head)
            g_head = only_head(gn[low:high], VD, head)
            p = p_in[head, part * half : part * half + high, :]
            t = t_in[head, part * half : part * half + high, :]
            g = dot_nt(v[:high], g_head) - shift[head : head + 1, low:high]
            ds = (g * t.astype(F32)).astype(BF16)
            part_gv, part_gk = dot(p, g_head), dot(ds, q_head)
            for j in range(part + 1):
                gv[j] = gv[j] + part_gv[j * half : (j + 1) * half]
                gk[j] = gk[j] + part_gk[j * half : (j + 1) * half]
            gq = gq + dot_tn(ds, only_head(k[:high], QK, head))
        g_out[low:high, hv : hv + hq] = (gq * (2.0 * QK**-0.5)).astype(BF16)
    for j in range(2):
        g_out[j * half : (j + 1) * half, :hv] = gv[j].astype(BF16)
        g_out[j * half : (j + 1) * half, hv + hq :] = (gk[j] * 2.0).astype(BF16)


def input_kernel(place, *refs, share, hv, hq):
    grads = refs[:share]
    gr, tok, res, own, other, gain, w_query, w_key, w_value, out, output = refs[share:]
    blocks = absolute_order([g[...] for g in grads], place[0])
    values = jnp.concatenate([b[:, :hv] for b in blocks], axis=1)
    queries = jnp.concatenate([b[:, hv : hv + hq] for b in blocks], axis=1)
    keys = jnp.concatenate([b[:, hv + hq :] for b in blocks], axis=1)
    e = dot_nt(queries, w_query[...]) + dot_nt(keys, w_key[...]) + dot_nt(values, w_value[...])
    x = tok[...].astype(F32)
    r = lax.rsqrt(jnp.mean(x * x, axis=1, keepdims=True) + EPSILON)
    weighted = e * gain[...]
    scale = r * r * r * jnp.mean(weighted * x, axis=1, keepdims=True)
    out[...] = (gr[...] + r * weighted - x * scale).astype(BF16)
    step, half = pl.program_id(0), tok.shape[0]
    index = lax.broadcasted_iota(jnp.int32, (half, 1), 0) + step * half
    live = (index < bounds_of(place)[-1]).astype(F32)
    feed = jnp.where(step == (place[0] & 1), own[...], other[...]).astype(F32)
    output[...] = (res[...] + live * feed).astype(BF16)


def finish_kernel(where, *refs, share, hv, hq):
    sums = refs[:share]
    gain, w_query, w_key, w_value, q_out, k_out, v_out, gain_out = refs[share:]
    blocks = [b.T for b in absolute_order([s[...].astype(F32) for s in sums], where[0])]
    values = jnp.concatenate([b[:, :hv] for b in blocks], axis=1)
    queries = jnp.concatenate([b[:, hv : hv + hq] for b in blocks], axis=1)
    keys = jnp.concatenate([b[:, hv + hq :] for b in blocks], axis=1)
    q_out[...] = queries
    k_out[...] = keys
    v_out[...] = values
    total = jnp.sum(values * w_value[...].astype(F32), axis=1, keepdims=True)
    total = total + jnp.sum(queries * w_query[...].astype(F32) + keys * w_key[...].astype(F32), axis=1, keepdims=True)
    spread = jnp.broadcast_to(total, (total.shape[0], total.shape[0]))
    diagonal = lax.broadcasted_iota(jnp.int32, spread.shape, 0) == lax.broadcasted_iota(jnp.int32, spread.shape, 1)
    row = jnp.sum(jnp.where(diagonal, spread, 0.0), axis=0, keepdims=True)
    gain_out[...] = row / block_columns(gain, where[1], gain_out.shape[1])


def whole(array):
    return pl.BlockSpec(array.shape, lambda *_: (0,) * len(array.shape))


def shape_of(*args):
    return jax.ShapeDtypeStruct(args[:-1], args[-1])


def vmem_of(*args):
    return pltpu.VMEM(args[:-1], args[-1])


def params():
    return pltpu.CompilerParams(vmem_limit_bytes=VMEM_LIMIT)


def call(kernel, name, scalars, arrays, shapes, grid=1, specs=None, out_specs=None, scratch=(), **fixed):
    specs, out_specs = specs or {}, out_specs or {}
    return pl.pallas_call(
        functools.partial(kernel, **fixed) if fixed else kernel,
        grid_spec=pltpu.PrefetchScalarGridSpec(
            num_scalar_prefetch=1,
            grid=(grid,),
            in_specs=[specs.get(i, whole(a)) for i, a in enumerate(arrays)],
            out_specs=[out_specs.get(i, whole(s)) for i, s in enumerate(shapes)],
            scratch_shapes=list(scratch),
        ),
        out_shape=list(shapes),
        compiler_params=params(),
        cost_estimate=pl.CostEstimate(flops=COSTS.get(name, 1000), bytes_accessed=1000, transcendentals=0),
        name=name,
    )(scalars, *arrays)


def after(arrays, *earlier):
    held = lax.optimization_barrier((*arrays, *earlier))
    return held[: len(arrays)]


def in_hbm(array):
    return pltpu.with_memory_space_constraint(array, pltpu.HBM)


def local(
    tokens, gain_one, w_query, w_key, w_value, w_out, gain_two, w_gate, w_up, w_down, lengths, cotangent
):
    rows, width = tokens.shape
    share, groups = lax.axis_size("feat"), lax.axis_size("dp")
    feat, group = lax.axis_index("feat"), lax.axis_index("dp")
    hq, hv = w_query.shape[1] // share, w_value.shape[1] // share
    hidden = w_gate.shape[1]
    chunk = width // groups
    half = rows // 2
    pack = hv + 2 * hq
    where = jnp.concatenate([jnp.stack([feat, group]).astype(jnp.int32), lengths[0]])
    w_gate, w_up = w_gate.T, w_up.T
    gain_a, gain_b = gain_one[None, :], gain_two[None, :]

    def swap(array, axis, mask):
        count = share if axis == "feat" else groups
        return lax.ppermute(array, axis, [(i, i ^ mask) for i in range(count)])

    def masks_of(count):
        found, mask = [], 1
        while mask < count:
            found.append(mask)
            mask *= 2
        return found

    feat_masks = masks_of(share)[::-1]
    dp_masks = masks_of(groups)
    x_first = tuple(dp_masks)
    z_first = tuple(dp_masks[1:] + dp_masks[:1])

    def gather_feat(own, *earlier):
        held = {0: own}
        for mask in feat_masks:
            for j in list(held):
                [held[j ^ mask]] = after([swap(held[j], "feat", mask)], *earlier)
        return [held[j] for j in range(share)]

    def plus(array, come):
        return (array.astype(F32) + come.astype(F32)).astype(BF16)

    wide = max(hq, 128)
    anywhere = pl.BlockSpec(memory_space=pl.ANY)
    later = [w_down, w_out, w_gate, w_up]
    near = pl.BlockSpec((width, wide), lambda i: (0, lax.axis_index("feat") * hq // wide))
    attend_args = [in_hbm(a) for a in (lengths, tokens, gain_a, w_query, w_key, w_value)]
    attend_shapes = [
        vmem_of(rows, width, BF16),
        vmem_of(rows, hq, BF16),
        vmem_of(rows, hq, BF16),
        vmem_of(rows, hv, BF16),
        vmem_of(rows, hv, BF16),
        vmem_of(rows, hv, F32),
    ]
    normed, q, k, v, ctx, den = pl.pallas_call(
        attend_kernel,
        grid=(1,),
        in_specs=[
            pl.BlockSpec(memory_space=pltpu.SMEM),
            whole(tokens),
            whole(gain_a),
            near,
            near,
            pl.BlockSpec((width, hv), lambda i: (0, lax.axis_index("feat"))),
        ],
        out_specs=[whole(a) for a in attend_shapes],
        out_shape=attend_shapes,
        compiler_params=params(),
        cost_estimate=pl.CostEstimate(flops=1000, bytes_accessed=1000, transcendentals=0),
        name="attend",
    )(*attend_args)
    whole_vmem = pl.BlockSpec(memory_space=pltpu.VMEM)
    w_down, w_out, w_gate, w_up, ginner = call(
        fetch_kernel,
        "fetch",
        where,
        [ctx, in_hbm(cotangent), *map(in_hbm, later)],
        [*(pltpu.VMEM(a.shape, a.dtype) for a in later), vmem_of(rows, hidden, F32)],
        specs={i: anywhere for i in (0, 2, 3, 4, 5)},
        out_specs={0: whole_vmem, **{i: anywhere for i in range(1, 4)}},
        scratch=[pltpu.SemaphoreType.DMA((4,))],
    )
    ctx_all = gather_feat(ctx, w_down)

    feed_in = [*ctx_all, tokens, ginner, gain_b, w_out, w_gate, w_up]
    feed_shapes = [
        vmem_of(rows, width, F32),
        vmem_of(rows, width, BF16),
        vmem_of(rows, hidden, BF16),
        vmem_of(rows, hidden, BF16),
        vmem_of(rows, hidden, BF16),
        shape_of(half, width, BF16),
        shape_of(half, width, BF16),
    ]
    residual, normed_two, inner, grad_gate, grad_up, back_away, back_own = call(
        feed_kernel,
        "feed",
        where,
        feed_in,
        feed_shapes,
        share=share,
    )

    z_order = z_first
    split = max(hidden // 256, 1) * 128 + (128 if hidden % 256 >= 128 else 0)
    few = groups // 4
    x_args = [inner, grad_gate, cotangent, normed_two]
    z_args = [grad_gate, grad_up, normed_two]
    x_pairs = lambda refs: [(refs[0][...], refs[2]), (refs[1][:, :split], refs[3])]
    z_pairs = lambda refs: [(refs[0][:, split:], refs[2]), (refs[1][...], refs[2])]
    x_fixed = dict(pairs=x_pairs, order=x_first, chunk=chunk)
    z_fixed = dict(pairs=z_pairs, order=z_order, chunk=chunk)
    x_many, z_many, late_many = hidden + split, 2 * hidden - split, hv + 16 + pack

    def hops(name, held, sent, masks, earlier):
        [come] = after([swap(sent, "dp", masks[0])], earlier)
        for mask in masks[1:]:
            count = held.shape[0] // 2
            shapes = [shape_of(count, *held.shape[1:], BF16)] * 2
            held, sent = call(hop_kernel, name, where, [held, come], shapes)
            come = swap(sent, "dp", mask)
        return held, come, sent

    last = back_own
    x_sent, z_sent, feed_away, feed_own = call(
        aways_kernel,
        "aways",
        where,
        [inner, grad_gate, grad_up, cotangent, normed_two, w_down],
        [
            shape_of(2 * few, x_many, chunk, BF16),
            shape_of(2 * few, z_many, chunk, BF16),
            shape_of(half, width, BF16),
            shape_of(half, width, BF16),
        ],
        x_fixed=x_fixed,
        z_fixed=z_fixed,
    )
    last = z_sent
    [come] = after([swap(back_away, "feat", 1)], last)
    last = back_own = plus(back_own, come)
    scores, slopes, r_two = call(
        prepare_kernel,
        "prepare",
        where,
        [*after([q], last), k, residual],
        [
            vmem_of(hq // QK, 3 * half, half, BF16),
            vmem_of(hq // QK, 3 * half, half, BF16),
            vmem_of(rows, 1, F32),
        ],
    )
    last = scores
    for mask in feat_masks[:-1]:
        [come] = after([swap(back_own, "feat", mask)], last)
        last = back_own = plus(back_own, come)
    [come] = after([swap(feed_away, "feat", 1)], last)
    last = feed_own = plus(feed_own, come)
    [back_other] = after([swap(back_own, "feat", 1)], last)
    grad_res, grad_mixed, grads, gain_part = call(
        back_kernel,
        "back",
        where,
        [back_own, back_other, residual, r_two, cotangent, gain_b, w_out, q, k, v, ctx, den, scores, slopes],
        [
            vmem_of(rows, width, F32),
            vmem_of(rows, width, BF16),
            vmem_of(rows, pack, BF16),
            shape_of(1, width, F32),
        ],
        specs={6: pl.BlockSpec((hv, width), lambda i, p: (p[0], 0))},
        scratch=[pltpu.VMEM((rows, hv), BF16)],
    )
    last = gain_part
    late_args = [ctx, grads, normed, grad_mixed, gain_part]
    late_pairs = lambda refs: [(refs[0][...], refs[3]), (None, refs[4]), (refs[1][...], refs[2])]
    late_fixed = dict(pairs=late_pairs, order=x_first, chunk=chunk)
    held = {0: grads}
    for mask in feat_masks[:-1]:
        for j in list(held):
            held[j ^ mask] = swap(held[j], "feat", mask)
    far = [j for j in held if j]
    [late_sent] = call(
        away_kernel,
        "late_away",
        where,
        [*after(late_args[:1], last), *late_args[1:]],
        [shape_of(2 * few, late_many, chunk, BF16)],
        **late_fixed,
    )
    late_come = swap(late_sent, "dp", x_first[0])
    last = late_sent
    [come] = after([swap(z_sent, "dp", z_order[0])], last)
    shapes = [shape_of(few, z_many, chunk, BF16)] * 2
    z_held, z_sent = call(keep_kernel, "z_keep", where, [*z_args, come], shapes, **z_fixed)
    last = z_sent
    [come] = after([swap(x_sent, "dp", x_first[0])], last)
    shapes = [shape_of(few, x_many, chunk, BF16)] * 2
    x_held, x_sent = call(keep_kernel, "x_keep", where, [*x_args, come], shapes, **x_fixed)
    last = x_sent
    for mask in feat_masks[:-1]:
        [come] = after([swap(feed_own, "feat", mask)], last)
        last = feed_own = plus(feed_own, come)
    held.update(zip(far, after([held[j] for j in far], last)))
    last = held[far[-1]]
    [come] = after([late_come], last)
    late, *direct = call(
        direct_kernel,
        "late_keep",
        where,
        [*late_args, come],
        [shape_of(late_many, chunk, F32)] + [shape_of(late_many, chunk, BF16)] * (2 * few - 1),
        inputs=len(late_args),
        **late_fixed,
    )
    comes = [swap(piece, "dp", offset) for offset, piece in zip(positions(x_first)[1:], direct)]
    last = direct[-1]
    z_held, z_come, last = hops("z_hop", z_held, z_sent, z_order[1:], last)
    x_held, x_come, last = hops("x_hop", x_held, x_sent, x_first[1:], last)
    for j in list(held):
        [held[j ^ 1]] = after([swap(held[j], "feat", 1)], last)
    last = held[1]
    sum_out, sum_gain_two, sum_own = call(
        late_kernel,
        "late",
        where,
        [late, *after(comes, last)],
        [shape_of(hv, chunk, F32), shape_of(1, chunk, F32), shape_of(pack, chunk, BF16)],
    )
    last = sum_own
    sums = {0: sum_own}
    for mask in feat_masks[:-1]:
        for j in list(sums):
            sums[j ^ mask] = swap(sums[j], "feat", mask)
    sums_far = [j for j in sums if j]
    [feed_other] = after([swap(feed_own, "feat", 1)], last)
    last = feed_other
    def by_rows(array):
        return pl.BlockSpec((half,) + array.shape[1:], lambda i, p: (i, 0))

    in_args = [*[held[j] for j in range(share)], *after([grad_res], last), tokens, residual, feed_own, feed_other, gain_a, w_query, w_key, w_value]
    grad_input, output = call(
        input_kernel,
        "grad_input",
        where,
        in_args,
        [shape_of(rows, width, BF16)] * 2,
        grid=2,
        specs={i: by_rows(in_args[i]) for i in range(share + 3)},
        out_specs={i: pl.BlockSpec((half, width), lambda i, p: (i, 0)) for i in range(2)},
        share=share,
        hv=hv,
        hq=hq,
    )
    last = grad_input
    x_come, z_come = after([x_come, z_come], last)
    sum_down, sum_gate, sum_up = call(
        hidden_kernel, "hidden", where, [x_held, x_come, z_held, z_come], [shape_of(hidden, chunk, F32)] * 3
    )
    last = sum_down
    for j in list(sums):
        sums[j ^ 1] = swap(sums[j], "feat", 1)

    def own_rows(array):
        return pl.BlockSpec((chunk, array.shape[1]), lambda i, p: (p[1], 0))

    sum_query, sum_key, sum_value, sum_gain_one = call(
        finish_kernel,
        "finish",
        where,
        [*after([sums[j] for j in range(share)], last), gain_a, w_query, w_key, w_value],
        [
            shape_of(chunk, hq * share, F32),
            shape_of(chunk, hq * share, F32),
            shape_of(chunk, hv * share, F32),
            shape_of(1, chunk, F32),
        ],
        specs={
            share + 1: own_rows(w_query),
            share + 2: own_rows(w_key),
            share + 3: own_rows(w_value),
        },
        share=share,
        hv=hv,
        hq=hq,
    )
    last = sum_query

    return (
        output,
        grad_input,
        sum_gain_one[0],
        sum_query,
        sum_key,
        sum_value,
        sum_out,
        sum_gain_two[0],
        sum_gate.T,
        sum_up.T,
        sum_down,
    )


def solution(mesh):
    in_specs = (
        P("dp", None),
        P(),
        P(),
        P(),
        P(),
        P(),
        P(),
        P(None, "feat"),
        P(None, "feat"),
        P("feat", None),
        P("dp", None),
        P("dp", None),
    )
    out_specs = (
        P("dp", None),
        P("dp", None),
        P("dp"),
        P("dp", None),
        P("dp", None),
        P("dp", None),
        P("feat", "dp"),
        P("dp"),
        P("dp", "feat"),
        P("dp", "feat"),
        P("feat", "dp"),
    )
    return jax.shard_map(local, mesh=mesh, in_specs=in_specs, out_specs=out_specs, check_vma=False)
```

```python
import functools

import jax
import jax.numpy as jnp
from jax import lax
from jax.experimental import pallas as pl
from jax.experimental.pallas import tpu as pltpu
from jax.sharding import PartitionSpec as P

HEADS = 16
QK = 16
VD = 64
EPSILON = 1e-05
F32 = jnp.float32
BF16 = jnp.bfloat16
COSTS = {"feed": 3000000000, "grad_input": 1000, "hidden": 10000000000, "late": 10000000000}
VMEM_LIMIT = 20 * 1024 * 1024


def dot(a, b):
    return lax.dot_general(a, b, (((1,), (0,)), ((), ())), preferred_element_type=F32)


def dot_nt(a, b):
    return lax.dot_general(a, b, (((1,), (1,)), ((), ())), preferred_element_type=F32)


def dot_tn(a, b):
    return lax.dot_general(a, b, (((0,), (0,)), ((), ())), preferred_element_type=F32)


def lane_mask(shape, width, head):
    return lax.broadcasted_iota(jnp.int32, shape, 1) // width == head


def only_head(array, width, head):
    return jnp.where(lane_mask(array.shape, width, head), array, jnp.zeros_like(array))


def absolute_order(blocks, place):
    blocks = list(blocks)
    mask = 1
    while mask < len(blocks):
        flip = (place & mask) != 0
        blocks = [jnp.where(flip, blocks[j ^ mask], blocks[j]) for j in range(len(blocks))]
        mask *= 2
    return blocks


def bounds_of(where):
    bounds, total = [], 0
    for slot in range(2, len(where) if isinstance(where, tuple) else where.shape[0]):
        total = total + where[slot]
        bounds.append(total)
    return bounds


def starts_of(bounds, index):
    start = jnp.zeros_like(index)
    for bound in bounds:
        start = jnp.maximum(start, jnp.where(index >= bound, bound, 0))
    return start


def pick_columns(wide, index, width):
    each = wide.shape[1] // width
    picked = wide[:, :width]
    for i in range(1, each):
        picked = jnp.where(index % each == i, wide[:, i * width : (i + 1) * width], picked)
    return picked


def block_columns(ref, index, width):
    if width % 128 == 0:
        return ref[:, pl.ds(pl.multiple_of(index * width, 128), width)]
    each = 128 // width
    return pick_columns(ref[:, pl.ds(pl.multiple_of(index // each * 128, 128), 128)], index, width)


def positions(order):
    found = [0]
    for mask in order:
        found = [r for r in found] + [r ^ mask for r in found]
    count = len(found)
    result = []
    for p in range(count):
        r, top = 0, count // 2
        for mask in order:
            if p & top:
                r ^= mask
            top //= 2
        result.append(r)
    return result


def chunk_columns(ref, group, offsets, chunk):
    return jnp.concatenate([block_columns(ref, group ^ r, chunk) for r in offsets], axis=1)


def attend_kernel(lengths, tok, gain, w_query, w_key, w_value, *refs):
    n_out, q_out, k_out, v_out, ctx_out, den_out = refs
    rows = tok.shape[0]
    hq, hv = q_out.shape[1], v_out.shape[1]
    block = rows // 2
    feat = lax.axis_index("feat")
    where = (0, 0, *[lengths[0, i] for i in range(lengths.shape[1])])
    x = tok[...].astype(F32)
    r = lax.rsqrt(jnp.mean(x * x, axis=1, keepdims=True) + EPSILON)
    n = (x * r * gain[...]).astype(BF16)
    n_out[...] = n
    small = dot(n, jnp.concatenate([w_query[...], w_key[...]], axis=1))
    v = dot(n, w_value[...]).astype(BF16)
    wide = w_query.shape[1]
    q = (pick_columns(small[:, :wide], feat, hq) * QK**-0.5).astype(BF16)
    k = pick_columns(small[:, wide:], feat, hq).astype(BF16)
    v_out[...] = v
    q_out[...] = q
    k_out[...] = k
    bounds = bounds_of(where)
    start = starts_of(bounds, lax.broadcasted_iota(jnp.int32, (rows, 1), 0))
    number = [jnp.zeros((block, hv), F32) for _ in range(2)]
    total = [jnp.zeros((block, hv), F32) for _ in range(2)]
    for part in range(2):
        low, high = part * block, (part + 1) * block
        row = lax.broadcasted_iota(jnp.int32, (rows - low, block), 0) + low
        col = lax.broadcasted_iota(jnp.int32, (rows - low, block), 1) + low
        allowed = (col <= row) & (col >= start[low:])
        for head in range(hq // QK):
            t = dot_nt(only_head(q[low:], QK, head), k[low:high]) + 1.0
            exact = jnp.where(allowed, t * t + 1.0, 0.0)
            p = exact.astype(BF16)
            part_number = dot(p, only_head(v[low:high], VD, head))
            part_total = jnp.where(lane_mask((rows - low, hv), VD, head), jnp.sum(exact, axis=1, keepdims=True), 0.0)
            for i in range(part, 2):
                here = slice(i * block - low, (i + 1) * block - low)
                number[i] = number[i] + part_number[here]
                total[i] = total[i] + part_total[here]
    for i in range(2):
        ctx_out[i * block : (i + 1) * block, :] = (number[i] / total[i]).astype(BF16)
        den_out[i * block : (i + 1) * block, :] = total[i]


def fetch_kernel(where, ctx, cot, *refs):
    *refs, ginner_out, sems = refs
    count = len(refs) // 2
    copies = [pltpu.make_async_copy(refs[i], refs[count + i], sems.at[i]) for i in range(count)]
    for copy in copies:
        copy.start()
    copies[0].wait()
    live = lax.broadcasted_iota(jnp.int32, (cot.shape[0], 1), 0) < bounds_of(where)[-1]
    gfeed = jnp.where(live, cot[...], jnp.zeros_like(cot))
    ginner_out[...] = dot_nt(gfeed, refs[count][...])
    for copy in copies[1:]:
        copy.wait()


def feed_kernel(place, *refs, share):
    ctx = refs[:share]
    tok, ginner_in, gain, w_out, w_gate, w_up = refs[share : 6 + share]
    res_out, n_out, inner_out, gg_out, gu_out, away_out, own_out = refs[6 + share :]
    half = tok.shape[0] // 2
    core = place[0] & 1
    contexts = absolute_order([c[...] for c in ctx], place[0])
    context = jnp.concatenate(contexts, axis=1)
    rows = slice(None)
    index = lax.broadcasted_iota(jnp.int32, (2 * half, 1), 0)
    live = (index < bounds_of(place)[-1]).astype(F32)
    residual = tok[...].astype(F32) + live * dot(context, w_out[...])
    res_out[...] = residual
    r = lax.rsqrt(jnp.mean(residual * residual, axis=1, keepdims=True) + EPSILON)
    n = (residual * r * gain[...]).astype(BF16)
    n_out[...] = n
    hidden = w_gate.shape[0]
    for low in range(0, hidden, 256):
        part = slice(low, min(low + 256, hidden))
        gate = dot_nt(n, w_gate[part, :])
        up = dot_nt(n, w_up[part, :])
        ginner = ginner_in[:, part]
        sig = jax.nn.sigmoid(gate)
        act = gate * sig
        inner_out[:, part] = (act * up * live).astype(BF16)
        gg_out[:, part] = (ginner * up * sig * (1.0 + gate * (1.0 - sig))).astype(BF16)
        gu_out[:, part] = (ginner * act).astype(BF16)
    for which, out in ((1 - core, away_out), (core, own_out)):
        here = pl.ds(pl.multiple_of(which * half, half), half)
        out[...] = (dot(gg_out[here, :], w_gate[...]) + dot(gu_out[here, :], w_up[...])).astype(BF16)


def down_kernel(place, inner, w_down, away_out, own_out):
    half = own_out.shape[0]
    core = place[0] & 1
    for which, out in ((1 - core, away_out), (core, own_out)):
        out[...] = dot(inner[pl.ds(pl.multiple_of(which * half, half), half), :], w_down[...]).astype(BF16)


def products(where, pairs, offsets, chunk):
    found = []
    for left, right in pairs:
        part = chunk_columns(right, where[1], offsets, chunk)
        found.append(jnp.broadcast_to(part, (16, part.shape[1])) if left is None else dot_tn(left, part))
    return found


def away_kernel(where, *refs, pairs, order, chunk, away=True):
    out = refs[-1]
    offsets = positions(order)
    count = len(offsets) // 2
    low = 0
    for part in products(where, pairs(refs), offsets[count:] if away else offsets[:count], chunk):
        high = low + part.shape[0]
        for i in range(count):
            out[i, low:high, :] = part[:, i * chunk : (i + 1) * chunk].astype(BF16)
        low = high


def aways_kernel(where, inner, gate, up, cot, normed, w_down, x_out, z_out, feed_away, feed_own, *, x_fixed, z_fixed):
    away_kernel(where, inner, gate, cot, normed, x_out, **x_fixed)
    away_kernel(where, gate, up, normed, z_out, **z_fixed)
    down_kernel(where, inner, w_down, feed_away, feed_own)


def pair_keeps_kernel(where, inner, gate, up, cot, normed, x_out, z_out, *, x_fixed, z_fixed):
    away_kernel(where, inner, gate, cot, normed, x_out, **x_fixed, away=False)
    away_kernel(where, gate, up, normed, z_out, **z_fixed, away=False)


def pair_aways_kernel(where, inner, gate, up, cot, normed, x_out, z_out, *, x_fixed, z_fixed):
    away_kernel(where, inner, gate, cot, normed, x_out, **x_fixed)
    away_kernel(where, gate, up, normed, z_out, **z_fixed)


def keep_kernel(where, *refs, pairs, order, chunk):
    arrived, keep_out, away_out = refs[-3:]
    offsets = positions(order)
    count = len(offsets) // 2
    low = 0
    for part in products(where, pairs(refs), offsets[:count], chunk):
        high = low + part.shape[0]
        for i in range(count):
            total = part[:, i * chunk : (i + 1) * chunk] + arrived[i, low:high, :].astype(F32)
            if i < count // 2:
                keep_out[i, low:high, :] = total.astype(keep_out.dtype)
            else:
                away_out[i - count // 2, low:high, :] = total.astype(BF16)
        low = high


def direct_kernel(where, *refs, pairs, order, chunk, inputs):
    arrived, outs = refs[inputs], refs[inputs + 1 :]
    offsets = positions(order)
    count = len(offsets) // 2
    low = 0
    for part in products(where, pairs(refs), offsets[:count], chunk):
        high = low + part.shape[0]
        for i in range(count):
            total = part[:, i * chunk : (i + 1) * chunk] + arrived[i, low:high, :].astype(F32)
            outs[i][low:high, :] = total.astype(outs[i].dtype)
        low = high


def hop_kernel(where, held, come, keep_out, away_out):
    count = keep_out.shape[0]
    for i in range(count):
        keep_out[i] = (held[i].astype(F32) + come[i].astype(F32)).astype(keep_out.dtype)
        away_out[i] = (held[count + i].astype(F32) + come[count + i].astype(F32)).astype(BF16)


def hidden_kernel(where, x_held, x_come, z_held, z_come, down_out, gate_out, up_out):
    hidden = down_out.shape[0]
    split = x_held.shape[1] - hidden
    x = x_held[0].astype(F32) + x_come[0].astype(F32)
    z = z_held[0].astype(F32) + z_come[0].astype(F32)
    down_out[...] = x[:hidden]
    gate_out[:split, :] = x[hidden:]
    gate_out[split:, :] = z[: hidden - split]
    up_out[...] = z[hidden - split :]


def late_kernel(where, held, *refs):
    comes, (out, gain_out, own_out) = refs[:-3], refs[-3:]
    total = held[...].reshape(held.shape[-2:]).astype(F32)
    for come in comes:
        total = total + come[...].reshape(come.shape[-2:]).astype(F32)
    many = out.shape[0]
    out[...] = total[:many]
    gain_out[...] = total[many : many + 1]
    own_out[...] = total[many + 16 :].T.astype(BF16)


def prepare_kernel(where, q_in, k_in, res, p_out, t_out, r_out):
    rows, hq = q_in.shape
    half = rows // 2
    bounds = bounds_of(where)
    residual = res[...]
    r_out[...] = lax.rsqrt(jnp.mean(residual * residual, axis=1, keepdims=True) + EPSILON)
    q, k = q_in[...], k_in[...]
    for part in range(2):
        low, high = part * half, (part + 1) * half
        row = lax.broadcasted_iota(jnp.int32, (high, half), 0)
        col = lax.broadcasted_iota(jnp.int32, (high, half), 1) + low
        start = starts_of(bounds, lax.broadcasted_iota(jnp.int32, (1, half), 1) + low)
        allowed = (row <= col) & (row >= start)
        for head in range(hq // QK):
            t = dot_nt(k[:high], only_head(q[low:high], QK, head)) + 1.0
            here = slice(part * half, part * half + high)
            p_out[head, here, :] = jnp.where(allowed, t * t + 1.0, 0.0).astype(BF16)
            t_out[head, here, :] = jnp.where(allowed, t, 0.0).astype(BF16)


def back_kernel(
    place, own, other, res, r_in, cot, gain, w_own, q_in, k_in, v_in, ctx_in, den_in, p_in, t_in,
    gr_out, gm_out, g_out, gain_out, gctx,
):
    rows = res.shape[0]
    hq, hv = q_in.shape[1], v_in.shape[1]
    half = rows // 2
    core = place[0] & 1
    bounds = bounds_of(place)
    gain_sum = jnp.zeros((1, gain_out.shape[1]), F32)
    for which, source in ((core, own), (1 - core, other)):
        here = pl.ds(pl.multiple_of(which * half, half), half)
        live = (lax.broadcasted_iota(jnp.int32, (half, 1), 0) + which * half < bounds[-1]).astype(F32)
        e = source[...].astype(F32)
        residual, r = res[here, :], r_in[here, :]
        weighted = e * gain[...]
        gain_sum = gain_sum + jnp.sum(e * residual * r, axis=0, keepdims=True)
        scale = r * r * r * jnp.mean(weighted * residual, axis=1, keepdims=True)
        grad = cot[here, :].astype(F32) + r * weighted - residual * scale
        gr_out[here, :] = grad
        gm = (live * grad).astype(BF16)
        gm_out[here, :] = gm
        gctx[here, :] = dot_nt(gm, w_own[...]).astype(BF16)
    gain_out[...] = gain_sum
    number = gctx[...].astype(F32) / den_in[...]
    gn = number.astype(BF16)
    product = number * ctx_in[...].astype(F32)
    leading = product.astype(BF16)
    remainder = (product - leading.astype(F32)).astype(BF16)
    select = (
        lax.broadcasted_iota(jnp.int32, (16, hv), 1) // VD == lax.broadcasted_iota(jnp.int32, (16, hv), 0)
    )
    select = jnp.where(select, 1.0, 0.0).astype(BF16)
    shift = dot_nt(select, leading) + dot_nt(select, remainder)
    q, k, v = q_in[...], k_in[...], v_in[...]
    gk = [jnp.zeros((half, hq), F32) for _ in range(2)]
    gv = [jnp.zeros((half, hv), F32) for _ in range(2)]
    for part in range(2):
        low, high = part * half, (part + 1) * half
        gq = jnp.zeros((half, hq), F32)
        for head in range(hq // QK):
            q_head = only_head(q[low:high], QK, head)
            g_head = only_head(gn[low:high], VD, head)
            p = p_in[head, part * half : part * half + high, :]
            t = t_in[head, part * half : part * half + high, :]
            g = dot_nt(v[:high], g_head) - shift[head : head + 1, low:high]
            ds = (g * t.astype(F32)).astype(BF16)
            part_gv, part_gk = dot(p, g_head), dot(ds, q_head)
            for j in range(part + 1):
                gv[j] = gv[j] + part_gv[j * half : (j + 1) * half]
                gk[j] = gk[j] + part_gk[j * half : (j + 1) * half]
            gq = gq + dot_tn(ds, only_head(k[:high], QK, head))
        g_out[low:high, hv : hv + hq] = (gq * (2.0 * QK**-0.5)).astype(BF16)
    for j in range(2):
        g_out[j * half : (j + 1) * half, :hv] = gv[j].astype(BF16)
        g_out[j * half : (j + 1) * half, hv + hq :] = (gk[j] * 2.0).astype(BF16)


def input_kernel(place, *refs, share, hv, hq):
    grads = refs[:share]
    gr, tok, res, own, other, gain, w_query, w_key, w_value, out, output = refs[share:]
    blocks = absolute_order([g[...] for g in grads], place[0])
    values = jnp.concatenate([b[:, :hv] for b in blocks], axis=1)
    queries = jnp.concatenate([b[:, hv : hv + hq] for b in blocks], axis=1)
    keys = jnp.concatenate([b[:, hv + hq :] for b in blocks], axis=1)
    e = dot_nt(queries, w_query[...]) + dot_nt(keys, w_key[...]) + dot_nt(values, w_value[...])
    x = tok[...].astype(F32)
    r = lax.rsqrt(jnp.mean(x * x, axis=1, keepdims=True) + EPSILON)
    weighted = e * gain[...]
    scale = r * r * r * jnp.mean(weighted * x, axis=1, keepdims=True)
    out[...] = (gr[...] + r * weighted - x * scale).astype(BF16)
    step, half = pl.program_id(0), tok.shape[0]
    index = lax.broadcasted_iota(jnp.int32, (half, 1), 0) + step * half
    live = (index < bounds_of(place)[-1]).astype(F32)
    feed = jnp.where(step == (place[0] & 1), own[...], other[...]).astype(F32)
    output[...] = (res[...] + live * feed).astype(BF16)


def finish_kernel(where, *refs, share, hv, hq):
    sums = refs[:share]
    gain, w_query, w_key, w_value, q_out, k_out, v_out, gain_out = refs[share:]
    blocks = absolute_order([s[...].astype(F32) for s in sums], where[0])
    values = jnp.concatenate([b[:, :hv] for b in blocks], axis=1)
    queries = jnp.concatenate([b[:, hv : hv + hq] for b in blocks], axis=1)
    keys = jnp.concatenate([b[:, hv + hq :] for b in blocks], axis=1)
    q_out[...] = queries
    k_out[...] = keys
    v_out[...] = values
    total = jnp.sum(values * w_value[...].astype(F32), axis=1, keepdims=True)
    total = total + jnp.sum(queries * w_query[...].astype(F32) + keys * w_key[...].astype(F32), axis=1, keepdims=True)
    spread = jnp.broadcast_to(total, (total.shape[0], total.shape[0]))
    diagonal = lax.broadcasted_iota(jnp.int32, spread.shape, 0) == lax.broadcasted_iota(jnp.int32, spread.shape, 1)
    row = jnp.sum(jnp.where(diagonal, spread, 0.0), axis=0, keepdims=True)
    gain_out[...] = row / block_columns(gain, where[1], gain_out.shape[1])


def last_kernel(where, *refs, share, hv, hq):
    hidden_kernel(where, *refs[:4], *refs[8 + share : 11 + share])
    finish_kernel(where, *refs[4 : 8 + share], *refs[11 + share :], share=share, hv=hv, hq=hq)


def whole(array):
    return pl.BlockSpec(array.shape, lambda *_: (0,) * len(array.shape))


def shape_of(*args):
    return jax.ShapeDtypeStruct(args[:-1], args[-1])


def vmem_of(*args):
    return pltpu.VMEM(args[:-1], args[-1])


def params():
    return pltpu.CompilerParams(vmem_limit_bytes=VMEM_LIMIT)


def call(kernel, name, scalars, arrays, shapes, grid=1, specs=None, out_specs=None, scratch=(), **fixed):
    specs, out_specs = specs or {}, out_specs or {}
    return pl.pallas_call(
        functools.partial(kernel, **fixed) if fixed else kernel,
        grid_spec=pltpu.PrefetchScalarGridSpec(
            num_scalar_prefetch=1,
            grid=(grid,),
            in_specs=[specs.get(i, whole(a)) for i, a in enumerate(arrays)],
            out_specs=[out_specs.get(i, whole(s)) for i, s in enumerate(shapes)],
            scratch_shapes=list(scratch),
        ),
        out_shape=list(shapes),
        compiler_params=params(),
        cost_estimate=pl.CostEstimate(flops=COSTS.get(name, 1000), bytes_accessed=1000, transcendentals=0),
        name=name,
    )(scalars, *arrays)


def after(arrays, *earlier):
    held = lax.optimization_barrier((*arrays, *earlier))
    return held[: len(arrays)]


def in_hbm(array):
    return pltpu.with_memory_space_constraint(array, pltpu.HBM)


def local(
    tokens, gain_one, w_query, w_key, w_value, w_out, gain_two, w_gate, w_up, w_down, lengths, cotangent
):
    rows, width = tokens.shape
    share, groups = lax.axis_size("feat"), lax.axis_size("dp")
    feat, group = lax.axis_index("feat"), lax.axis_index("dp")
    hq, hv = w_query.shape[1] // share, w_value.shape[1] // share
    hidden = w_gate.shape[1]
    chunk = width // groups
    half = rows // 2
    pack = hv + 2 * hq
    where = jnp.concatenate([jnp.stack([feat, group]).astype(jnp.int32), lengths[0]])
    w_gate, w_up = w_gate.T, w_up.T
    gain_a, gain_b = gain_one[None, :], gain_two[None, :]

    def swap(array, axis, mask):
        count = share if axis == "feat" else groups
        return lax.ppermute(array, axis, [(i, i ^ mask) for i in range(count)])

    def masks_of(count):
        found, mask = [], 1
        while mask < count:
            found.append(mask)
            mask *= 2
        return found

    feat_masks = masks_of(share)[::-1]
    dp_masks = masks_of(groups)
    x_first = tuple(dp_masks)
    z_first = tuple(dp_masks[1:] + dp_masks[:1])

    def gather_feat(own, *earlier):
        held = {0: own}
        for mask in feat_masks:
            for j in list(held):
                [held[j ^ mask]] = after([swap(held[j], "feat", mask)], *earlier)
        return [held[j] for j in range(share)]

    def plus(array, come):
        return (array.astype(F32) + come.astype(F32)).astype(BF16)

    wide = max(hq, 128)
    anywhere = pl.BlockSpec(memory_space=pl.ANY)
    later = [w_down, w_out, w_gate, w_up]
    near = pl.BlockSpec((width, wide), lambda i: (0, lax.axis_index("feat") * hq // wide))
    attend_args = [in_hbm(a) for a in (lengths, tokens, gain_a, w_query, w_key, w_value)]
    attend_shapes = [
        vmem_of(rows, width, BF16),
        vmem_of(rows, hq, BF16),
        vmem_of(rows, hq, BF16),
        vmem_of(rows, hv, BF16),
        vmem_of(rows, hv, BF16),
        vmem_of(rows, hv, F32),
    ]
    normed, q, k, v, ctx, den = pl.pallas_call(
        attend_kernel,
        grid=(1,),
        in_specs=[
            pl.BlockSpec(memory_space=pltpu.SMEM),
            whole(tokens),
            whole(gain_a),
            near,
            near,
            pl.BlockSpec((width, hv), lambda i: (0, lax.axis_index("feat"))),
        ],
        out_specs=[whole(a) for a in attend_shapes],
        out_shape=attend_shapes,
        compiler_params=params(),
        cost_estimate=pl.CostEstimate(flops=1000, bytes_accessed=1000, transcendentals=0),
        name="attend",
    )(*attend_args)
    whole_vmem = pl.BlockSpec(memory_space=pltpu.VMEM)
    w_down, w_out, w_gate, w_up, ginner = call(
        fetch_kernel,
        "fetch",
        where,
        [ctx, in_hbm(cotangent), *map(in_hbm, later)],
        [*(pltpu.VMEM(a.shape, a.dtype) for a in later), vmem_of(rows, hidden, F32)],
        specs={i: anywhere for i in (0, 2, 3, 4, 5)},
        out_specs={0: whole_vmem, **{i: anywhere for i in range(1, 4)}},
        scratch=[pltpu.SemaphoreType.DMA((4,))],
    )
    ctx_all = gather_feat(ctx, w_down)

    feed_in = [*ctx_all, tokens, ginner, gain_b, w_out, w_gate, w_up]
    feed_shapes = [
        vmem_of(rows, width, F32),
        vmem_of(rows, width, BF16),
        vmem_of(rows, hidden, BF16),
        vmem_of(rows, hidden, BF16),
        vmem_of(rows, hidden, BF16),
        shape_of(half, width, BF16),
        shape_of(half, width, BF16),
    ]
    residual, normed_two, inner, grad_gate, grad_up, back_away, back_own = call(
        feed_kernel,
        "feed",
        where,
        feed_in,
        feed_shapes,
        share=share,
    )

    z_order = z_first
    split = max(hidden // 256, 1) * 128 + (128 if hidden % 256 >= 128 else 0)
    few = groups // 4
    x_args = [inner, grad_gate, cotangent, normed_two]
    z_args = [grad_gate, grad_up, normed_two]
    x_pairs = lambda refs: [(refs[0][...], refs[2]), (refs[1][:, :split], refs[3])]
    z_pairs = lambda refs: [(refs[0][:, split:], refs[2]), (refs[1][...], refs[2])]
    x_fixed = dict(pairs=x_pairs, order=x_first, chunk=chunk)
    z_fixed = dict(pairs=z_pairs, order=z_order, chunk=chunk)
    x_many, z_many, late_many = hidden + split, 2 * hidden - split, hv + 16 + pack

    def hops(name, held, sent, masks, earlier):
        [come] = after([swap(sent, "dp", masks[0])], earlier)
        for mask in masks[1:]:
            count = held.shape[0] // 2
            shapes = [shape_of(count, *held.shape[1:], BF16)] * 2
            held, sent = call(hop_kernel, name, where, [held, come], shapes)
            come = swap(sent, "dp", mask)
        return held, come, sent

    last = back_own
    x_sent, z_sent, feed_away, feed_own = call(
        aways_kernel,
        "aways",
        where,
        [inner, grad_gate, grad_up, cotangent, normed_two, w_down],
        [
            shape_of(2 * few, x_many, chunk, BF16),
            shape_of(2 * few, z_many, chunk, BF16),
            shape_of(half, width, BF16),
            shape_of(half, width, BF16),
        ],
        x_fixed=x_fixed,
        z_fixed=z_fixed,
    )
    last = z_sent
    [come] = after([swap(back_away, "feat", 1)], last)
    last = back_own = plus(back_own, come)
    scores, slopes, r_two = call(
        prepare_kernel,
        "prepare",
        where,
        [*after([q], last), k, residual],
        [
            vmem_of(hq // QK, 3 * half, half, BF16),
            vmem_of(hq // QK, 3 * half, half, BF16),
            vmem_of(rows, 1, F32),
        ],
    )
    last = scores
    x_held, z_held = call(
        pair_keeps_kernel,
        "keeps",
        where,
        [*after([inner], last), grad_gate, grad_up, cotangent, normed_two],
        [shape_of(2 * few, x_many, chunk, BF16), shape_of(2 * few, z_many, chunk, BF16)],
        x_fixed=x_fixed,
        z_fixed=z_fixed,
    )
    last = z_held
    for mask in feat_masks[:-1]:
        [come] = after([swap(back_own, "feat", mask)], last)
        last = back_own = plus(back_own, come)
    [come] = after([swap(feed_away, "feat", 1)], last)
    last = feed_own = plus(feed_own, come)
    [back_other] = after([swap(back_own, "feat", 1)], last)
    grad_res, grad_mixed, grads, gain_part = call(
        back_kernel,
        "back",
        where,
        [back_own, back_other, residual, r_two, cotangent, gain_b, w_out, q, k, v, ctx, den, scores, slopes],
        [
            vmem_of(rows, width, F32),
            vmem_of(rows, width, BF16),
            vmem_of(rows, pack, BF16),
            shape_of(1, width, F32),
        ],
        specs={6: pl.BlockSpec((hv, width), lambda i, p: (p[0], 0))},
        scratch=[pltpu.VMEM((rows, hv), BF16)],
    )
    last = gain_part
    late_args = [ctx, grads, normed, grad_mixed, gain_part]
    late_pairs = lambda refs: [(refs[0][...], refs[3]), (None, refs[4]), (refs[1][...], refs[2])]
    late_fixed = dict(pairs=late_pairs, order=x_first, chunk=chunk)
    held = {0: grads}
    for mask in feat_masks[:-1]:
        for j in list(held):
            held[j ^ mask] = swap(held[j], "feat", mask)
    far = [j for j in held if j]
    [late_sent] = call(
        away_kernel,
        "late_away",
        where,
        [*after(late_args[:1], last), *late_args[1:]],
        [shape_of(2 * few, late_many, chunk, BF16)],
        **late_fixed,
    )
    late_come = swap(late_sent, "dp", x_first[0])
    last = late_sent
    [come] = after([swap(z_sent, "dp", z_order[0])], last)
    shapes = [shape_of(few, z_many, chunk, BF16)] * 2
    z_held, z_sent = call(hop_kernel, "z_keep", where, [z_held, come], shapes)
    last = z_sent
    [come] = after([swap(x_sent, "dp", x_first[0])], last)
    shapes = [shape_of(few, x_many, chunk, BF16)] * 2
    x_held, x_sent = call(hop_kernel, "x_keep", where, [x_held, come], shapes)
    last = x_sent
    for mask in feat_masks[:-1]:
        [come] = after([swap(feed_own, "feat", mask)], last)
        last = feed_own = plus(feed_own, come)
    held.update(zip(far, after([held[j] for j in far], last)))
    last = held[far[-1]]
    [come] = after([late_come], last)
    late, *direct = call(
        direct_kernel,
        "late_keep",
        where,
        [*late_args, come],
        [shape_of(late_many, chunk, F32)] + [shape_of(late_many, chunk, BF16)] * (2 * few - 1),
        inputs=len(late_args),
        **late_fixed,
    )
    comes = [swap(piece, "dp", offset) for offset, piece in zip(positions(x_first)[1:], direct)]
    last = direct[-1]
    z_held, z_come, last = hops("z_hop", z_held, z_sent, z_order[1:], last)
    x_held, x_come, last = hops("x_hop", x_held, x_sent, x_first[1:], last)
    for j in list(held):
        [held[j ^ 1]] = after([swap(held[j], "feat", 1)], last)
    last = held[1]
    sum_out, sum_gain_two, sum_own = call(
        late_kernel,
        "late",
        where,
        [late, *after(comes, last)],
        [shape_of(hv, chunk, F32), shape_of(1, chunk, F32), shape_of(chunk, pack, BF16)],
    )
    last = sum_own
    sums = {0: sum_own}
    for mask in feat_masks[:-1]:
        for j in list(sums):
            sums[j ^ mask] = swap(sums[j], "feat", mask)
    sums_far = [j for j in sums if j]
    [feed_other] = after([swap(feed_own, "feat", 1)], last)
    last = feed_other
    def by_rows(array):
        return pl.BlockSpec((half,) + array.shape[1:], lambda i, p: (i, 0))

    in_args = [*[held[j] for j in range(share)], *after([grad_res], last), tokens, residual, feed_own, feed_other, gain_a, w_query, w_key, w_value]
    grad_input, output = call(
        input_kernel,
        "grad_input",
        where,
        in_args,
        [shape_of(rows, width, BF16)] * 2,
        grid=2,
        specs={i: by_rows(in_args[i]) for i in range(share + 3)},
        out_specs={i: pl.BlockSpec((half, width), lambda i, p: (i, 0)) for i in range(2)},
        share=share,
        hv=hv,
        hq=hq,
    )
    last = grad_input
    x_come, z_come = after([x_come, z_come], last)
    sum_down, sum_gate, sum_up = call(
        hidden_kernel, "hidden", where, [x_held, x_come, z_held, z_come], [shape_of(hidden, chunk, F32)] * 3
    )
    last = sum_down
    for j in list(sums):
        sums[j ^ 1] = swap(sums[j], "feat", 1)

    def own_rows(array):
        return pl.BlockSpec((chunk, array.shape[1]), lambda i, p: (p[1], 0))

    sum_query, sum_key, sum_value, sum_gain_one = call(
        finish_kernel,
        "finish",
        where,
        [*after([sums[j] for j in range(share)], last), gain_a, w_query, w_key, w_value],
        [
            shape_of(chunk, hq * share, F32),
            shape_of(chunk, hq * share, F32),
            shape_of(chunk, hv * share, F32),
            shape_of(1, chunk, F32),
        ],
        specs={
            share + 1: own_rows(w_query),
            share + 2: own_rows(w_key),
            share + 3: own_rows(w_value),
        },
        share=share,
        hv=hv,
        hq=hq,
    )
    last = sum_query

    return (
        output,
        grad_input,
        sum_gain_one[0],
        sum_query,
        sum_key,
        sum_value,
        sum_out,
        sum_gain_two[0],
        sum_gate.T,
        sum_up.T,
        sum_down,
    )


def solution(mesh):
    in_specs = (
        P("dp", None),
        P(),
        P(),
        P(),
        P(),
        P(),
        P(),
        P(None, "feat"),
        P(None, "feat"),
        P("feat", None),
        P("dp", None),
        P("dp", None),
    )
    out_specs = (
        P("dp", None),
        P("dp", None),
        P("dp"),
        P("dp", None),
        P("dp", None),
        P("dp", None),
        P("feat", "dp"),
        P("dp"),
        P("dp", "feat"),
        P("dp", "feat"),
        P("feat", "dp"),
    )
    return jax.shard_map(local, mesh=mesh, in_specs=in_specs, out_specs=out_specs, check_vma=False)
```

```python
import functools

import jax
import jax.numpy as jnp
from jax import lax
from jax.experimental import pallas as pl
from jax.experimental.pallas import tpu as pltpu
from jax.sharding import PartitionSpec as P

HEADS = 16
QK = 16
VD = 64
EPSILON = 1e-05
F32 = jnp.float32
BF16 = jnp.bfloat16
COSTS = {"feed": 3000000000, "grad_input": 1000, "hidden": 10000000000, "late": 10000000000, "late_keep": 10000000000}
VMEM_LIMIT = 20 * 1024 * 1024


def dot(a, b):
    return lax.dot_general(a, b, (((1,), (0,)), ((), ())), preferred_element_type=F32)


def dot_nt(a, b):
    return lax.dot_general(a, b, (((1,), (1,)), ((), ())), preferred_element_type=F32)


def dot_tn(a, b):
    return lax.dot_general(a, b, (((0,), (0,)), ((), ())), preferred_element_type=F32)


def lane_mask(shape, width, head):
    return lax.broadcasted_iota(jnp.int32, shape, 1) // width == head


def only_head(array, width, head):
    return jnp.where(lane_mask(array.shape, width, head), array, jnp.zeros_like(array))


def absolute_order(blocks, place):
    blocks = list(blocks)
    mask = 1
    while mask < len(blocks):
        flip = (place & mask) != 0
        blocks = [jnp.where(flip, blocks[j ^ mask], blocks[j]) for j in range(len(blocks))]
        mask *= 2
    return blocks


def bounds_of(where):
    bounds, total = [], 0
    for slot in range(2, len(where) if isinstance(where, tuple) else where.shape[0]):
        total = total + where[slot]
        bounds.append(total)
    return bounds


def starts_of(bounds, index):
    start = jnp.zeros_like(index)
    for bound in bounds:
        start = jnp.maximum(start, jnp.where(index >= bound, bound, 0))
    return start


def pick_columns(wide, index, width):
    each = wide.shape[1] // width
    picked = wide[:, :width]
    for i in range(1, each):
        picked = jnp.where(index % each == i, wide[:, i * width : (i + 1) * width], picked)
    return picked


def block_columns(ref, index, width):
    if width % 128 == 0:
        return ref[:, pl.ds(pl.multiple_of(index * width, 128), width)]
    each = 128 // width
    return pick_columns(ref[:, pl.ds(pl.multiple_of(index // each * 128, 128), 128)], index, width)


def positions(order):
    found = [0]
    for mask in order:
        found = [r for r in found] + [r ^ mask for r in found]
    count = len(found)
    result = []
    for p in range(count):
        r, top = 0, count // 2
        for mask in order:
            if p & top:
                r ^= mask
            top //= 2
        result.append(r)
    return result


def chunk_columns(ref, group, offsets, chunk):
    return jnp.concatenate([block_columns(ref, group ^ r, chunk) for r in offsets], axis=1)


def attend_kernel(lengths, tok, gain, w_query, w_key, w_value, *refs):
    n_out, q_out, k_out, v_out, ctx_out, den_out = refs
    rows = tok.shape[0]
    hq, hv = q_out.shape[1], v_out.shape[1]
    block = rows // 2
    feat = lax.axis_index("feat")
    where = (0, 0, *[lengths[0, i] for i in range(lengths.shape[1])])
    x = tok[...].astype(F32)
    r = lax.rsqrt(jnp.mean(x * x, axis=1, keepdims=True) + EPSILON)
    n = (x * r * gain[...]).astype(BF16)
    n_out[...] = n
    small = dot(n, jnp.concatenate([w_query[...], w_key[...]], axis=1))
    v = dot(n, w_value[...]).astype(BF16)
    wide = w_query.shape[1]
    q = (pick_columns(small[:, :wide], feat, hq) * QK**-0.5).astype(BF16)
    k = pick_columns(small[:, wide:], feat, hq).astype(BF16)
    v_out[...] = v
    q_out[...] = q
    k_out[...] = k
    bounds = bounds_of(where)
    start = starts_of(bounds, lax.broadcasted_iota(jnp.int32, (rows, 1), 0))
    number = [jnp.zeros((block, hv), F32) for _ in range(2)]
    total = [jnp.zeros((block, hv), F32) for _ in range(2)]
    for part in range(2):
        low, high = part * block, (part + 1) * block
        row = lax.broadcasted_iota(jnp.int32, (rows - low, block), 0) + low
        col = lax.broadcasted_iota(jnp.int32, (rows - low, block), 1) + low
        allowed = (col <= row) & (col >= start[low:])
        for head in range(hq // QK):
            t = dot_nt(only_head(q[low:], QK, head), k[low:high]) + 1.0
            exact = jnp.where(allowed, t * t + 1.0, 0.0)
            p = exact.astype(BF16)
            part_number = dot(p, only_head(v[low:high], VD, head))
            part_total = jnp.where(lane_mask((rows - low, hv), VD, head), jnp.sum(exact, axis=1, keepdims=True), 0.0)
            for i in range(part, 2):
                here = slice(i * block - low, (i + 1) * block - low)
                number[i] = number[i] + part_number[here]
                total[i] = total[i] + part_total[here]
    for i in range(2):
        ctx_out[i * block : (i + 1) * block, :] = (number[i] / total[i]).astype(BF16)
        den_out[i * block : (i + 1) * block, :] = total[i]


def fetch_kernel(where, ctx, cot, *refs):
    *refs, ginner_out, sems = refs
    count = len(refs) // 2
    copies = [pltpu.make_async_copy(refs[i], refs[count + i], sems.at[i]) for i in range(count)]
    for copy in copies:
        copy.start()
    copies[0].wait()
    live = lax.broadcasted_iota(jnp.int32, (cot.shape[0], 1), 0) < bounds_of(where)[-1]
    gfeed = jnp.where(live, cot[...], jnp.zeros_like(cot))
    ginner_out[...] = dot_nt(gfeed, refs[count][...])
    for copy in copies[1:]:
        copy.wait()


def feed_kernel(place, *refs, share):
    ctx = refs[:share]
    tok, ginner_in, gain, w_out, w_gate, w_up = refs[share : 6 + share]
    res_out, n_out, inner_out, gg_out, gu_out, away_out, own_out = refs[6 + share :]
    half = tok.shape[0] // 2
    core = place[0] & 1
    contexts = absolute_order([c[...] for c in ctx], place[0])
    context = jnp.concatenate(contexts, axis=1)
    rows = slice(None)
    index = lax.broadcasted_iota(jnp.int32, (2 * half, 1), 0)
    live = (index < bounds_of(place)[-1]).astype(F32)
    residual = tok[...].astype(F32) + live * dot(context, w_out[...])
    res_out[...] = residual
    r = lax.rsqrt(jnp.mean(residual * residual, axis=1, keepdims=True) + EPSILON)
    n = (residual * r * gain[...]).astype(BF16)
    n_out[...] = n
    hidden = w_gate.shape[0]
    for low in range(0, hidden, 256):
        part = slice(low, min(low + 256, hidden))
        gate = dot_nt(n, w_gate[part, :])
        up = dot_nt(n, w_up[part, :])
        ginner = ginner_in[:, part]
        sig = jax.nn.sigmoid(gate)
        act = gate * sig
        inner_out[:, part] = (act * up * live).astype(BF16)
        gg_out[:, part] = (ginner * up * sig * (1.0 + gate * (1.0 - sig))).astype(BF16)
        gu_out[:, part] = (ginner * act).astype(BF16)
    for which, out in ((1 - core, away_out), (core, own_out)):
        here = pl.ds(pl.multiple_of(which * half, half), half)
        out[...] = (dot(gg_out[here, :], w_gate[...]) + dot(gu_out[here, :], w_up[...])).astype(BF16)


def down_kernel(place, inner, w_down, away_out, own_out):
    half = own_out.shape[0]
    core = place[0] & 1
    for which, out in ((1 - core, away_out), (core, own_out)):
        out[...] = dot(inner[pl.ds(pl.multiple_of(which * half, half), half), :], w_down[...]).astype(BF16)


def products(where, pairs, offsets, chunk):
    found = []
    for left, right in pairs:
        part = chunk_columns(right, where[1], offsets, chunk)
        found.append(jnp.broadcast_to(part, (16, part.shape[1])) if left is None else dot_tn(left, part))
    return found


def away_kernel(where, *refs, pairs, order, chunk, away=True):
    out = refs[-1]
    offsets = positions(order)
    count = len(offsets) // 2
    low = 0
    for part in products(where, pairs(refs), offsets[count:] if away else offsets[:count], chunk):
        high = low + part.shape[0]
        for i in range(count):
            out[i, low:high, :] = part[:, i * chunk : (i + 1) * chunk].astype(BF16)
        low = high


def aways_kernel(where, inner, gate, up, cot, normed, w_down, x_out, z_out, feed_away, feed_own, *, x_fixed, z_fixed):
    away_kernel(where, inner, gate, cot, normed, x_out, **x_fixed)
    away_kernel(where, gate, up, normed, z_out, **z_fixed)
    down_kernel(where, inner, w_down, feed_away, feed_own)


def pair_keeps_kernel(where, inner, gate, up, cot, normed, x_out, z_out, *, x_fixed, z_fixed):
    away_kernel(where, inner, gate, cot, normed, x_out, **x_fixed, away=False)
    away_kernel(where, gate, up, normed, z_out, **z_fixed, away=False)


def pair_aways_kernel(where, inner, gate, up, cot, normed, x_out, z_out, *, x_fixed, z_fixed):
    away_kernel(where, inner, gate, cot, normed, x_out, **x_fixed)
    away_kernel(where, gate, up, normed, z_out, **z_fixed)


def keep_kernel(where, *refs, pairs, order, chunk):
    arrived, keep_out, away_out = refs[-3:]
    offsets = positions(order)
    count = len(offsets) // 2
    low = 0
    for part in products(where, pairs(refs), offsets[:count], chunk):
        high = low + part.shape[0]
        for i in range(count):
            total = part[:, i * chunk : (i + 1) * chunk] + arrived[i, low:high, :].astype(F32)
            if i < count // 2:
                keep_out[i, low:high, :] = total.astype(keep_out.dtype)
            else:
                away_out[i - count // 2, low:high, :] = total.astype(BF16)
        low = high


def direct_kernel(where, *refs, pairs, order, chunk, inputs):
    arrived, outs = refs[inputs], refs[inputs + 1 :]
    offsets = positions(order)
    count = len(offsets) // 2
    low = 0
    for part in products(where, pairs(refs), offsets[:count], chunk):
        high = low + part.shape[0]
        for i in range(count):
            total = part[:, i * chunk : (i + 1) * chunk] + arrived[i, low:high, :].astype(F32)
            outs[i][low:high, :] = total.astype(outs[i].dtype)
        low = high


def add_kernel(where, held, come, *outs):
    for i, out in enumerate(outs):
        out[...] = (held[i].astype(F32) + come[i].astype(F32)).astype(out.dtype)


def hop_kernel(where, held, come, keep_out, away_out):
    count = keep_out.shape[0]
    for i in range(count):
        keep_out[i] = (held[i].astype(F32) + come[i].astype(F32)).astype(keep_out.dtype)
        away_out[i] = (held[count + i].astype(F32) + come[count + i].astype(F32)).astype(BF16)


def hidden_kernel(where, x_held, x_come, z_held, z_come, down_out, gate_out, up_out):
    hidden = down_out.shape[0]
    split = x_held.shape[1] - hidden
    x = x_held[0].astype(F32) + x_come[0].astype(F32)
    z = z_held[0].astype(F32) + z_come[0].astype(F32)
    down_out[...] = x[:hidden]
    gate_out[:split, :] = x[hidden:]
    gate_out[split:, :] = z[: hidden - split]
    up_out[...] = z[hidden - split :]


def late_kernel(where, held, *refs):
    comes, (out, gain_out, own_out) = refs[:-3], refs[-3:]
    total = held[...].reshape(held.shape[-2:]).astype(F32)
    for come in comes:
        total = total + come[...].reshape(come.shape[-2:]).astype(F32)
    many = out.shape[0]
    out[...] = total[:many]
    gain_out[...] = total[many : many + 1]
    own_out[...] = total[many + 16 :].T.astype(BF16)


def prepare_kernel(where, q_in, k_in, res, p_out, t_out, r_out):
    rows, hq = q_in.shape
    half = rows // 2
    bounds = bounds_of(where)
    residual = res[...]
    r_out[...] = lax.rsqrt(jnp.mean(residual * residual, axis=1, keepdims=True) + EPSILON)
    q, k = q_in[...], k_in[...]
    for part in range(2):
        low, high = part * half, (part + 1) * half
        row = lax.broadcasted_iota(jnp.int32, (high, half), 0)
        col = lax.broadcasted_iota(jnp.int32, (high, half), 1) + low
        start = starts_of(bounds, lax.broadcasted_iota(jnp.int32, (1, half), 1) + low)
        allowed = (row <= col) & (row >= start)
        for head in range(hq // QK):
            t = dot_nt(k[:high], only_head(q[low:high], QK, head)) + 1.0
            here = slice(part * half, part * half + high)
            p_out[head, here, :] = jnp.where(allowed, t * t + 1.0, 0.0).astype(BF16)
            t_out[head, here, :] = jnp.where(allowed, t, 0.0).astype(BF16)


def back_kernel(
    place, own, other, res, r_in, cot, gain, w_own, q_in, k_in, v_in, ctx_in, den_in, p_in, t_in,
    gr_out, gm_out, g_out, gain_out, gctx,
):
    rows = res.shape[0]
    hq, hv = q_in.shape[1], v_in.shape[1]
    half = rows // 2
    core = place[0] & 1
    bounds = bounds_of(place)
    gain_sum = jnp.zeros((1, gain_out.shape[1]), F32)
    for which, source in ((core, own), (1 - core, other)):
        here = pl.ds(pl.multiple_of(which * half, half), half)
        live = (lax.broadcasted_iota(jnp.int32, (half, 1), 0) + which * half < bounds[-1]).astype(F32)
        e = source[...].astype(F32)
        residual, r = res[here, :], r_in[here, :]
        weighted = e * gain[...]
        gain_sum = gain_sum + jnp.sum(e * residual * r, axis=0, keepdims=True)
        scale = r * r * r * jnp.mean(weighted * residual, axis=1, keepdims=True)
        grad = cot[here, :].astype(F32) + r * weighted - residual * scale
        gr_out[here, :] = grad
        gm = (live * grad).astype(BF16)
        gm_out[here, :] = gm
        gctx[here, :] = dot_nt(gm, w_own[...]).astype(BF16)
    gain_out[...] = gain_sum
    number = gctx[...].astype(F32) / den_in[...]
    gn = number.astype(BF16)
    product = number * ctx_in[...].astype(F32)
    leading = product.astype(BF16)
    remainder = (product - leading.astype(F32)).astype(BF16)
    select = (
        lax.broadcasted_iota(jnp.int32, (16, hv), 1) // VD == lax.broadcasted_iota(jnp.int32, (16, hv), 0)
    )
    select = jnp.where(select, 1.0, 0.0).astype(BF16)
    shift = dot_nt(select, leading) + dot_nt(select, remainder)
    q, k, v = q_in[...], k_in[...], v_in[...]
    gk = [jnp.zeros((half, hq), F32) for _ in range(2)]
    gv = [jnp.zeros((half, hv), F32) for _ in range(2)]
    for part in range(2):
        low, high = part * half, (part + 1) * half
        gq = jnp.zeros((half, hq), F32)
        for head in range(hq // QK):
            q_head = only_head(q[low:high], QK, head)
            g_head = only_head(gn[low:high], VD, head)
            p = p_in[head, part * half : part * half + high, :]
            t = t_in[head, part * half : part * half + high, :]
            g = dot_nt(v[:high], g_head) - shift[head : head + 1, low:high]
            ds = (g * t.astype(F32)).astype(BF16)
            part_gv, part_gk = dot(p, g_head), dot(ds, q_head)
            for j in range(part + 1):
                gv[j] = gv[j] + part_gv[j * half : (j + 1) * half]
                gk[j] = gk[j] + part_gk[j * half : (j + 1) * half]
            gq = gq + dot_tn(ds, only_head(k[:high], QK, head))
        g_out[low:high, hv : hv + hq] = (gq * (2.0 * QK**-0.5)).astype(BF16)
    for j in range(2):
        g_out[j * half : (j + 1) * half, :hv] = gv[j].astype(BF16)
        g_out[j * half : (j + 1) * half, hv + hq :] = (gk[j] * 2.0).astype(BF16)


def input_kernel(place, *refs, share, hv, hq):
    grads = refs[:share]
    gr, tok, res, own, other, gain, w_query, w_key, w_value, out, output = refs[share:]
    blocks = absolute_order([g[...] for g in grads], place[0])
    values = jnp.concatenate([b[:, :hv] for b in blocks], axis=1)
    queries = jnp.concatenate([b[:, hv : hv + hq] for b in blocks], axis=1)
    keys = jnp.concatenate([b[:, hv + hq :] for b in blocks], axis=1)
    e = dot_nt(queries, w_query[...]) + dot_nt(keys, w_key[...]) + dot_nt(values, w_value[...])
    x = tok[...].astype(F32)
    r = lax.rsqrt(jnp.mean(x * x, axis=1, keepdims=True) + EPSILON)
    weighted = e * gain[...]
    scale = r * r * r * jnp.mean(weighted * x, axis=1, keepdims=True)
    out[...] = (gr[...] + r * weighted - x * scale).astype(BF16)
    step, half = pl.program_id(0), tok.shape[0]
    index = lax.broadcasted_iota(jnp.int32, (half, 1), 0) + step * half
    live = (index < bounds_of(place)[-1]).astype(F32)
    feed = jnp.where(step == (place[0] & 1), own[...], other[...]).astype(F32)
    output[...] = (res[...] + live * feed).astype(BF16)


def finish_kernel(where, *refs, share, hv, hq):
    sums = refs[:share]
    gain, w_query, w_key, w_value, q_out, k_out, v_out, gain_out = refs[share:]
    blocks = absolute_order([s[...].astype(F32) for s in sums], where[0])
    values = jnp.concatenate([b[:, :hv] for b in blocks], axis=1)
    queries = jnp.concatenate([b[:, hv : hv + hq] for b in blocks], axis=1)
    keys = jnp.concatenate([b[:, hv + hq :] for b in blocks], axis=1)
    q_out[...] = queries
    k_out[...] = keys
    v_out[...] = values
    total = jnp.sum(values * w_value[...].astype(F32), axis=1, keepdims=True)
    total = total + jnp.sum(queries * w_query[...].astype(F32) + keys * w_key[...].astype(F32), axis=1, keepdims=True)
    spread = jnp.broadcast_to(total, (total.shape[0], total.shape[0]))
    diagonal = lax.broadcasted_iota(jnp.int32, spread.shape, 0) == lax.broadcasted_iota(jnp.int32, spread.shape, 1)
    row = jnp.sum(jnp.where(diagonal, spread, 0.0), axis=0, keepdims=True)
    gain_out[...] = row / block_columns(gain, where[1], gain_out.shape[1])


def last_kernel(where, *refs, share, hv, hq):
    hidden_kernel(where, *refs[:4], *refs[8 + share : 11 + share])
    finish_kernel(where, *refs[4 : 8 + share], *refs[11 + share :], share=share, hv=hv, hq=hq)


def whole(array):
    return pl.BlockSpec(array.shape, lambda *_: (0,) * len(array.shape))


def shape_of(*args):
    return jax.ShapeDtypeStruct(args[:-1], args[-1])


def vmem_of(*args):
    return pltpu.VMEM(args[:-1], args[-1])


def params():
    return pltpu.CompilerParams(vmem_limit_bytes=VMEM_LIMIT)


def call(kernel, name, scalars, arrays, shapes, grid=1, specs=None, out_specs=None, scratch=(), **fixed):
    specs, out_specs = specs or {}, out_specs or {}
    return pl.pallas_call(
        functools.partial(kernel, **fixed) if fixed else kernel,
        grid_spec=pltpu.PrefetchScalarGridSpec(
            num_scalar_prefetch=1,
            grid=(grid,),
            in_specs=[specs.get(i, whole(a)) for i, a in enumerate(arrays)],
            out_specs=[out_specs.get(i, whole(s)) for i, s in enumerate(shapes)],
            scratch_shapes=list(scratch),
        ),
        out_shape=list(shapes),
        compiler_params=params(),
        cost_estimate=pl.CostEstimate(flops=COSTS.get(name, 1000), bytes_accessed=1000, transcendentals=0),
        name=name,
    )(scalars, *arrays)


def after(arrays, *earlier):
    held = lax.optimization_barrier((*arrays, *earlier))
    return held[: len(arrays)]


def in_hbm(array):
    return pltpu.with_memory_space_constraint(array, pltpu.HBM)


def local(
    tokens, gain_one, w_query, w_key, w_value, w_out, gain_two, w_gate, w_up, w_down, lengths, cotangent
):
    rows, width = tokens.shape
    share, groups = lax.axis_size("feat"), lax.axis_size("dp")
    feat, group = lax.axis_index("feat"), lax.axis_index("dp")
    hq, hv = w_query.shape[1] // share, w_value.shape[1] // share
    hidden = w_gate.shape[1]
    chunk = width // groups
    half = rows // 2
    pack = hv + 2 * hq
    where = jnp.concatenate([jnp.stack([feat, group]).astype(jnp.int32), lengths[0]])
    w_gate, w_up = w_gate.T, w_up.T
    gain_a, gain_b = gain_one[None, :], gain_two[None, :]

    def swap(array, axis, mask):
        count = share if axis == "feat" else groups
        return lax.ppermute(array, axis, [(i, i ^ mask) for i in range(count)])

    def masks_of(count):
        found, mask = [], 1
        while mask < count:
            found.append(mask)
            mask *= 2
        return found

    feat_masks = masks_of(share)[::-1]
    dp_masks = masks_of(groups)
    x_first = tuple(dp_masks)
    z_first = tuple(dp_masks[1:] + dp_masks[:1])

    def gather_feat(own, *earlier):
        held = {0: own}
        for mask in feat_masks:
            for j in list(held):
                [held[j ^ mask]] = after([swap(held[j], "feat", mask)], *earlier)
        return [held[j] for j in range(share)]

    def plus(array, come):
        return (array.astype(F32) + come.astype(F32)).astype(BF16)

    wide = max(hq, 128)
    anywhere = pl.BlockSpec(memory_space=pl.ANY)
    later = [w_down, w_out, w_gate, w_up]
    near = pl.BlockSpec((width, wide), lambda i: (0, lax.axis_index("feat") * hq // wide))
    attend_args = [in_hbm(a) for a in (lengths, tokens, gain_a, w_query, w_key, w_value)]
    attend_shapes = [
        vmem_of(rows, width, BF16),
        vmem_of(rows, hq, BF16),
        vmem_of(rows, hq, BF16),
        vmem_of(rows, hv, BF16),
        vmem_of(rows, hv, BF16),
        vmem_of(rows, hv, F32),
    ]
    normed, q, k, v, ctx, den = pl.pallas_call(
        attend_kernel,
        grid=(1,),
        in_specs=[
            pl.BlockSpec(memory_space=pltpu.SMEM),
            whole(tokens),
            whole(gain_a),
            near,
            near,
            pl.BlockSpec((width, hv), lambda i: (0, lax.axis_index("feat"))),
        ],
        out_specs=[whole(a) for a in attend_shapes],
        out_shape=attend_shapes,
        compiler_params=params(),
        cost_estimate=pl.CostEstimate(flops=1000, bytes_accessed=1000, transcendentals=0),
        name="attend",
    )(*attend_args)
    whole_vmem = pl.BlockSpec(memory_space=pltpu.VMEM)
    w_down, w_out, w_gate, w_up, ginner = call(
        fetch_kernel,
        "fetch",
        where,
        [ctx, in_hbm(cotangent), *map(in_hbm, later)],
        [*(pltpu.VMEM(a.shape, a.dtype) for a in later), vmem_of(rows, hidden, F32)],
        specs={i: anywhere for i in (0, 2, 3, 4, 5)},
        out_specs={0: whole_vmem, **{i: anywhere for i in range(1, 4)}},
        scratch=[pltpu.SemaphoreType.DMA((4,))],
    )
    ctx_all = gather_feat(ctx, w_down)

    feed_in = [*ctx_all, tokens, ginner, gain_b, w_out, w_gate, w_up]
    feed_shapes = [
        vmem_of(rows, width, F32),
        vmem_of(rows, width, BF16),
        vmem_of(rows, hidden, BF16),
        vmem_of(rows, hidden, BF16),
        vmem_of(rows, hidden, BF16),
        shape_of(half, width, BF16),
        shape_of(half, width, BF16),
    ]
    residual, normed_two, inner, grad_gate, grad_up, back_away, back_own = call(
        feed_kernel,
        "feed",
        where,
        feed_in,
        feed_shapes,
        share=share,
    )

    z_order = z_first
    split = max(hidden // 256, 1) * 128 + (128 if hidden % 256 >= 128 else 0)
    few = groups // 4
    x_args = [inner, grad_gate, cotangent, normed_two]
    z_args = [grad_gate, grad_up, normed_two]
    x_pairs = lambda refs: [(refs[0][...], refs[2]), (refs[1][:, :split], refs[3])]
    z_pairs = lambda refs: [(refs[0][:, split:], refs[2]), (refs[1][...], refs[2])]
    x_fixed = dict(pairs=x_pairs, order=x_first, chunk=chunk)
    z_fixed = dict(pairs=z_pairs, order=z_order, chunk=chunk)
    x_many, z_many, late_many = hidden + split, 2 * hidden - split, hv + 16 + pack

    def hops(name, held, sent, masks, earlier):
        [come] = after([swap(sent, "dp", masks[0])], earlier)
        for mask in masks[1:]:
            count = held.shape[0] // 2
            shapes = [shape_of(count, *held.shape[1:], BF16)] * 2
            held, sent = call(hop_kernel, name, where, [held, come], shapes)
            come = swap(sent, "dp", mask)
        return held, come, sent

    last = back_own
    x_sent, z_sent = call(
        pair_aways_kernel,
        "pair",
        where,
        [inner, grad_gate, grad_up, cotangent, normed_two],
        [shape_of(2 * few, x_many, chunk, BF16), shape_of(2 * few, z_many, chunk, BF16)],
        x_fixed=x_fixed,
        z_fixed=z_fixed,
    )
    last = z_sent
    [come] = after([swap(back_away, "feat", 1)], last)
    last = back_own = plus(back_own, come)
    feed_away, feed_own = call(
        down_kernel, "down", where, [*after([inner], last), w_down], [shape_of(half, width, BF16)] * 2
    )
    last = feed_own
    [come] = after([swap(feed_away, "feat", 1)], last)
    last = feed_own = plus(feed_own, come)
    scores, slopes, r_two = call(
        prepare_kernel,
        "prepare",
        where,
        [*after([q], last), k, residual],
        [
            vmem_of(hq // QK, 3 * half, half, BF16),
            vmem_of(hq // QK, 3 * half, half, BF16),
            vmem_of(rows, 1, F32),
        ],
    )
    last = scores
    x_held, z_held = call(
        pair_keeps_kernel,
        "keeps",
        where,
        [*after([inner], last), grad_gate, grad_up, cotangent, normed_two],
        [shape_of(2 * few, x_many, chunk, BF16), shape_of(2 * few, z_many, chunk, BF16)],
        x_fixed=x_fixed,
        z_fixed=z_fixed,
    )
    last = z_held
    for mask in feat_masks[:-1]:
        [come] = after([swap(back_own, "feat", mask)], last)
        last = back_own = plus(back_own, come)
    [back_other] = after([swap(back_own, "feat", 1)], last)
    grad_res, grad_mixed, grads, gain_part = call(
        back_kernel,
        "back",
        where,
        [back_own, back_other, residual, r_two, cotangent, gain_b, w_out, q, k, v, ctx, den, scores, slopes],
        [
            vmem_of(rows, width, F32),
            vmem_of(rows, width, BF16),
            vmem_of(rows, pack, BF16),
            shape_of(1, width, F32),
        ],
        specs={6: pl.BlockSpec((hv, width), lambda i, p: (p[0], 0))},
        scratch=[pltpu.VMEM((rows, hv), BF16)],
    )
    last = gain_part
    late_args = [ctx, grads, normed, grad_mixed, gain_part]
    late_pairs = lambda refs: [(refs[0][...], refs[3]), (None, refs[4]), (refs[1][...], refs[2])]
    late_fixed = dict(pairs=late_pairs, order=x_first, chunk=chunk)
    held = {0: grads}
    for mask in feat_masks[:-1]:
        for j in list(held):
            held[j ^ mask] = swap(held[j], "feat", mask)
    far = [j for j in held if j]
    [late_sent] = call(
        away_kernel,
        "late_away",
        where,
        [*after(late_args[:1], last), *late_args[1:]],
        [shape_of(2 * few, late_many, chunk, BF16)],
        **late_fixed,
    )
    late_come = swap(late_sent, "dp", x_first[0])
    last = late_sent
    [come] = after([swap(z_sent, "dp", z_order[0])], last)
    shapes = [shape_of(few, z_many, chunk, BF16)] * 2
    z_held, z_sent = call(hop_kernel, "z_keep", where, [z_held, come], shapes)
    last = z_sent
    [come] = after([swap(x_sent, "dp", x_first[0])], last)
    shapes = [shape_of(few, x_many, chunk, BF16)] * 2
    x_held, x_sent = call(hop_kernel, "x_keep", where, [x_held, come], shapes)
    last = x_sent
    [late_held] = call(
        away_kernel,
        "late_product",
        where,
        [*after(late_args[:1], last), *late_args[1:]],
        [shape_of(2 * few, late_many, chunk, BF16)],
        **late_fixed,
        away=False,
    )
    last = late_held
    for mask in feat_masks[:-1]:
        [come] = after([swap(feed_own, "feat", mask)], last)
        last = feed_own = plus(feed_own, come)
    held.update(zip(far, after([held[j] for j in far], last)))
    last = held[far[-1]]
    [come] = after([late_come], last)
    late, *direct = call(
        add_kernel,
        "late_keep",
        where,
        [late_held, come],
        [shape_of(late_many, chunk, F32)] + [shape_of(late_many, chunk, BF16)] * (2 * few - 1),
    )
    comes = [swap(piece, "dp", offset) for offset, piece in zip(positions(x_first)[1:], direct)]
    last = direct[-1]
    z_held, z_come, last = hops("z_hop", z_held, z_sent, z_order[1:], last)
    x_held, x_come, last = hops("x_hop", x_held, x_sent, x_first[1:], last)
    for j in list(held):
        [held[j ^ 1]] = after([swap(held[j], "feat", 1)], last)
    last = held[1]
    sum_out, sum_gain_two, sum_own = call(
        late_kernel,
        "late",
        where,
        [late, *after(comes, last)],
        [shape_of(hv, chunk, F32), shape_of(1, chunk, F32), shape_of(chunk, pack, BF16)],
    )
    last = sum_own
    sums = {0: sum_own}
    for mask in feat_masks[:-1]:
        for j in list(sums):
            sums[j ^ mask] = swap(sums[j], "feat", mask)
    sums_far = [j for j in sums if j]
    [feed_other] = after([swap(feed_own, "feat", 1)], last)
    last = feed_other
    def by_rows(array):
        return pl.BlockSpec((half,) + array.shape[1:], lambda i, p: (i, 0))

    in_args = [*[held[j] for j in range(share)], *after([grad_res], last), tokens, residual, feed_own, feed_other, gain_a, w_query, w_key, w_value]
    grad_input, output = call(
        input_kernel,
        "grad_input",
        where,
        in_args,
        [shape_of(rows, width, BF16)] * 2,
        grid=2,
        specs={i: by_rows(in_args[i]) for i in range(share + 3)},
        out_specs={i: pl.BlockSpec((half, width), lambda i, p: (i, 0)) for i in range(2)},
        share=share,
        hv=hv,
        hq=hq,
    )
    last = grad_input
    x_come, z_come = after([x_come, z_come], last)
    sum_down, sum_gate, sum_up = call(
        hidden_kernel, "hidden", where, [x_held, x_come, z_held, z_come], [shape_of(hidden, chunk, F32)] * 3
    )
    last = sum_down
    for j in list(sums):
        sums[j ^ 1] = swap(sums[j], "feat", 1)

    def own_rows(array):
        return pl.BlockSpec((chunk, array.shape[1]), lambda i, p: (p[1], 0))

    sum_query, sum_key, sum_value, sum_gain_one = call(
        finish_kernel,
        "finish",
        where,
        [*after([sums[j] for j in range(share)], last), gain_a, w_query, w_key, w_value],
        [
            shape_of(chunk, hq * share, F32),
            shape_of(chunk, hq * share, F32),
            shape_of(chunk, hv * share, F32),
            shape_of(1, chunk, F32),
        ],
        specs={
            share + 1: own_rows(w_query),
            share + 2: own_rows(w_key),
            share + 3: own_rows(w_value),
        },
        share=share,
        hv=hv,
        hq=hq,
    )
    last = sum_query

    return (
        output,
        grad_input,
        sum_gain_one[0],
        sum_query,
        sum_key,
        sum_value,
        sum_out,
        sum_gain_two[0],
        sum_gate.T,
        sum_up.T,
        sum_down,
    )


def solution(mesh):
    in_specs = (
        P("dp", None),
        P(),
        P(),
        P(),
        P(),
        P(),
        P(),
        P(None, "feat"),
        P(None, "feat"),
        P("feat", None),
        P("dp", None),
        P("dp", None),
    )
    out_specs = (
        P("dp", None),
        P("dp", None),
        P("dp"),
        P("dp", None),
        P("dp", None),
        P("dp", None),
        P("feat", "dp"),
        P("dp"),
        P("dp", "feat"),
        P("dp", "feat"),
        P("feat", "dp"),
    )
    return jax.shard_map(local, mesh=mesh, in_specs=in_specs, out_specs=out_specs, check_vma=False)
```

```python
import functools

import jax
import jax.numpy as jnp
from jax import lax
from jax.experimental import pallas as pl
from jax.experimental.pallas import tpu as pltpu
from jax.sharding import PartitionSpec as P

HEADS = 16
QK = 16
VD = 64
EPSILON = 1e-05
F32 = jnp.float32
BF16 = jnp.bfloat16
COSTS = {"feed": 3000000000, "grad_input": 1000, "hidden": 10000000000, "late": 10000000000, "late_keep": 10000000000}
VMEM_LIMIT = 20 * 1024 * 1024


def dot(a, b):
    return lax.dot_general(a, b, (((1,), (0,)), ((), ())), preferred_element_type=F32)


def dot_nt(a, b):
    return lax.dot_general(a, b, (((1,), (1,)), ((), ())), preferred_element_type=F32)


def dot_tn(a, b):
    return lax.dot_general(a, b, (((0,), (0,)), ((), ())), preferred_element_type=F32)


def lane_mask(shape, width, head):
    return lax.broadcasted_iota(jnp.int32, shape, 1) // width == head


def only_head(array, width, head):
    return jnp.where(lane_mask(array.shape, width, head), array, jnp.zeros_like(array))


def absolute_order(blocks, place):
    blocks = list(blocks)
    mask = 1
    while mask < len(blocks):
        flip = (place & mask) != 0
        blocks = [jnp.where(flip, blocks[j ^ mask], blocks[j]) for j in range(len(blocks))]
        mask *= 2
    return blocks


def bounds_of(where):
    bounds, total = [], 0
    for slot in range(2, len(where) if isinstance(where, tuple) else where.shape[0]):
        total = total + where[slot]
        bounds.append(total)
    return bounds


def starts_of(bounds, index):
    start = jnp.zeros_like(index)
    for bound in bounds:
        start = jnp.maximum(start, jnp.where(index >= bound, bound, 0))
    return start


def pick_columns(wide, index, width):
    each = wide.shape[1] // width
    picked = wide[:, :width]
    for i in range(1, each):
        picked = jnp.where(index % each == i, wide[:, i * width : (i + 1) * width], picked)
    return picked


def block_columns(ref, index, width):
    if width % 128 == 0:
        return ref[:, pl.ds(pl.multiple_of(index * width, 128), width)]
    each = 128 // width
    return pick_columns(ref[:, pl.ds(pl.multiple_of(index // each * 128, 128), 128)], index, width)


def positions(order):
    found = [0]
    for mask in order:
        found = [r for r in found] + [r ^ mask for r in found]
    count = len(found)
    result = []
    for p in range(count):
        r, top = 0, count // 2
        for mask in order:
            if p & top:
                r ^= mask
            top //= 2
        result.append(r)
    return result


def chunk_columns(ref, group, offsets, chunk):
    return jnp.concatenate([block_columns(ref, group ^ r, chunk) for r in offsets], axis=1)


def attend_kernel(lengths, tok, gain, w_query, w_key, w_value, *refs):
    n_out, q_out, k_out, v_out, ctx_out, den_out = refs
    rows = tok.shape[0]
    hq, hv = q_out.shape[1], v_out.shape[1]
    block = rows // 2
    feat = lax.axis_index("feat")
    where = (0, 0, *[lengths[0, i] for i in range(lengths.shape[1])])
    x = tok[...].astype(F32)
    r = lax.rsqrt(jnp.mean(x * x, axis=1, keepdims=True) + EPSILON)
    n = (x * r * gain[...]).astype(BF16)
    n_out[...] = n
    small = dot(n, jnp.concatenate([w_query[...], w_key[...]], axis=1))
    v = dot(n, w_value[...]).astype(BF16)
    wide = w_query.shape[1]
    q = (pick_columns(small[:, :wide], feat, hq) * QK**-0.5).astype(BF16)
    k = pick_columns(small[:, wide:], feat, hq).astype(BF16)
    v_out[...] = v
    q_out[...] = q
    k_out[...] = k
    bounds = bounds_of(where)
    start = starts_of(bounds, lax.broadcasted_iota(jnp.int32, (rows, 1), 0))
    number = [jnp.zeros((block, hv), F32) for _ in range(2)]
    total = [jnp.zeros((block, hv), F32) for _ in range(2)]
    for part in range(2):
        low, high = part * block, (part + 1) * block
        row = lax.broadcasted_iota(jnp.int32, (rows - low, block), 0) + low
        col = lax.broadcasted_iota(jnp.int32, (rows - low, block), 1) + low
        allowed = (col <= row) & (col >= start[low:])
        for head in range(hq // QK):
            t = dot_nt(only_head(q[low:], QK, head), k[low:high]) + 1.0
            exact = jnp.where(allowed, t * t + 1.0, 0.0)
            p = exact.astype(BF16)
            part_number = dot(p, only_head(v[low:high], VD, head))
            part_total = jnp.where(lane_mask((rows - low, hv), VD, head), jnp.sum(exact, axis=1, keepdims=True), 0.0)
            for i in range(part, 2):
                here = slice(i * block - low, (i + 1) * block - low)
                number[i] = number[i] + part_number[here]
                total[i] = total[i] + part_total[here]
    for i in range(2):
        ctx_out[i * block : (i + 1) * block, :] = (number[i] / total[i]).astype(BF16)
        den_out[i * block : (i + 1) * block, :] = total[i]


def fetch_kernel(where, ctx, cot, *refs):
    *refs, ginner_out, sems = refs
    count = len(refs) // 2
    copies = [pltpu.make_async_copy(refs[i], refs[count + i], sems.at[i]) for i in range(count)]
    for copy in copies:
        copy.start()
    copies[0].wait()
    live = lax.broadcasted_iota(jnp.int32, (cot.shape[0], 1), 0) < bounds_of(where)[-1]
    gfeed = jnp.where(live, cot[...], jnp.zeros_like(cot))
    ginner_out[...] = dot_nt(gfeed, refs[count][...])
    for copy in copies[1:]:
        copy.wait()


def feed_kernel(place, *refs, share):
    ctx = refs[:share]
    tok, ginner_in, gain, w_out, w_gate, w_up = refs[share : 6 + share]
    res_out, n_out, inner_out, gg_out, gu_out, away_out, own_out = refs[6 + share :]
    half = tok.shape[0] // 2
    core = place[0] & 1
    contexts = absolute_order([c[...] for c in ctx], place[0])
    context = jnp.concatenate(contexts, axis=1)
    rows = slice(None)
    index = lax.broadcasted_iota(jnp.int32, (2 * half, 1), 0)
    live = (index < bounds_of(place)[-1]).astype(F32)
    residual = tok[...].astype(F32) + live * dot(context, w_out[...])
    res_out[...] = residual
    r = lax.rsqrt(jnp.mean(residual * residual, axis=1, keepdims=True) + EPSILON)
    n = (residual * r * gain[...]).astype(BF16)
    n_out[...] = n
    hidden = w_gate.shape[0]
    for low in range(0, hidden, 256):
        part = slice(low, min(low + 256, hidden))
        gate = dot_nt(n, w_gate[part, :])
        up = dot_nt(n, w_up[part, :])
        ginner = ginner_in[:, part]
        sig = jax.nn.sigmoid(gate)
        act = gate * sig
        inner_out[:, part] = (act * up * live).astype(BF16)
        gg_out[:, part] = (ginner * up * sig * (1.0 + gate * (1.0 - sig))).astype(BF16)
        gu_out[:, part] = (ginner * act).astype(BF16)
    for which, out in ((1 - core, away_out), (core, own_out)):
        here = pl.ds(pl.multiple_of(which * half, half), half)
        out[...] = (dot(gg_out[here, :], w_gate[...]) + dot(gu_out[here, :], w_up[...])).astype(BF16)


def down_kernel(place, inner, w_down, away_out, own_out):
    half = own_out.shape[0]
    core = place[0] & 1
    for which, out in ((1 - core, away_out), (core, own_out)):
        out[...] = dot(inner[pl.ds(pl.multiple_of(which * half, half), half), :], w_down[...]).astype(BF16)


def products(where, pairs, offsets, chunk):
    found = []
    for left, right in pairs:
        part = chunk_columns(right, where[1], offsets, chunk)
        found.append(jnp.broadcast_to(part, (16, part.shape[1])) if left is None else dot_tn(left, part))
    return found


def away_kernel(where, *refs, pairs, order, chunk, away=True):
    out = refs[-1]
    offsets = positions(order)
    count = len(offsets) // 2
    low = 0
    for part in products(where, pairs(refs), offsets[count:] if away else offsets[:count], chunk):
        high = low + part.shape[0]
        for i in range(count):
            out[i, low:high, :] = part[:, i * chunk : (i + 1) * chunk].astype(BF16)
        low = high


def aways_kernel(where, inner, gate, up, cot, normed, w_down, x_out, z_out, feed_away, feed_own, *, x_fixed, z_fixed):
    away_kernel(where, inner, gate, cot, normed, x_out, **x_fixed)
    away_kernel(where, gate, up, normed, z_out, **z_fixed)
    down_kernel(where, inner, w_down, feed_away, feed_own)


def pair_keeps_kernel(where, inner, gate, up, cot, normed, x_out, z_out, *, x_fixed, z_fixed):
    away_kernel(where, inner, gate, cot, normed, x_out, **x_fixed, away=False)
    away_kernel(where, gate, up, normed, z_out, **z_fixed, away=False)


def pair_aways_kernel(where, inner, gate, up, cot, normed, x_out, z_out, *, x_fixed, z_fixed):
    away_kernel(where, inner, gate, cot, normed, x_out, **x_fixed)
    away_kernel(where, gate, up, normed, z_out, **z_fixed)


def keep_kernel(where, *refs, pairs, order, chunk):
    arrived, keep_out, away_out = refs[-3:]
    offsets = positions(order)
    count = len(offsets) // 2
    low = 0
    for part in products(where, pairs(refs), offsets[:count], chunk):
        high = low + part.shape[0]
        for i in range(count):
            total = part[:, i * chunk : (i + 1) * chunk] + arrived[i, low:high, :].astype(F32)
            if i < count // 2:
                keep_out[i, low:high, :] = total.astype(keep_out.dtype)
            else:
                away_out[i - count // 2, low:high, :] = total.astype(BF16)
        low = high


def direct_kernel(where, *refs, pairs, order, chunk, inputs):
    arrived, outs = refs[inputs], refs[inputs + 1 :]
    offsets = positions(order)
    count = len(offsets) // 2
    low = 0
    for part in products(where, pairs(refs), offsets[:count], chunk):
        high = low + part.shape[0]
        for i in range(count):
            total = part[:, i * chunk : (i + 1) * chunk] + arrived[i, low:high, :].astype(F32)
            outs[i][low:high, :] = total.astype(outs[i].dtype)
        low = high


def add_kernel(where, held, come, *outs):
    for i, out in enumerate(outs):
        out[...] = (held[i].astype(F32) + come[i].astype(F32)).astype(out.dtype)


def hop_kernel(where, held, come, keep_out, away_out):
    count = keep_out.shape[0]
    for i in range(count):
        keep_out[i] = (held[i].astype(F32) + come[i].astype(F32)).astype(keep_out.dtype)
        away_out[i] = (held[count + i].astype(F32) + come[count + i].astype(F32)).astype(BF16)


def hidden_kernel(where, x_held, x_come, z_held, z_come, down_out, gate_out, up_out):
    hidden = down_out.shape[0]
    split = x_held.shape[1] - hidden
    x = x_held[0].astype(F32) + x_come[0].astype(F32)
    z = z_held[0].astype(F32) + z_come[0].astype(F32)
    down_out[...] = x[:hidden]
    gate_out[:split, :] = x[hidden:]
    gate_out[split:, :] = z[: hidden - split]
    up_out[...] = z[hidden - split :]


def late_kernel(where, held, *refs):
    comes, (out, gain_out, own_out) = refs[:-3], refs[-3:]
    total = held[...].reshape(held.shape[-2:]).astype(F32)
    for come in comes:
        total = total + come[...].reshape(come.shape[-2:]).astype(F32)
    many = out.shape[0]
    out[...] = total[:many]
    gain_out[...] = total[many : many + 1]
    own_out[...] = total[many + 16 :].T.astype(BF16)


def prepare_kernel(where, q_in, k_in, res, p_out, t_out, r_out):
    rows, hq = q_in.shape
    half = rows // 2
    bounds = bounds_of(where)
    residual = res[...]
    r_out[...] = lax.rsqrt(jnp.mean(residual * residual, axis=1, keepdims=True) + EPSILON)
    q, k = q_in[...], k_in[...]
    for part in range(2):
        low, high = part * half, (part + 1) * half
        row = lax.broadcasted_iota(jnp.int32, (high, half), 0)
        col = lax.broadcasted_iota(jnp.int32, (high, half), 1) + low
        start = starts_of(bounds, lax.broadcasted_iota(jnp.int32, (1, half), 1) + low)
        allowed = (row <= col) & (row >= start)
        for head in range(hq // QK):
            t = dot_nt(k[:high], only_head(q[low:high], QK, head)) + 1.0
            here = slice(part * half, part * half + high)
            p_out[head, here, :] = jnp.where(allowed, t * t + 1.0, 0.0).astype(BF16)
            t_out[head, here, :] = jnp.where(allowed, t, 0.0).astype(BF16)


def back_kernel(
    place, own, other, res, r_in, cot, gain, w_own, q_in, k_in, v_in, ctx_in, den_in, p_in, t_in,
    gr_out, gm_out, g_out, gain_out, gctx,
):
    rows = res.shape[0]
    hq, hv = q_in.shape[1], v_in.shape[1]
    half = rows // 2
    core = place[0] & 1
    bounds = bounds_of(place)
    gain_sum = jnp.zeros((1, gain_out.shape[1]), F32)
    for which, source in ((core, own), (1 - core, other)):
        here = pl.ds(pl.multiple_of(which * half, half), half)
        live = (lax.broadcasted_iota(jnp.int32, (half, 1), 0) + which * half < bounds[-1]).astype(F32)
        e = source[...].astype(F32)
        residual, r = res[here, :], r_in[here, :]
        weighted = e * gain[...]
        gain_sum = gain_sum + jnp.sum(e * residual * r, axis=0, keepdims=True)
        scale = r * r * r * jnp.mean(weighted * residual, axis=1, keepdims=True)
        grad = cot[here, :].astype(F32) + r * weighted - residual * scale
        gr_out[here, :] = grad
        gm = (live * grad).astype(BF16)
        gm_out[here, :] = gm
        gctx[here, :] = dot_nt(gm, w_own[...]).astype(BF16)
    gain_out[...] = gain_sum
    number = gctx[...].astype(F32) / den_in[...]
    gn = number.astype(BF16)
    product = number * ctx_in[...].astype(F32)
    leading = product.astype(BF16)
    remainder = (product - leading.astype(F32)).astype(BF16)
    select = (
        lax.broadcasted_iota(jnp.int32, (16, hv), 1) // VD == lax.broadcasted_iota(jnp.int32, (16, hv), 0)
    )
    select = jnp.where(select, 1.0, 0.0).astype(BF16)
    shift = dot_nt(select, leading) + dot_nt(select, remainder)
    q, k, v = q_in[...], k_in[...], v_in[...]
    gk = [jnp.zeros((half, hq), F32) for _ in range(2)]
    gv = [jnp.zeros((half, hv), F32) for _ in range(2)]
    for part in range(2):
        low, high = part * half, (part + 1) * half
        gq = jnp.zeros((half, hq), F32)
        for head in range(hq // QK):
            q_head = only_head(q[low:high], QK, head)
            g_head = only_head(gn[low:high], VD, head)
            p = p_in[head, part * half : part * half + high, :]
            t = t_in[head, part * half : part * half + high, :]
            g = dot_nt(v[:high], g_head) - shift[head : head + 1, low:high]
            ds = (g * t.astype(F32)).astype(BF16)
            part_gv, part_gk = dot(p, g_head), dot(ds, q_head)
            for j in range(part + 1):
                gv[j] = gv[j] + part_gv[j * half : (j + 1) * half]
                gk[j] = gk[j] + part_gk[j * half : (j + 1) * half]
            gq = gq + dot_tn(ds, only_head(k[:high], QK, head))
        g_out[low:high, hv : hv + hq] = (gq * (2.0 * QK**-0.5)).astype(BF16)
    for j in range(2):
        g_out[j * half : (j + 1) * half, :hv] = gv[j].astype(BF16)
        g_out[j * half : (j + 1) * half, hv + hq :] = (gk[j] * 2.0).astype(BF16)


def input_kernel(place, *refs, share, hv, hq):
    grads = refs[:share]
    gr, tok, res, own, other, gain, w_query, w_key, w_value, out, output = refs[share:]
    blocks = absolute_order([g[...] for g in grads], place[0])
    values = jnp.concatenate([b[:, :hv] for b in blocks], axis=1)
    queries = jnp.concatenate([b[:, hv : hv + hq] for b in blocks], axis=1)
    keys = jnp.concatenate([b[:, hv + hq :] for b in blocks], axis=1)
    e = dot_nt(queries, w_query[...]) + dot_nt(keys, w_key[...]) + dot_nt(values, w_value[...])
    x = tok[...].astype(F32)
    r = lax.rsqrt(jnp.mean(x * x, axis=1, keepdims=True) + EPSILON)
    weighted = e * gain[...]
    scale = r * r * r * jnp.mean(weighted * x, axis=1, keepdims=True)
    out[...] = (gr[...] + r * weighted - x * scale).astype(BF16)
    step, half = pl.program_id(0), tok.shape[0]
    index = lax.broadcasted_iota(jnp.int32, (half, 1), 0) + step * half
    live = (index < bounds_of(place)[-1]).astype(F32)
    feed = jnp.where(step == (place[0] & 1), own[...], other[...]).astype(F32)
    output[...] = (res[...] + live * feed).astype(BF16)


def finish_kernel(where, *refs, share, hv, hq):
    sums = refs[:share]
    gain, w_query, w_key, w_value, q_out, k_out, v_out, gain_out = refs[share:]
    blocks = absolute_order([s[...].astype(F32) for s in sums], where[0])
    values = jnp.concatenate([b[:, :hv] for b in blocks], axis=1)
    queries = jnp.concatenate([b[:, hv : hv + hq] for b in blocks], axis=1)
    keys = jnp.concatenate([b[:, hv + hq :] for b in blocks], axis=1)
    q_out[...] = queries
    k_out[...] = keys
    v_out[...] = values
    total = jnp.sum(values * w_value[...].astype(F32), axis=1, keepdims=True)
    total = total + jnp.sum(queries * w_query[...].astype(F32) + keys * w_key[...].astype(F32), axis=1, keepdims=True)
    spread = jnp.broadcast_to(total, (total.shape[0], total.shape[0]))
    diagonal = lax.broadcasted_iota(jnp.int32, spread.shape, 0) == lax.broadcasted_iota(jnp.int32, spread.shape, 1)
    row = jnp.sum(jnp.where(diagonal, spread, 0.0), axis=0, keepdims=True)
    gain_out[...] = row / block_columns(gain, where[1], gain_out.shape[1])


def last_kernel(where, *refs, share, hv, hq):
    hidden_kernel(where, *refs[:4], *refs[8 + share : 11 + share])
    finish_kernel(where, *refs[4 : 8 + share], *refs[11 + share :], share=share, hv=hv, hq=hq)


def back_late_kernel(where, *refs, order, chunk):
    *ins, normed, gr_out, gm_out, g_out, gain_out, late_out, gctx = refs
    back_kernel(where, *ins, gr_out, gm_out, g_out, gain_out, gctx)
    pairs = lambda _: [(ins[10][...], gm_out), (None, gain_out), (g_out[...], normed)]
    away_kernel(where, late_out, pairs=pairs, order=order, chunk=chunk)


def whole(array):
    return pl.BlockSpec(array.shape, lambda *_: (0,) * len(array.shape))


def shape_of(*args):
    return jax.ShapeDtypeStruct(args[:-1], args[-1])


def vmem_of(*args):
    return pltpu.VMEM(args[:-1], args[-1])


def params():
    return pltpu.CompilerParams(vmem_limit_bytes=VMEM_LIMIT)


def call(kernel, name, scalars, arrays, shapes, grid=1, specs=None, out_specs=None, scratch=(), **fixed):
    specs, out_specs = specs or {}, out_specs or {}
    return pl.pallas_call(
        functools.partial(kernel, **fixed) if fixed else kernel,
        grid_spec=pltpu.PrefetchScalarGridSpec(
            num_scalar_prefetch=1,
            grid=(grid,),
            in_specs=[specs.get(i, whole(a)) for i, a in enumerate(arrays)],
            out_specs=[out_specs.get(i, whole(s)) for i, s in enumerate(shapes)],
            scratch_shapes=list(scratch),
        ),
        out_shape=list(shapes),
        compiler_params=params(),
        cost_estimate=pl.CostEstimate(flops=COSTS.get(name, 1000), bytes_accessed=1000, transcendentals=0),
        name=name,
    )(scalars, *arrays)


def after(arrays, *earlier):
    held = lax.optimization_barrier((*arrays, *earlier))
    return held[: len(arrays)]


def in_hbm(array):
    return pltpu.with_memory_space_constraint(array, pltpu.HBM)


def local(
    tokens, gain_one, w_query, w_key, w_value, w_out, gain_two, w_gate, w_up, w_down, lengths, cotangent
):
    rows, width = tokens.shape
    share, groups = lax.axis_size("feat"), lax.axis_size("dp")
    feat, group = lax.axis_index("feat"), lax.axis_index("dp")
    hq, hv = w_query.shape[1] // share, w_value.shape[1] // share
    hidden = w_gate.shape[1]
    chunk = width // groups
    half = rows // 2
    pack = hv + 2 * hq
    where = jnp.concatenate([jnp.stack([feat, group]).astype(jnp.int32), lengths[0]])
    w_gate, w_up = w_gate.T, w_up.T
    gain_a, gain_b = gain_one[None, :], gain_two[None, :]

    def swap(array, axis, mask):
        count = share if axis == "feat" else groups
        return lax.ppermute(array, axis, [(i, i ^ mask) for i in range(count)])

    def masks_of(count):
        found, mask = [], 1
        while mask < count:
            found.append(mask)
            mask *= 2
        return found

    feat_masks = masks_of(share)[::-1]
    dp_masks = masks_of(groups)
    x_first = tuple(dp_masks)
    z_first = tuple(dp_masks[1:] + dp_masks[:1])

    def gather_feat(own, *earlier):
        held = {0: own}
        for mask in feat_masks:
            for j in list(held):
                [held[j ^ mask]] = after([swap(held[j], "feat", mask)], *earlier)
        return [held[j] for j in range(share)]

    def plus(array, come):
        return (array.astype(F32) + come.astype(F32)).astype(BF16)

    wide = max(hq, 128)
    anywhere = pl.BlockSpec(memory_space=pl.ANY)
    later = [w_down, w_out, w_gate, w_up]
    near = pl.BlockSpec((width, wide), lambda i: (0, lax.axis_index("feat") * hq // wide))
    attend_args = [in_hbm(a) for a in (lengths, tokens, gain_a, w_query, w_key, w_value)]
    attend_shapes = [
        vmem_of(rows, width, BF16),
        vmem_of(rows, hq, BF16),
        vmem_of(rows, hq, BF16),
        vmem_of(rows, hv, BF16),
        vmem_of(rows, hv, BF16),
        vmem_of(rows, hv, F32),
    ]
    normed, q, k, v, ctx, den = pl.pallas_call(
        attend_kernel,
        grid=(1,),
        in_specs=[
            pl.BlockSpec(memory_space=pltpu.SMEM),
            whole(tokens),
            whole(gain_a),
            near,
            near,
            pl.BlockSpec((width, hv), lambda i: (0, lax.axis_index("feat"))),
        ],
        out_specs=[whole(a) for a in attend_shapes],
        out_shape=attend_shapes,
        compiler_params=params(),
        cost_estimate=pl.CostEstimate(flops=1000, bytes_accessed=1000, transcendentals=0),
        name="attend",
    )(*attend_args)
    whole_vmem = pl.BlockSpec(memory_space=pltpu.VMEM)
    w_down, w_out, w_gate, w_up, ginner = call(
        fetch_kernel,
        "fetch",
        where,
        [ctx, in_hbm(cotangent), *map(in_hbm, later)],
        [*(pltpu.VMEM(a.shape, a.dtype) for a in later), vmem_of(rows, hidden, F32)],
        specs={i: anywhere for i in (0, 2, 3, 4, 5)},
        out_specs={0: whole_vmem, **{i: anywhere for i in range(1, 4)}},
        scratch=[pltpu.SemaphoreType.DMA((4,))],
    )
    ctx_all = gather_feat(ctx, w_down)

    feed_in = [*ctx_all, tokens, ginner, gain_b, w_out, w_gate, w_up]
    feed_shapes = [
        vmem_of(rows, width, F32),
        vmem_of(rows, width, BF16),
        vmem_of(rows, hidden, BF16),
        vmem_of(rows, hidden, BF16),
        vmem_of(rows, hidden, BF16),
        shape_of(half, width, BF16),
        shape_of(half, width, BF16),
    ]
    residual, normed_two, inner, grad_gate, grad_up, back_away, back_own = call(
        feed_kernel,
        "feed",
        where,
        feed_in,
        feed_shapes,
        share=share,
    )

    z_order = z_first
    split = max(hidden // 256, 1) * 128 + (128 if hidden % 256 >= 128 else 0)
    few = groups // 4
    x_args = [inner, grad_gate, cotangent, normed_two]
    z_args = [grad_gate, grad_up, normed_two]
    x_pairs = lambda refs: [(refs[0][...], refs[2]), (refs[1][:, :split], refs[3])]
    z_pairs = lambda refs: [(refs[0][:, split:], refs[2]), (refs[1][...], refs[2])]
    x_fixed = dict(pairs=x_pairs, order=x_first, chunk=chunk)
    z_fixed = dict(pairs=z_pairs, order=z_order, chunk=chunk)
    x_many, z_many, late_many = hidden + split, 2 * hidden - split, hv + 16 + pack

    def hops(name, held, sent, masks, earlier):
        [come] = after([swap(sent, "dp", masks[0])], earlier)
        for mask in masks[1:]:
            count = held.shape[0] // 2
            shapes = [shape_of(count, *held.shape[1:], BF16)] * 2
            held, sent = call(hop_kernel, name, where, [held, come], shapes)
            come = swap(sent, "dp", mask)
        return held, come, sent

    last = back_own
    x_sent, z_sent = call(
        pair_aways_kernel,
        "pair",
        where,
        [inner, grad_gate, grad_up, cotangent, normed_two],
        [shape_of(2 * few, x_many, chunk, BF16), shape_of(2 * few, z_many, chunk, BF16)],
        x_fixed=x_fixed,
        z_fixed=z_fixed,
    )
    last = z_sent
    [come] = after([swap(back_away, "feat", 1)], last)
    last = back_own = plus(back_own, come)
    feed_away, feed_own = call(
        down_kernel, "down", where, [*after([inner], last), w_down], [shape_of(half, width, BF16)] * 2
    )
    last = feed_own
    [come] = after([swap(feed_away, "feat", 1)], last)
    last = feed_own = plus(feed_own, come)
    scores, slopes, r_two = call(
        prepare_kernel,
        "prepare",
        where,
        [*after([q], last), k, residual],
        [
            vmem_of(hq // QK, 3 * half, half, BF16),
            vmem_of(hq // QK, 3 * half, half, BF16),
            vmem_of(rows, 1, F32),
        ],
    )
    last = scores
    x_held, z_held = call(
        pair_keeps_kernel,
        "keeps",
        where,
        [*after([inner], last), grad_gate, grad_up, cotangent, normed_two],
        [shape_of(2 * few, x_many, chunk, BF16), shape_of(2 * few, z_many, chunk, BF16)],
        x_fixed=x_fixed,
        z_fixed=z_fixed,
    )
    last = z_held
    for mask in feat_masks[:-1]:
        [come] = after([swap(back_own, "feat", mask)], last)
        last = back_own = plus(back_own, come)
    [back_other] = after([swap(back_own, "feat", 1)], last)
    grad_res, grad_mixed, grads, gain_part, late_sent = call(
        back_late_kernel,
        "back",
        where,
        [back_own, back_other, residual, r_two, cotangent, gain_b, w_out, q, k, v, ctx, den, scores, slopes, normed],
        [
            vmem_of(rows, width, F32),
            vmem_of(rows, width, BF16),
            vmem_of(rows, pack, BF16),
            shape_of(1, width, F32),
            shape_of(2 * few, hv + 16 + pack, chunk, BF16),
        ],
        specs={6: pl.BlockSpec((hv, width), lambda i, p: (p[0], 0))},
        scratch=[pltpu.VMEM((rows, hv), BF16)],
        order=x_first,
        chunk=chunk,
    )
    late_args = [ctx, grads, normed, grad_mixed, gain_part]
    late_pairs = lambda refs: [(refs[0][...], refs[3]), (None, refs[4]), (refs[1][...], refs[2])]
    late_fixed = dict(pairs=late_pairs, order=x_first, chunk=chunk)
    held = {0: grads}
    for mask in feat_masks[:-1]:
        for j in list(held):
            held[j ^ mask] = swap(held[j], "feat", mask)
    far = [j for j in held if j]
    late_come = swap(late_sent, "dp", x_first[0])
    last = late_sent
    [come] = after([swap(z_sent, "dp", z_order[0])], last)
    shapes = [shape_of(few, z_many, chunk, BF16)] * 2
    z_held, z_sent = call(hop_kernel, "z_keep", where, [z_held, come], shapes)
    last = z_sent
    [come] = after([swap(x_sent, "dp", x_first[0])], last)
    shapes = [shape_of(few, x_many, chunk, BF16)] * 2
    x_held, x_sent = call(hop_kernel, "x_keep", where, [x_held, come], shapes)
    last = x_sent
    [late_held] = call(
        away_kernel,
        "late_product",
        where,
        [*after(late_args[:1], last), *late_args[1:]],
        [shape_of(2 * few, late_many, chunk, BF16)],
        **late_fixed,
        away=False,
    )
    last = late_held
    for mask in feat_masks[:-1]:
        [come] = after([swap(feed_own, "feat", mask)], last)
        last = feed_own = plus(feed_own, come)
    held.update(zip(far, after([held[j] for j in far], last)))
    last = held[far[-1]]
    [come] = after([late_come], last)
    late, *direct = call(
        add_kernel,
        "late_keep",
        where,
        [late_held, come],
        [shape_of(late_many, chunk, F32)] + [shape_of(late_many, chunk, BF16)] * (2 * few - 1),
    )
    comes = [swap(piece, "dp", offset) for offset, piece in zip(positions(x_first)[1:], direct)]
    last = direct[-1]
    z_held, z_come, last = hops("z_hop", z_held, z_sent, z_order[1:], last)
    x_held, x_come, last = hops("x_hop", x_held, x_sent, x_first[1:], last)
    for j in list(held):
        [held[j ^ 1]] = after([swap(held[j], "feat", 1)], last)
    last = held[1]
    sum_out, sum_gain_two, sum_own = call(
        late_kernel,
        "late",
        where,
        [late, *after(comes, last)],
        [shape_of(hv, chunk, F32), shape_of(1, chunk, F32), shape_of(chunk, pack, BF16)],
    )
    last = sum_own
    sums = {0: sum_own}
    for mask in feat_masks[:-1]:
        for j in list(sums):
            sums[j ^ mask] = swap(sums[j], "feat", mask)
    sums_far = [j for j in sums if j]
    [feed_other] = after([swap(feed_own, "feat", 1)], last)
    last = feed_other
    def by_rows(array):
        return pl.BlockSpec((half,) + array.shape[1:], lambda i, p: (i, 0))

    in_args = [*[held[j] for j in range(share)], *after([grad_res], last), tokens, residual, feed_own, feed_other, gain_a, w_query, w_key, w_value]
    grad_input, output = call(
        input_kernel,
        "grad_input",
        where,
        in_args,
        [shape_of(rows, width, BF16)] * 2,
        grid=2,
        specs={i: by_rows(in_args[i]) for i in range(share + 3)},
        out_specs={i: pl.BlockSpec((half, width), lambda i, p: (i, 0)) for i in range(2)},
        share=share,
        hv=hv,
        hq=hq,
    )
    last = grad_input
    x_come, z_come = after([x_come, z_come], last)
    sum_down, sum_gate, sum_up = call(
        hidden_kernel, "hidden", where, [x_held, x_come, z_held, z_come], [shape_of(hidden, chunk, F32)] * 3
    )
    last = sum_down
    for j in list(sums):
        sums[j ^ 1] = swap(sums[j], "feat", 1)

    def own_rows(array):
        return pl.BlockSpec((chunk, array.shape[1]), lambda i, p: (p[1], 0))

    sum_query, sum_key, sum_value, sum_gain_one = call(
        finish_kernel,
        "finish",
        where,
        [*after([sums[j] for j in range(share)], last), gain_a, w_query, w_key, w_value],
        [
            shape_of(chunk, hq * share, F32),
            shape_of(chunk, hq * share, F32),
            shape_of(chunk, hv * share, F32),
            shape_of(1, chunk, F32),
        ],
        specs={
            share + 1: own_rows(w_query),
            share + 2: own_rows(w_key),
            share + 3: own_rows(w_value),
        },
        share=share,
        hv=hv,
        hq=hq,
    )
    last = sum_query

    return (
        output,
        grad_input,
        sum_gain_one[0],
        sum_query,
        sum_key,
        sum_value,
        sum_out,
        sum_gain_two[0],
        sum_gate.T,
        sum_up.T,
        sum_down,
    )


def solution(mesh):
    in_specs = (
        P("dp", None),
        P(),
        P(),
        P(),
        P(),
        P(),
        P(),
        P(None, "feat"),
        P(None, "feat"),
        P("feat", None),
        P("dp", None),
        P("dp", None),
    )
    out_specs = (
        P("dp", None),
        P("dp", None),
        P("dp"),
        P("dp", None),
        P("dp", None),
        P("dp", None),
        P("feat", "dp"),
        P("dp"),
        P("dp", "feat"),
        P("dp", "feat"),
        P("feat", "dp"),
    )
    return jax.shard_map(local, mesh=mesh, in_specs=in_specs, out_specs=out_specs, check_vma=False)
```
